32 devices in a mesh: lon: 8 (over z, x), lat: 4 (over y, core).
Axes of the slice: x: 2, y: 2, z: 4, core: 2. Of those that a mesh axis runs over, the one named last changes fastest.
Arguments:
- obs_values: bfloat16 [1024, 31, 256], P(('lon', 'lat')), may hold values from -6 to 6
- obs_offset: float32 [1024, 2, 256], P(('lon', 'lat')), may hold values from -0.5 to 0.5
- obs_cell: int32 [1024, 256], P(('lon', 'lat')), may hold values from 0 to 511
- obs_slot: int32 [1024, 256], P(('lon', 'lat')), may hold values from 0 to 11
- obs_count: int32 [32, 32], P(('lon', 'lat')), may hold values from 1 to 256, as said below
- embed_weight: bfloat16 [384, 256], replicated, may hold values from -0.3125 to 0.3125
- embed_bias: float32 [256], replicated, may hold values from -3 to 3
- stride_weight: bfloat16 [9, 256, 256], replicated, may hold values from -0.125 to 0.125
- stride_bias: float32 [256], replicated, may hold values from -3 to 3
- depth_weight: float32 [9, 256], replicated, may hold values from -2 to 2
- norm_gain: float32 [256], replicated, may hold values from 0.1 to 1.9
Outputs:
- encoded: bfloat16 [32, 128, 256], P('lat', 'lon')
The draws below stay inside these ranges and needn't reach their ends.
Inputs may be any that keep to these rules, and one draw needn't show every extreme that they name: `obs_count`: every entry is at least 1; in every draw one destination tile receives exactly 256 live slots from every source shard.
All inputs are finite; a program needn't handle non-finite values.
Results may differ from the reference program's by a relative error of at most 0.011.
Values may be sent and summed in bfloat16 or wider, within the bound.
No kernel may reach another device: no remote copies, remote signals or barrier semaphores. Data moves between devices by JAX's collectives and lax.ppermute only.
A program may use at most 128 MiB of HBM per device.

```python
import jax
import jax.numpy as jnp
from jax import lax

D = 256
OBS_VARS = 31
SLOTS = 12
TLAT = 16
TLON = 32
CAP = 256
LAT_TILES = 4
NTILES = 32
CELLS = 512
GLAT = 64
GLON = 256


def draw_obs_count(key, part):
    base_key = jax.random.fold_in(key, 11)
    heat_key, level_key, hot_key = jax.random.split(base_key, 3)
    heat = jax.random.randint(heat_key, (NTILES,), 1, 5, dtype=jnp.int32)
    level = jax.random.randint(level_key, (NTILES, NTILES), 0, CAP + 1, dtype=jnp.int32)
    counts = jnp.maximum(1, level * heat[None, :] // 4)
    hottest = jax.random.randint(hot_key, (), 0, NTILES, dtype=jnp.int32)
    column = jnp.arange(NTILES, dtype=jnp.int32)[None, :]
    counts = jnp.where(column == hottest, CAP, counts)
    return counts.astype(jnp.int32)


def plant(values, stream_key, smallest, top_value):
    longest = values.shape.index(max(values.shape))
    spots = []
    for shift in (0, 1):
        where = [jax.random.randint(jax.random.fold_in(stream_key, axis), (), 0, length) for axis, length in enumerate(values.shape)]
        where[longest] = (where[longest] + shift) % values.shape[longest]
        spots.append(tuple(where))
    return values.at[spots[0]].set(smallest).at[spots[1]].set(top_value)


def block_scale(key, shape, pieces, smallest, high):
    def one(axis_at, blocks):
        draws = jax.random.uniform(jax.random.fold_in(jax.random.fold_in(key, 6), axis_at), (blocks,), jnp.float32, smallest / len(pieces), high / len(pieces))
        return jnp.repeat(jnp.exp(draws), shape[axis_at] // blocks).reshape((-1,) + (1,) * (len(shape) - axis_at - 1))

    factor_of = one(*pieces[0])
    for cut in pieces[1:]:
        factor_of = factor_of * one(*cut)
    return factor_of


def noise(own_key, extent, scale, most, cuts=(), held_as=jnp.bfloat16):
    gain = block_scale(own_key, extent, cuts, -0.22, 0.18) if cuts else 1.0
    array = jax.random.normal(own_key, extent, jnp.float32) * scale * gain
    return jnp.minimum(jnp.maximum(array, -most), most).astype(held_as)


def setup_inputs(seed: int = 0) -> dict:
    key_list = jax.random.split(jax.random.key(seed), 12)
    return {
        "obs_values": noise(key_list[0], (NTILES * NTILES, OBS_VARS, CAP), 1.0, 6.0, ((0, 32),)),
        "obs_offset": jnp.clip(jax.random.uniform(key_list[1], (NTILES * NTILES, 2, CAP), jnp.float32, -0.5, 0.5) * block_scale(key_list[1], (NTILES * NTILES, 2, CAP), ((0, 32),), -0.4, 0.0), -0.5, 0.5),
        "obs_cell": plant(jax.random.randint(key_list[2], (NTILES * NTILES, CAP), 0, CELLS), jax.random.fold_in(key_list[2], 1), 0, CELLS - 1).astype(jnp.int32),
        "obs_slot": plant(jax.random.randint(key_list[3], (NTILES * NTILES, CAP), 0, SLOTS), jax.random.fold_in(key_list[3], 1), 0, SLOTS - 1).astype(jnp.int32),
        "obs_count": draw_obs_count(jax.random.fold_in(key_list[11], 71), 0),
        "embed_weight": noise(key_list[5], (SLOTS * (OBS_VARS + 1), D), (SLOTS * (OBS_VARS + 1)) ** -0.5, 0.3125),
        "embed_bias": noise(key_list[6], (D,), 0.5, 3.0, (), jnp.float32),
        "stride_weight": noise(key_list[7], (9, D, D), (9 * D) ** -0.5, 0.125),
        "stride_bias": noise(key_list[8], (D,), 0.5, 3.0, (), jnp.float32),
        "depth_weight": noise(key_list[9], (9, D), 9 ** -0.5, 2.0, (), jnp.float32),
        "norm_gain": jnp.clip(1.0 + 0.18 * jax.random.normal(key_list[10], (D,), jnp.float32), 0.1, 1.9),
    }


def layer_norm(mixed, norm_gain):
    centre = mixed - lax.optimization_barrier(jnp.mean(mixed, axis=-1, keepdims=True))
    spread = lax.optimization_barrier(jnp.mean(centre * centre, axis=-1, keepdims=True))
    return centre * lax.rsqrt(spread + 1e-05) * norm_gain

def reference(obs_values, obs_offset, obs_cell, obs_slot, obs_count, embed_weight, embed_bias, stride_weight, stride_bias, depth_weight, norm_gain):
    tiles = NTILES
    width = OBS_VARS + 1
    position = lax.broadcasted_iota(jnp.int32, obs_cell.shape, 1)
    live = position < obs_count.reshape(-1)[:, None]
    radius = obs_offset[:, 0, :] * obs_offset[:, 0, :] + obs_offset[:, 1, :] * obs_offset[:, 1, :]
    weight = jnp.where(live, jnp.exp(-2.0 * radius), jnp.float32(0.0))
    scaled = obs_values.astype(jnp.float32) * weight[:, None, :]
    packed = jnp.concatenate([scaled, weight[:, None, :]], axis=1).astype(jnp.bfloat16)
    target = jnp.arange(tiles * tiles, dtype=jnp.int32) % tiles
    lon_tile = (target // LAT_TILES).astype(jnp.int32)
    lat_tile = (target % LAT_TILES).astype(jnp.int32)
    grid_row = lat_tile[:, None] * TLAT + obs_cell // TLON
    grid_col = lon_tile[:, None] * TLON + obs_cell % TLON
    segment = ((obs_slot * GLAT + grid_row) * GLON + grid_col).astype(jnp.int32)
    data = jnp.transpose(packed, (0, 2, 1)).reshape(-1, width).astype(jnp.float32)
    total = jax.ops.segment_sum(data, segment.reshape(-1), num_segments=SLOTS * GLAT * GLON)
    total = jnp.transpose(total.reshape(SLOTS, GLAT, GLON, width), (1, 2, 0, 3))
    density = total[..., width - 1:]
    ratio = total[..., :width - 1] / (1.0 + density)
    gridded = jnp.concatenate([ratio, density], axis=3).reshape(GLAT * GLON, SLOTS * width).astype(jnp.bfloat16)
    projected = jnp.dot(gridded, embed_weight, preferred_element_type=jnp.float32) + embed_bias
    embedded = jax.nn.gelu(projected).astype(jnp.bfloat16).reshape(GLAT, GLON, D)
    framed = jnp.concatenate([jnp.zeros((1, GLON, D), jnp.bfloat16), embedded], axis=0)
    framed = jnp.concatenate([framed[:, GLON - 1:], framed], axis=1)
    patches = jnp.concatenate([framed[row_at:row_at + GLAT - 1:2, col_at:col_at + GLON - 1:2] for row_at in range(3) for col_at in range(3)], axis=2)
    strided = jnp.dot(patches.reshape(-1, 9 * D), stride_weight.reshape(9 * D, D), preferred_element_type=jnp.float32) + stride_bias
    coarse = jax.nn.gelu(strided).astype(jnp.bfloat16).reshape(GLAT // 2, GLON // 2, D)
    wide = jnp.concatenate([coarse[:, -1:], coarse, coarse[:, :1]], axis=1)
    zero_row = jnp.zeros((1, GLON // 2 + 2, D), jnp.bfloat16)
    full = jnp.concatenate([zero_row, wide, zero_row], axis=0).astype(jnp.float32)
    depth = jnp.zeros((GLAT // 2, GLON // 2, D), jnp.float32)
    for row_at in range(3):
        for col_at in range(3):
            depth = depth + full[row_at:row_at + GLAT // 2, col_at:col_at + GLON // 2] * depth_weight[3 * row_at + col_at]
    mixed = coarse.astype(jnp.float32) + depth
    return layer_norm(mixed, norm_gain).astype(jnp.bfloat16)
```

```python
import functools

import jax
import jax.numpy as jnp
from jax import lax
from jax.experimental import pallas as pl
from jax.experimental.pallas import tpu as pltpu
from jax.sharding import PartitionSpec as P

D = 256
OBS_VARS = 31
WIDTH = OBS_VARS + 1
SLOTS = 12
TLAT = 16
TLON = 32
HALF = TLON // 2
LANES = 128
VMEM_LIMIT = 48 << 20


def whole(shape):
    return pl.BlockSpec(shape, lambda *_: (0,) * len(shape))


def pack_kernel(count_ref, values_ref, offset_ref, cell_ref, slot_ref, out_ref):
    tiles, _, capacity = values_ref.shape
    halves = capacity // LANES
    position = lax.broadcasted_iota(jnp.int32, (1, capacity), 1)
    cell = cell_ref[...]
    column = cell % TLON
    row = (cell // TLON).astype(jnp.float32)
    code = ((column % 2) * HALF + column // 2).astype(jnp.float32)
    slot = slot_ref[...].astype(jnp.float32)
    for d in range(tiles):
        offset = offset_ref[d]
        radius = offset[0:1] * offset[0:1] + offset[1:2] * offset[1:2]
        weight = jnp.where(position < count_ref[0, d], jnp.exp(-2.0 * radius), 0.0)
        scaled = values_ref[d].astype(jnp.float32) * weight
        packed = jnp.concatenate([scaled, weight], axis=0).astype(jnp.bfloat16)
        codes = [
            part[d : d + 1, h * LANES : (h + 1) * LANES]
            for part in (slot, row, code)
            for h in range(halves)
        ]
        codes.append(jnp.zeros((8 - len(codes), LANES), jnp.float32))
        for h in range(halves):
            out_ref[d, h * WIDTH : (h + 1) * WIDTH, :] = packed[:, h * LANES : (h + 1) * LANES]
        out_ref[d, halves * WIDTH :, :] = jnp.concatenate(codes, axis=0).astype(jnp.bfloat16)


def pack(obs_values, obs_offset, obs_cell, obs_slot, obs_count):
    tiles, _, capacity = obs_values.shape
    rows = capacity // LANES * WIDTH + 8
    return pl.pallas_call(
        pack_kernel,
        grid=(1,),
        in_specs=[
            pl.BlockSpec(memory_space=pltpu.SMEM),
            whole(obs_values.shape),
            whole(obs_offset.shape),
            whole(obs_cell.shape),
            whole(obs_slot.shape),
        ],
        out_specs=whole((tiles, rows, LANES)),
        out_shape=jax.ShapeDtypeStruct((tiles, rows, LANES), jnp.bfloat16),
        compiler_params=pltpu.CompilerParams(vmem_limit_bytes=VMEM_LIMIT),
    )(obs_count, obs_values, obs_offset, obs_cell, obs_slot)


def scatter_kernel(
    x_ref, weight_ref, bias_ref, tile_ref, east_ref, west_ref, hot, spread, total, *, steps
):
    step = pl.program_id(0)
    sources = x_ref.shape[0]
    halves = x_ref.shape[1] // WIDTH
    bins = SLOTS * WIDTH
    iota = lax.broadcasted_iota(jnp.int32, (TLON, LANES), 0).astype(jnp.float32)
    zero = jnp.zeros((TLON, LANES), jnp.bfloat16)
    for g in range(sources):
        codes = x_ref[g, halves * WIDTH :, :].astype(jnp.float32)
        for h in range(halves):
            lanes = slice((halves * g + h) * LANES, (halves * g + h + 1) * LANES)
            value = x_ref[g, h * WIDTH : (h + 1) * WIDTH, :]
            slot = codes[h : h + 1]
            row = codes[halves + h : halves + h + 1]
            column = codes[2 * halves + h : 2 * halves + h + 1]
            lower = jnp.where(row >= TLAT // 2, 1.0, 0.0)
            within = row - lower * (TLAT // 2)
            group = slot + lower * SLOTS
            group = jnp.broadcast_to(group, (WIDTH, LANES)).astype(jnp.bfloat16)
            within = jnp.broadcast_to(within, (TLON, LANES)).astype(jnp.bfloat16)
            column = jnp.where(iota == column, 1.0, 0.0).astype(jnp.bfloat16)
            for r in range(TLAT // 2):
                hot[r * TLON : (r + 1) * TLON, lanes] = jnp.where(
                    within == jnp.bfloat16(r), column, zero
                )
            for s in range(2 * SLOTS):
                spread[s * WIDTH : (s + 1) * WIDTH, lanes] = jnp.where(
                    group == jnp.bfloat16(s), value, zero
                )
    part = lax.dot_general(
        spread[...], hot[...], (((1,), (1,)), ((), ())), preferred_element_type=jnp.float32
    )

    @pl.when(step == 0)
    def _():
        total[...] = part

    @pl.when(step > 0)
    def _():
        total[...] += part

    @pl.when(step == steps - 1)
    def _():
        for half in range(2):
            rows = []
            for s in range(SLOTS):
                first = half * bins + s * WIDTH
                block = total[first : first + WIDTH, :]
                density = block[OBS_VARS:WIDTH, :]
                inverse = 1.0 / (1.0 + density)
                channel = lax.broadcasted_iota(jnp.int32, block.shape, 0)
                rows.append(
                    jnp.where(channel == OBS_VARS, block, block * inverse).astype(jnp.bfloat16)
                )
            gridded = jnp.concatenate(rows, axis=0)
            projected = lax.dot_general(
                gridded,
                weight_ref[...],
                (((0,), (0,)), ((), ())),
                preferred_element_type=jnp.float32,
            )
            embedded = jax.nn.gelu(projected + bias_ref[...]).reshape(TLAT // 2, TLON, D)
            at = slice(half * (TLAT // 2), (half + 1) * (TLAT // 2))
            tile_ref[at] = embedded.astype(jnp.bfloat16)
            last = [embedded[:, c : c + 1] for c in (TLON - 2, HALF - 1, TLON - 1)]
            first = [embedded[:, c : c + 1] for c in (0, HALF)]
            east_ref[at] = jnp.concatenate(last, axis=1).astype(jnp.bfloat16)
            west_ref[at] = jnp.concatenate(first, axis=1).astype(jnp.bfloat16)


def scatter(arrived, embed_weight, embed_bias):
    tiles, rows, _ = arrived.shape
    sources = min(tiles, 32)
    steps = tiles // sources
    depth = sources * (rows // WIDTH) * LANES
    bins = SLOTS * WIDTH
    shapes = [(TLAT, TLON, D), (TLAT, 3, D), (TLAT, 2, D)]
    return pl.pallas_call(
        functools.partial(scatter_kernel, steps=steps),
        grid=(steps,),
        in_specs=[
            pl.BlockSpec((sources, rows, LANES), lambda i: (i, 0, 0)),
            whole(embed_weight.shape),
            whole((1, D)),
        ],
        out_specs=[whole(shape) for shape in shapes],
        out_shape=[jax.ShapeDtypeStruct(shape, jnp.bfloat16) for shape in shapes],
        scratch_shapes=[
            pltpu.VMEM((TLAT // 2 * TLON, depth), jnp.bfloat16),
            pltpu.VMEM((2 * bins, depth), jnp.bfloat16),
            pltpu.VMEM((2 * bins, TLAT // 2 * TLON), jnp.float32),
        ],
        compiler_params=pltpu.CompilerParams(vmem_limit_bytes=VMEM_LIMIT),
    )(arrived, embed_weight, embed_bias.reshape(1, D))


def finish_kernel(
    place_ref,
    tile_ref,
    west_ref,
    east_ref,
    north_ref,
    south_ref,
    weight_ref,
    bias_ref,
    depth_ref,
    gain_ref,
    out_ref,
    even,
    odd,
    coarse_ref,
):
    def place(rows, tile, west, east):
        even[rows, 0:1] = west[:, 1:2]
        even[rows, 1 : HALF + 1] = tile[:, :HALF]
        even[rows, HALF + 1 : HALF + 2] = east[:, 0:1]
        odd[rows, 0:1] = west[:, 0:1]
        odd[rows, 1:2] = west[:, 2:3]
        odd[rows, 2 : HALF + 2] = tile[:, HALF:]
        odd[rows, HALF + 2 : HALF + 3] = east[:, 1:2]

    north = north_ref[...].astype(jnp.float32)
    south = south_ref[...].astype(jnp.float32)
    place(
        slice(3, TLAT + 3),
        tile_ref[...].astype(jnp.float32),
        west_ref[...].astype(jnp.float32),
        east_ref[...].astype(jnp.float32),
    )
    place(slice(0, 3), north[:, :TLON], north[:, TLON : TLON + 3], north[:, TLON + 3 :])
    place(
        slice(TLAT + 3, TLAT + 5), south[:, :TLON], south[:, TLON : TLON + 3], south[:, TLON + 3 :]
    )
    out_rows = TLAT // 2
    span = 24
    pieces = []
    for a in range(3):
        for source, at in ((odd, 0), (even, 0), (odd, 1)):
            rows = [source[2 * p + a, at : at + span, :] for p in range(out_rows + 2)]
            pieces.append(jnp.concatenate(rows, axis=0).astype(jnp.bfloat16))
    strided = jnp.dot(
        jnp.concatenate(pieces, axis=1), weight_ref[...], preferred_element_type=jnp.float32
    )
    coarse = jax.nn.gelu(strided + bias_ref[...]).astype(jnp.bfloat16).astype(jnp.float32)
    coarse_ref[...] = coarse.reshape(out_rows + 2, span, D)

    @pl.when(place_ref[0] == 0)
    def _():
        coarse_ref[0] = jnp.zeros((span, D), jnp.float32)

    @pl.when(place_ref[0] == place_ref[1] - 1)
    def _():
        coarse_ref[out_rows + 1] = jnp.zeros((span, D), jnp.float32)

    mixed = coarse_ref[1 : out_rows + 1, 1 : HALF + 1]
    for a in range(3):
        for c in range(3):
            tap = depth_ref[3 * a + c : 3 * a + c + 1, :]
            mixed = mixed + coarse_ref[a : a + out_rows, c : c + HALF] * tap
    centre = mixed - jnp.mean(mixed, axis=-1, keepdims=True)
    variance = jnp.mean(centre * centre, axis=-1, keepdims=True)
    out_ref[...] = (centre * lax.rsqrt(variance + 1e-05) * gain_ref[...]).astype(jnp.bfloat16)


def finish(place, tile, west, east, north, south, stride_weight, stride_bias, depth_weight, gain):
    arrays = [
        tile,
        west,
        east,
        north,
        south,
        stride_weight.reshape(9 * D, D),
        stride_bias.reshape(1, D),
        depth_weight,
        gain.reshape(1, D),
    ]
    out = (TLAT // 2, HALF, D)
    return pl.pallas_call(
        finish_kernel,
        grid=(1,),
        in_specs=[pl.BlockSpec(memory_space=pltpu.SMEM)] + [whole(a.shape) for a in arrays],
        out_specs=whole(out),
        out_shape=jax.ShapeDtypeStruct(out, jnp.bfloat16),
        scratch_shapes=[
            pltpu.VMEM((TLAT + 5, 24, D), jnp.float32),
            pltpu.VMEM((TLAT + 5, 32, D), jnp.float32),
            pltpu.VMEM((TLAT // 2 + 2, 24, D), jnp.float32),
        ],
        compiler_params=pltpu.CompilerParams(vmem_limit_bytes=VMEM_LIMIT),
    )(place, *arrays)


def shifted(value, axis, by, wrap):
    size = lax.axis_size(axis)
    pairs = [(i, (i + by) % size) for i in range(size) if wrap or 0 <= i + by < size]
    return lax.ppermute(value, axis, pairs)


def on_device(
    obs_values,
    obs_offset,
    obs_cell,
    obs_slot,
    obs_count,
    embed_weight,
    embed_bias,
    stride_weight,
    stride_bias,
    depth_weight,
    norm_gain,
):
    packed = pack(obs_values, obs_offset, obs_cell, obs_slot, obs_count)
    arrived = lax.all_to_all(packed, ("lon", "lat"), split_axis=0, concat_axis=0, tiled=True)
    tile, last, first = scatter(arrived, embed_weight, embed_bias)
    west = shifted(last, "lon", 1, True)
    east = shifted(first, "lon", -1, True)
    framed = jnp.concatenate([tile, west, east], axis=1)
    north = shifted(framed[TLAT - 3 :], "lat", 1, False)
    south = shifted(framed[:2], "lat", -1, False)
    place = jnp.stack([lax.axis_index("lat"), jnp.int32(lax.axis_size("lat"))])
    return finish(
        place,
        tile,
        west,
        east,
        north,
        south,
        stride_weight,
        stride_bias,
        depth_weight,
        norm_gain,
    )


def solution(mesh):
    placed = (
        P(("lon", "lat"), None, None),
        P(("lon", "lat"), None, None),
        P(("lon", "lat"), None),
        P(("lon", "lat"), None),
        P(("lon", "lat"), None),
        P(),
        P(),
        P(),
        P(),
        P(),
        P(),
    )
    return jax.shard_map(
        on_device, mesh=mesh, in_specs=placed, out_specs=P("lat", "lon", None), check_vma=False
    )
```

```python
import functools

import jax
import jax.numpy as jnp
from jax import lax
from jax.experimental import pallas as pl
from jax.experimental.pallas import tpu as pltpu
from jax.sharding import PartitionSpec as P

D = 256
OBS_VARS = 31
WIDTH = OBS_VARS + 1
SLOTS = 12
BINS = SLOTS * WIDTH
TLAT = 16
TLON = 32
HALF = TLON // 2
ROWS = TLAT // 2
LANES = 128
GROUP = 16
CHUNK = 8
SPAN = 24
FRAME = TLON + 5

ANY = pl.BlockSpec(memory_space=pl.ANY)
VMEM = pl.BlockSpec(memory_space=pltpu.VMEM)


def pack_kernel(
    count_hbm,
    values_hbm,
    offset_hbm,
    cell_hbm,
    slot_hbm,
    out_hbm,
    count,
    values,
    offset,
    cell,
    slot,
    rows,
    out,
    here,
    sent,
):
    tiles, capacity = cell.shape
    halves = capacity // LANES
    stride = halves * WIDTH + 8
    groups = tiles // GROUP

    def at(j):
        return pl.ds(j * GROUP, GROUP)

    pairs = ((count_hbm, count), (offset_hbm, offset), (cell_hbm, cell), (slot_hbm, slot))
    small = [
        pltpu.make_async_copy(a, b, here.at[groups + i]) for i, (a, b) in enumerate(pairs)
    ]
    large = [
        pltpu.make_async_copy(values_hbm.at[:, at(j)], values.at[:, at(j)], here.at[j])
        for j in range(groups)
    ]
    for copy in small + large:
        copy.start()
    for copy in small:
        copy.wait()
    square = (tiles, tiles)
    diagonal = lax.broadcasted_iota(jnp.int32, square, 0) == lax.broadcasted_iota(
        jnp.int32, square, 1
    )
    counts = jnp.sum(jnp.where(diagonal, count[...], 0), axis=1, keepdims=True)
    position = lax.broadcasted_iota(jnp.int32, (tiles, capacity), 1)
    dy, dx = offset[:, 0, :], offset[:, 1, :]
    weight = jnp.where(position < counts, jnp.exp(-2.0 * (dy * dy + dx * dx)), 0.0)
    column = cell[...] % TLON
    codes = (
        slot[...].astype(jnp.float32),
        (cell[...] // TLON).astype(jnp.float32),
        ((column % 2) * HALF + column // 2).astype(jnp.float32),
    )
    zero = jnp.zeros((GROUP, LANES), jnp.float32)
    base = halves * WIDTH
    sends = []
    for j in range(groups):
        own = slice(j * GROUP, (j + 1) * GROUP)

        def put(row, value, h, first=j * GROUP * stride):
            rows[pl.ds(first + row, GROUP, stride=stride), :] = value[
                :, h * LANES : (h + 1) * LANES
            ]

        for h in range(halves):
            put(h * WIDTH + OBS_VARS, weight[own], h)
            for i, code in enumerate(codes):
                put(base + i * halves + h, code[own], h)
        for r in range(len(codes) * halves, 8):
            put(base + r, zero, 0)
        large[j].wait()
        for k in range(OBS_VARS):
            scaled = values[k, own, :].astype(jnp.float32) * weight[own]
            for h in range(halves):
                put(h * WIDTH + k, scaled, h)
        for d in range(j * GROUP, (j + 1) * GROUP):
            out[d] = rows[d * stride : (d + 1) * stride, :].astype(jnp.bfloat16)
        sends.append(pltpu.make_async_copy(out.at[at(j)], out_hbm.at[at(j)], sent.at[j]))
        sends[-1].start()
    for copy in sends:
        copy.wait()


def pack(obs_values, obs_offset, obs_cell, obs_slot, obs_count):
    tiles, _, capacity = obs_values.shape
    stride = capacity // LANES * WIDTH + 8
    values = jnp.transpose(obs_values, (1, 0, 2))
    shape = (tiles, stride, LANES)
    arrays = (obs_count, values, obs_offset, obs_cell, obs_slot)
    return pl.pallas_call(
        pack_kernel,
        in_specs=[ANY] * len(arrays),
        out_specs=ANY,
        out_shape=jax.ShapeDtypeStruct(shape, jnp.bfloat16),
        scratch_shapes=[pltpu.VMEM(a.shape, a.dtype) for a in arrays]
        + [
            pltpu.VMEM((tiles * stride, LANES), jnp.float32),
            pltpu.VMEM(shape, jnp.bfloat16),
            pltpu.SemaphoreType.DMA((tiles // GROUP + 4,)),
            pltpu.SemaphoreType.DMA((tiles // GROUP,)),
        ],
        compiler_params=pltpu.CompilerParams(vmem_limit_bytes=60 << 20),
    )(*arrays)


def scatter_kernel(x_ref, weight_ref, bias_ref, tile_ref, last_ref, first_ref, hot, spread, total):
    tiles, rows, _ = x_ref.shape
    halves = rows // WIDTH
    iota = lax.broadcasted_iota(jnp.int32, (TLON, LANES), 0).astype(jnp.float32)
    zero = jnp.zeros((TLON, LANES), jnp.bfloat16)

    def part(source, first):
        for g in range(CHUNK):
            codes = x_ref[source + g, halves * WIDTH :, :].astype(jnp.float32)
            for h in range(halves):
                at = first + (halves * g + h) * LANES
                lanes = slice(at, at + LANES)
                value = x_ref[source + g, h * WIDTH : (h + 1) * WIDTH, :]
                slot = codes[h : h + 1]
                row = codes[halves + h : halves + h + 1]
                column = codes[2 * halves + h : 2 * halves + h + 1]
                lower = jnp.where(row >= ROWS, 1.0, 0.0)
                group = jnp.broadcast_to(slot + lower * SLOTS, (WIDTH, LANES))
                within = jnp.broadcast_to(row - lower * ROWS, (TLON, LANES))
                group = group.astype(jnp.bfloat16)
                within = within.astype(jnp.bfloat16)
                column = jnp.where(iota == column, 1.0, 0.0).astype(jnp.bfloat16)
                for r in range(ROWS):
                    hot[r * TLON : (r + 1) * TLON, lanes] = jnp.where(
                        within == jnp.bfloat16(r), column, zero
                    )
                for s in range(2 * SLOTS):
                    spread[s * WIDTH : (s + 1) * WIDTH, lanes] = jnp.where(
                        group == jnp.bfloat16(s), value, zero
                    )
        lanes = slice(first, first + CHUNK * halves * LANES)
        return lax.dot_general(
            spread[:, lanes],
            hot[:, lanes],
            (((1,), (1,)), ((), ())),
            preferred_element_type=jnp.float32,
        )

    def summed(start):
        chunks = range(hot.shape[1] // (CHUNK * halves * LANES))
        return functools.reduce(
            jnp.add, [part(start + c * CHUNK, c * CHUNK * halves * LANES) for c in chunks]
        )

    sources = hot.shape[1] // (halves * LANES)
    if tiles == sources:
        total[...] = summed(0)
    else:
        total[...] = jnp.zeros(total.shape, jnp.float32)

        @pl.loop(0, tiles // sources)
        def _(step):
            total[...] += summed(step * sources)

    for half in range(2):
        groups = []
        for s in range(SLOTS):
            first = half * BINS + s * WIDTH
            block = total[first : first + WIDTH, :]
            inverse = 1.0 / (1.0 + block[OBS_VARS:WIDTH, :])
            channel = lax.broadcasted_iota(jnp.int32, block.shape, 0)
            ratio = jnp.where(channel == OBS_VARS, block, block * inverse)
            groups.append(ratio.astype(jnp.bfloat16))
        projected = lax.dot_general(
            jnp.concatenate(groups, axis=0),
            weight_ref[...],
            (((0,), (0,)), ((), ())),
            preferred_element_type=jnp.float32,
        )
        embedded = jax.nn.gelu(projected + bias_ref[...]).reshape(ROWS, TLON, D)
        at = slice(half * ROWS, (half + 1) * ROWS)
        tile_ref[at] = embedded.astype(jnp.bfloat16)
        last = [embedded[:, c : c + 1] for c in (TLON - 2, HALF - 1, TLON - 1)]
        first = [embedded[:, c : c + 1] for c in (0, HALF)]
        last_ref[at] = jnp.concatenate(last, axis=1).astype(jnp.bfloat16)
        first_ref[at] = jnp.concatenate(first, axis=1).astype(jnp.bfloat16)


def scatter(arrived, embed_weight, embed_bias):
    tiles, rows, _ = arrived.shape
    depth = min(tiles, 32) * (rows // WIDTH) * LANES
    shapes = [(TLAT, TLON, D), (TLAT, 3, D), (TLAT, 2, D)]
    return pl.pallas_call(
        scatter_kernel,
        in_specs=[VMEM] * 3,
        out_specs=[VMEM] * 3,
        out_shape=[jax.ShapeDtypeStruct(shape, jnp.bfloat16) for shape in shapes],
        scratch_shapes=[
            pltpu.VMEM((ROWS * TLON, depth), jnp.bfloat16),
            pltpu.VMEM((2 * BINS, depth), jnp.bfloat16),
            pltpu.VMEM((2 * BINS, ROWS * TLON), jnp.float32),
        ],
        compiler_params=pltpu.CompilerParams(vmem_limit_bytes=32 << 20),
    )(arrived, embed_weight, embed_bias.reshape(1, D))


def put_rows(even, odd, rows, tile, west, east):
    even[rows, 0:1] = west[:, 1:2]
    even[rows, 1 : HALF + 1] = tile[:, :HALF]
    even[rows, HALF + 1 : HALF + 2] = east[:, 0:1]
    odd[rows, 0:1] = west[:, 0:1]
    odd[rows, 1:2] = west[:, 2:3]
    odd[rows, 2 : HALF + 2] = tile[:, HALF:]
    odd[rows, HALF + 2 : HALF + 3] = east[:, 1:2]


def strided_rows(even, odd, starts, weight_ref, bias_ref):
    pieces = []
    for a in range(3):
        for source, at in ((odd, 0), (even, 0), (odd, 1)):
            rows = [source[start + a, at : at + SPAN, :] for start in starts]
            pieces.append(jnp.concatenate(rows, axis=0).astype(jnp.bfloat16))
    strided = jnp.dot(
        jnp.concatenate(pieces, axis=1), weight_ref[...], preferred_element_type=jnp.float32
    )
    coarse = jax.nn.gelu(strided + bias_ref[...]).astype(jnp.bfloat16)
    return coarse.astype(jnp.float32).reshape(len(starts), SPAN, D)


def finished(coarse, first, count, depth_ref, gain_ref):
    mixed = coarse[first + 1 : first + count + 1, 1 : HALF + 1]
    for a in range(3):
        for c in range(3):
            tap = depth_ref[3 * a + c : 3 * a + c + 1, :]
            mixed = mixed + coarse[first + a : first + a + count, c : c + HALF] * tap
    centre = mixed - jnp.mean(mixed, axis=-1, keepdims=True)
    variance = jnp.mean(centre * centre, axis=-1, keepdims=True)
    return (centre * lax.rsqrt(variance + 1e-05) * gain_ref[...]).astype(jnp.bfloat16)


def inner_kernel(
    tile_ref,
    west_ref,
    east_ref,
    weight_ref,
    bias_ref,
    depth_ref,
    gain_ref,
    upper_ref,
    lower_ref,
    out_ref,
    even,
    odd,
    coarse,
):
    tile, west, east = (r[...].astype(jnp.float32) for r in (tile_ref, west_ref, east_ref))
    put_rows(even, odd, slice(0, TLAT), tile, west, east)
    coarse[...] = strided_rows(even, odd, range(1, TLAT - 2, 2), weight_ref, bias_ref)
    upper_ref[...] = coarse[0:2]
    lower_ref[...] = coarse[ROWS - 3 : ROWS - 1]
    out_ref[...] = finished(coarse, 0, ROWS - 3, depth_ref, gain_ref)


def inner(*arrays):
    pair = jax.ShapeDtypeStruct((2, SPAN, D), jnp.float32)
    return pl.pallas_call(
        inner_kernel,
        in_specs=[VMEM] * len(arrays),
        out_specs=[VMEM] * 3,
        out_shape=[pair, pair, jax.ShapeDtypeStruct((ROWS - 3, HALF, D), jnp.bfloat16)],
        scratch_shapes=[
            pltpu.VMEM((TLAT, SPAN, D), jnp.float32),
            pltpu.VMEM((TLAT, SPAN + 8, D), jnp.float32),
            pltpu.VMEM((ROWS - 1, SPAN, D), jnp.float32),
        ],
        compiler_params=pltpu.CompilerParams(vmem_limit_bytes=16 << 20),
        cost_estimate=pl.CostEstimate(
            flops=2 * 7 * SPAN * 9 * D * D, bytes_accessed=2 << 20, transcendentals=0
        ),
    )(*arrays)


def outer_kernel(
    place_ref,
    upper_ref,
    lower_ref,
    done_ref,
    tile_ref,
    west_ref,
    east_ref,
    pair_ref,
    other_ref,
    weight_ref,
    bias_ref,
    depth_ref,
    gain_ref,
    out_hbm,
    even,
    odd,
    coarse,
    top,
    bottom,
    sent,
):
    inner_copy = pltpu.make_async_copy(done_ref, out_hbm.at[2 : ROWS - 1], sent.at[0])
    inner_copy.start()
    paired, other = (r[...].astype(jnp.float32) for r in (pair_ref, other_ref))
    lower, above, below = (place_ref[i : i + 1] for i in range(3))
    upper = 1.0 - lower
    north = paired * (lower * above) + other * (upper * above)
    south = paired * upper + other * lower
    for at, source, rows in ((0, north, slice(0, 3)), (6, south, slice(0, 2))):
        part = source[rows]
        put_rows(
            even,
            odd,
            slice(at, at + rows.stop),
            part[:, :TLON],
            part[:, TLON : TLON + 3],
            part[:, TLON + 3 :],
        )
    for at, rows in ((3, slice(0, 2)), (5, slice(TLAT - 1, TLAT))):
        put_rows(
            even,
            odd,
            slice(at, at + rows.stop - rows.start),
            tile_ref[rows].astype(jnp.float32),
            west_ref[rows].astype(jnp.float32),
            east_ref[rows].astype(jnp.float32),
        )
    edge = strided_rows(even, odd, (0, 2, 5), weight_ref, bias_ref)
    coarse[0] = edge[0] * above
    coarse[1] = edge[1]
    coarse[2:4] = upper_ref[...]
    coarse[4:6] = lower_ref[...]
    coarse[6] = edge[2] * below
    top[...] = finished(coarse, 0, 2, depth_ref, gain_ref)
    bottom[...] = finished(coarse, 4, 1, depth_ref, gain_ref)
    copies = [
        inner_copy,
        pltpu.make_async_copy(top, out_hbm.at[0:2], sent.at[1]),
        pltpu.make_async_copy(bottom, out_hbm.at[ROWS - 1 : ROWS], sent.at[2]),
    ]
    for copy in copies[1:]:
        copy.start()
    for copy in copies:
        copy.wait()


def outer(*arrays):
    return pl.pallas_call(
        outer_kernel,
        in_specs=[VMEM] * len(arrays),
        out_specs=ANY,
        out_shape=jax.ShapeDtypeStruct((ROWS, HALF, D), jnp.bfloat16),
        scratch_shapes=[
            pltpu.VMEM((8, SPAN, D), jnp.float32),
            pltpu.VMEM((8, SPAN + 8, D), jnp.float32),
            pltpu.VMEM((7, SPAN, D), jnp.float32),
            pltpu.VMEM((2, HALF, D), jnp.bfloat16),
            pltpu.VMEM((1, HALF, D), jnp.bfloat16),
            pltpu.SemaphoreType.DMA((3,)),
        ],
        compiler_params=pltpu.CompilerParams(vmem_limit_bytes=16 << 20),
    )(*arrays)


def on_device(
    obs_values,
    obs_offset,
    obs_cell,
    obs_slot,
    obs_count,
    embed_weight,
    embed_bias,
    stride_weight,
    stride_bias,
    depth_weight,
    norm_gain,
):
    lon_count, lat_count = lax.axis_size("lon"), lax.axis_size("lat")
    lat = lax.axis_index("lat")
    packed = pack(obs_values, obs_offset, obs_cell, obs_slot, obs_count)
    arrived = lax.all_to_all(packed, ("lon", "lat"), split_axis=0, concat_axis=0, tiled=True)
    tile, last, first = scatter(arrived, embed_weight, embed_bias)
    ring = [(i, (i + 1) % lon_count) for i in range(lon_count)]
    west = lax.ppermute(last, "lon", ring)
    east = lax.ppermute(first, "lon", [(j, i) for i, j in ring])
    weight, bias = stride_weight.reshape(9 * D, D), stride_bias.reshape(1, D)
    framed = jnp.concatenate([tile, west, east], axis=1)
    top, bottom = framed[:3], framed[TLAT - 3 :]
    lower = lat % 2 == 1
    pairs = [(i, i + 1) for i in range(0, lat_count - 1, 2)]
    others = [(i, (i + 1) % lat_count) for i in range(1, lat_count, 2)]
    other = lax.ppermute(
        jnp.where(lower, bottom, top), "lat", others + [(j, i) for i, j in others]
    )
    paired = lax.ppermute(
        jnp.where(lower, top, bottom), "lat", pairs + [(j, i) for i, j in pairs]
    )
    gain = norm_gain.reshape(1, D)
    place = jnp.stack([lower, lat > 0, lat < lat_count - 1]).astype(jnp.float32)
    place = jnp.broadcast_to(place[:, None], (3, D))
    inside = inner(tile, west, east, weight, bias, depth_weight, gain)
    return outer(
        place, *inside, tile, west, east, paired, other, weight, bias, depth_weight, gain
    )


def solution(mesh):
    placed = (
        P(("lon", "lat"), None, None),
        P(("lon", "lat"), None, None),
        P(("lon", "lat"), None),
        P(("lon", "lat"), None),
        P(("lon", "lat"), None),
        P(),
        P(),
        P(),
        P(),
        P(),
        P(),
    )
    return jax.shard_map(
        on_device, mesh=mesh, in_specs=placed, out_specs=P("lat", "lon", None), check_vma=False
    )
```

```python
import functools

import jax
import jax.numpy as jnp
from jax import lax
from jax.experimental import pallas as pl
from jax.experimental.pallas import tpu as pltpu
from jax.sharding import PartitionSpec as P

D = 256
OBS_VARS = 31
WIDTH = OBS_VARS + 1
SLOTS = 12
BINS = SLOTS * WIDTH
TLAT = 16
TLON = 32
HALF = TLON // 2
ROWS = TLAT // 2
LANES = 128
GROUP = 16
TILE = 4
CHUNK = 32
SPAN = 24
FRAME = TLON + 5

ANY = pl.BlockSpec(memory_space=pl.ANY)
VMEM = pl.BlockSpec(memory_space=pltpu.VMEM)


def pack_kernel(
    count_hbm,
    values_hbm,
    offset_hbm,
    cell_hbm,
    slot_hbm,
    out_hbm,
    count,
    values,
    offset,
    cell,
    slot,
    rows,
    out,
    here,
    sent,
):
    tiles, capacity = cell.shape
    halves = capacity // LANES
    used = out.shape[1] * TILE
    stride = rows.shape[0] // tiles
    groups = tiles // GROUP

    def at(j):
        return pl.ds(j * GROUP, GROUP)

    pairs = ((count_hbm, count), (offset_hbm, offset), (cell_hbm, cell), (slot_hbm, slot))
    small = [
        pltpu.make_async_copy(a, b, here.at[groups + i]) for i, (a, b) in enumerate(pairs)
    ]
    large = [
        pltpu.make_async_copy(values_hbm.at[:, at(j)], values.at[:, at(j)], here.at[j])
        for j in range(groups)
    ]
    for copy in small + large:
        copy.start()
    for copy in small:
        copy.wait()
    square = (tiles, tiles)
    diagonal = lax.broadcasted_iota(jnp.int32, square, 0) == lax.broadcasted_iota(
        jnp.int32, square, 1
    )
    counts = jnp.sum(jnp.where(diagonal, count[...], 0), axis=1, keepdims=True)
    position = lax.broadcasted_iota(jnp.int32, (tiles, capacity), 1)
    dy, dx = offset[:, 0, :], offset[:, 1, :]
    weight = jnp.where(position < counts, jnp.exp(-2.0 * (dy * dy + dx * dx)), 0.0)
    column = cell[...] % TLON
    pair = column // 2
    middle = (pair >= ROWS // 2) & (pair < 3 * ROWS // 2)
    within = pair - jnp.where(pair < ROWS // 2, 0, jnp.where(middle, ROWS // 2, ROWS))
    codes = (
        (slot[...] * TLAT + cell[...] // TLON).astype(jnp.float32),
        (jnp.where(middle, HALF, 0) + (column % 2) * ROWS + within).astype(jnp.float32),
    )
    base = halves * WIDTH
    sends = []
    for j in range(groups):
        own = slice(j * GROUP, (j + 1) * GROUP)

        def put(row, value, h, first=j * GROUP * stride):
            rows[pl.ds(first + row, GROUP, stride=stride), :] = value[
                :, h * LANES : (h + 1) * LANES
            ]

        for h in range(halves):
            put(h * WIDTH + OBS_VARS, weight[own], h)
            for i, code in enumerate(codes):
                put(base + i * halves + h, code[own], h)
        large[j].wait()
        for k in range(OBS_VARS):
            scaled = values[k, own, :].astype(jnp.float32) * weight[own]
            for h in range(halves):
                put(h * WIDTH + k, scaled, h)
        for d in range(j * GROUP, (j + 1) * GROUP):
            for i in range(used // TILE):
                first = d * stride + i * TILE
                out[d, i] = rows[first : first + TILE, :].astype(jnp.bfloat16)
        sends.append(pltpu.make_async_copy(out.at[at(j)], out_hbm.at[at(j)], sent.at[j]))
        sends[-1].start()
    for copy in sends:
        copy.wait()


def pack(obs_values, obs_offset, obs_cell, obs_slot, obs_count):
    tiles, _, capacity = obs_values.shape
    used = capacity // LANES * (WIDTH + 2)
    stride = -(-used // 8) * 8
    values = jnp.transpose(obs_values, (1, 0, 2))
    shape = (tiles, used // TILE, TILE, LANES)
    arrays = (obs_count, values, obs_offset, obs_cell, obs_slot)
    return pl.pallas_call(
        pack_kernel,
        in_specs=[ANY] * len(arrays),
        out_specs=ANY,
        out_shape=jax.ShapeDtypeStruct(shape, jnp.bfloat16),
        scratch_shapes=[pltpu.VMEM(a.shape, a.dtype) for a in arrays]
        + [
            pltpu.VMEM((tiles * stride, LANES), jnp.float32),
            pltpu.VMEM(shape, jnp.bfloat16),
            pltpu.SemaphoreType.DMA((tiles // GROUP + 4,)),
            pltpu.SemaphoreType.DMA((tiles // GROUP,)),
        ],
        compiler_params=pltpu.CompilerParams(vmem_limit_bytes=60 << 20),
    )(*arrays)


def embedded_cells(x_ref, weight_ref, bias_ref, total, middle):
    tiles, blocks, _, _ = x_ref.shape
    halves = blocks * TILE // WIDTH
    step = WIDTH // TILE
    iota = lax.broadcasted_iota(jnp.int32, (HALF, LANES), 0).astype(jnp.float32)
    none = jnp.zeros((HALF, LANES), jnp.bfloat16)
    zero = jnp.zeros((WIDTH, LANES), jnp.bfloat16)

    def operands(source):
        codes = x_ref[source, halves * step].astype(jnp.float32)
        spread, hot = [], []
        for h in range(halves):
            value = x_ref[source, h * step : (h + 1) * step].reshape(WIDTH, LANES)
            code = codes[h : h + 1]
            slot = jnp.floor(code * (1.0 / TLAT))
            row = jnp.broadcast_to(code - slot * TLAT, (HALF, LANES)).astype(jnp.bfloat16)
            column = codes[halves + h : halves + h + 1]
            group = jnp.where(column >= HALF, 1.0, 0.0)
            slot = jnp.where(group == middle, slot, SLOTS)
            slot = jnp.broadcast_to(slot, (WIDTH, LANES)).astype(jnp.bfloat16)
            column = jnp.where(iota == column - group * HALF, 1.0, 0.0).astype(jnp.bfloat16)
            by_slot = [jnp.where(slot == jnp.bfloat16(s), value, zero) for s in range(SLOTS)]
            by_row = [jnp.where(row == jnp.bfloat16(r), column, none) for r in range(TLAT)]
            spread.append(jnp.concatenate(by_slot, axis=0))
            hot.append(jnp.concatenate(by_row, axis=0))
        return jnp.concatenate(spread, axis=1), jnp.concatenate(hot, axis=1)

    def summed(first, count):
        spread, hot = zip(*(operands(first + g) for g in range(count)))
        return lax.dot_general(
            jnp.concatenate(spread, axis=1),
            jnp.concatenate(hot, axis=1),
            (((1,), (1,)), ((), ())),
            preferred_element_type=jnp.float32,
        )

    count = min(tiles, CHUNK)
    total[...] = summed(0, count)

    @pl.loop(1, tiles // count)
    def _(step):
        total[...] += summed(step * count, count)

    groups = []
    for s in range(SLOTS):
        block = total[s * WIDTH : (s + 1) * WIDTH, :]
        inverse = 1.0 / (1.0 + block[OBS_VARS:WIDTH, :])
        channel = lax.broadcasted_iota(jnp.int32, block.shape, 0)
        ratio = jnp.where(channel == OBS_VARS, block, block * inverse)
        groups.append(ratio.astype(jnp.bfloat16))
    projected = lax.dot_general(
        jnp.concatenate(groups, axis=0),
        weight_ref[...],
        (((0,), (0,)), ((), ())),
        preferred_element_type=jnp.float32,
    )
    return jax.nn.gelu(projected + bias_ref[...]).reshape(TLAT, HALF, D)


def sides_kernel(x_ref, weight_ref, bias_ref, sides_ref, last_ref, first_ref, total):
    sides = embedded_cells(x_ref, weight_ref, bias_ref, total, 0.0)
    sides_ref[...] = sides
    last = [sides[:, c : c + 1] for c in (HALF - 2, ROWS - 1, HALF - 1)]
    first = [sides[:, c : c + 1] for c in (0, ROWS)]
    last_ref[...] = jnp.concatenate(last, axis=1).astype(jnp.bfloat16)
    first_ref[...] = jnp.concatenate(first, axis=1).astype(jnp.bfloat16)


def middle_kernel(x_ref, weight_ref, bias_ref, sides_ref, tile_ref, total):
    middle = embedded_cells(x_ref, weight_ref, bias_ref, total, 1.0)
    sides = sides_ref[...]
    quarter = ROWS // 2
    whole = []
    for parity in range(2):
        at = parity * ROWS
        whole += [
            sides[:, at : at + quarter],
            middle[:, at : at + ROWS],
            sides[:, at + quarter : at + ROWS],
        ]
    tile_ref[...] = jnp.concatenate(whole, axis=1).astype(jnp.bfloat16)


def scatter(kernel, arrived, embed_weight, embed_bias, *more, outs):
    tiles = arrived.shape[0]
    return pl.pallas_call(
        kernel,
        in_specs=[VMEM] * (3 + len(more)),
        out_specs=[VMEM] * len(outs),
        out_shape=outs,
        scratch_shapes=[pltpu.VMEM((BINS, TLAT * HALF), jnp.float32)],
        compiler_params=pltpu.CompilerParams(vmem_limit_bytes=32 << 20),
        cost_estimate=pl.CostEstimate(
            flops=2 * tiles * 256 * BINS * TLAT * HALF, bytes_accessed=4 << 20, transcendentals=0
        ),
    )(arrived, embed_weight, embed_bias.reshape(1, D), *more)


def put_rows(even, odd, rows, tile, west, east):
    even[rows, 0:1] = west[:, 1:2]
    even[rows, 1 : HALF + 1] = tile[:, :HALF]
    even[rows, HALF + 1 : HALF + 2] = east[:, 0:1]
    odd[rows, 0:1] = west[:, 0:1]
    odd[rows, 1:2] = west[:, 2:3]
    odd[rows, 2 : HALF + 2] = tile[:, HALF:]
    odd[rows, HALF + 2 : HALF + 3] = east[:, 1:2]


def strided_rows(even, odd, starts, weight_ref, bias_ref):
    pieces = []
    for a in range(3):
        for source, at in ((odd, 0), (even, 0), (odd, 1)):
            rows = [source[start + a, at : at + SPAN, :] for start in starts]
            pieces.append(jnp.concatenate(rows, axis=0).astype(jnp.bfloat16))
    strided = jnp.dot(
        jnp.concatenate(pieces, axis=1), weight_ref[...], preferred_element_type=jnp.float32
    )
    coarse = jax.nn.gelu(strided + bias_ref[...]).astype(jnp.bfloat16)
    return coarse.astype(jnp.float32).reshape(len(starts), SPAN, D)


def finished(coarse, first, count, depth_ref, gain_ref):
    mixed = coarse[first + 1 : first + count + 1, 1 : HALF + 1]
    for a in range(3):
        for c in range(3):
            tap = depth_ref[3 * a + c : 3 * a + c + 1, :]
            mixed = mixed + coarse[first + a : first + a + count, c : c + HALF] * tap
    centre = mixed - jnp.mean(mixed, axis=-1, keepdims=True)
    variance = jnp.mean(centre * centre, axis=-1, keepdims=True)
    return (centre * lax.rsqrt(variance + 1e-05) * gain_ref[...]).astype(jnp.bfloat16)


def inner_kernel(
    tile_ref,
    west_ref,
    east_ref,
    weight_ref,
    bias_ref,
    depth_ref,
    gain_ref,
    upper_ref,
    lower_ref,
    out_ref,
    even,
    odd,
    coarse,
):
    tile, west, east = (r[...].astype(jnp.float32) for r in (tile_ref, west_ref, east_ref))
    put_rows(even, odd, slice(0, TLAT), tile, west, east)
    coarse[...] = strided_rows(even, odd, range(1, TLAT - 2, 2), weight_ref, bias_ref)
    upper_ref[...] = coarse[0:2]
    lower_ref[...] = coarse[ROWS - 3 : ROWS - 1]
    out_ref[...] = finished(coarse, 0, ROWS - 3, depth_ref, gain_ref)


def inner(*arrays):
    pair = jax.ShapeDtypeStruct((2, SPAN, D), jnp.float32)
    return pl.pallas_call(
        inner_kernel,
        in_specs=[VMEM] * len(arrays),
        out_specs=[VMEM] * 3,
        out_shape=[pair, pair, jax.ShapeDtypeStruct((ROWS - 3, HALF, D), jnp.bfloat16)],
        scratch_shapes=[
            pltpu.VMEM((TLAT, SPAN, D), jnp.float32),
            pltpu.VMEM((TLAT, SPAN + 8, D), jnp.float32),
            pltpu.VMEM((ROWS - 1, SPAN, D), jnp.float32),
        ],
        compiler_params=pltpu.CompilerParams(vmem_limit_bytes=16 << 20),
        cost_estimate=pl.CostEstimate(
            flops=2 * 7 * SPAN * 9 * D * D, bytes_accessed=2 << 20, transcendentals=0
        ),
    )(*arrays)


def outer_kernel(
    place_ref,
    upper_ref,
    lower_ref,
    done_ref,
    tile_ref,
    west_ref,
    east_ref,
    pair_ref,
    other_ref,
    weight_ref,
    bias_ref,
    depth_ref,
    gain_ref,
    out_hbm,
    even,
    odd,
    coarse,
    top,
    bottom,
    sent,
):
    inner_copy = pltpu.make_async_copy(done_ref, out_hbm.at[2 : ROWS - 1], sent.at[0])
    inner_copy.start()
    paired, other = (r[...].astype(jnp.float32) for r in (pair_ref, other_ref))
    lower, above, below = (place_ref[i : i + 1] for i in range(3))
    upper = 1.0 - lower
    north = paired * (lower * above) + other * (upper * above)
    south = paired * upper + other * lower
    for at, source, rows in ((0, north, slice(0, 3)), (6, south, slice(0, 2))):
        part = source[rows]
        put_rows(
            even,
            odd,
            slice(at, at + rows.stop),
            part[:, :TLON],
            part[:, TLON : TLON + 3],
            part[:, TLON + 3 :],
        )
    for at, rows in ((3, slice(0, 2)), (5, slice(TLAT - 1, TLAT))):
        put_rows(
            even,
            odd,
            slice(at, at + rows.stop - rows.start),
            tile_ref[rows].astype(jnp.float32),
            west_ref[rows].astype(jnp.float32),
            east_ref[rows].astype(jnp.float32),
        )
    edge = strided_rows(even, odd, (0, 2, 5), weight_ref, bias_ref)
    coarse[0] = edge[0] * above
    coarse[1] = edge[1]
    coarse[2:4] = upper_ref[...]
    coarse[4:6] = lower_ref[...]
    coarse[6] = edge[2] * below
    top[...] = finished(coarse, 0, 2, depth_ref, gain_ref)
    bottom[...] = finished(coarse, 4, 1, depth_ref, gain_ref)
    copies = [
        inner_copy,
        pltpu.make_async_copy(top, out_hbm.at[0:2], sent.at[1]),
        pltpu.make_async_copy(bottom, out_hbm.at[ROWS - 1 : ROWS], sent.at[2]),
    ]
    for copy in copies[1:]:
        copy.start()
    for copy in copies:
        copy.wait()


def outer(*arrays):
    return pl.pallas_call(
        outer_kernel,
        in_specs=[VMEM] * len(arrays),
        out_specs=ANY,
        out_shape=jax.ShapeDtypeStruct((ROWS, HALF, D), jnp.bfloat16),
        scratch_shapes=[
            pltpu.VMEM((8, SPAN, D), jnp.float32),
            pltpu.VMEM((8, SPAN + 8, D), jnp.float32),
            pltpu.VMEM((7, SPAN, D), jnp.float32),
            pltpu.VMEM((2, HALF, D), jnp.bfloat16),
            pltpu.VMEM((1, HALF, D), jnp.bfloat16),
            pltpu.SemaphoreType.DMA((3,)),
        ],
        compiler_params=pltpu.CompilerParams(vmem_limit_bytes=16 << 20),
    )(*arrays)


def on_device(
    obs_values,
    obs_offset,
    obs_cell,
    obs_slot,
    obs_count,
    embed_weight,
    embed_bias,
    stride_weight,
    stride_bias,
    depth_weight,
    norm_gain,
):
    lon_count, lat_count = lax.axis_size("lon"), lax.axis_size("lat")
    lat = lax.axis_index("lat")
    packed = pack(obs_values, obs_offset, obs_cell, obs_slot, obs_count)
    arrived = lax.all_to_all(packed, ("lon", "lat"), split_axis=0, concat_axis=0, tiled=True)
    held = jax.ShapeDtypeStruct((TLAT, HALF, D), jnp.float32)
    edges = [jax.ShapeDtypeStruct((TLAT, n, D), jnp.bfloat16) for n in (3, 2)]
    sides, last, first = scatter(
        sides_kernel, arrived, embed_weight, embed_bias, outs=[held] + edges
    )
    ring = [(i, (i + 1) % lon_count) for i in range(lon_count)]
    west = lax.ppermute(last, "lon", ring)
    east = lax.ppermute(first, "lon", [(j, i) for i, j in ring])
    cells = jax.ShapeDtypeStruct((TLAT, TLON, D), jnp.bfloat16)
    (tile,) = scatter(middle_kernel, arrived, embed_weight, embed_bias, sides, outs=[cells])
    weight, bias = stride_weight.reshape(9 * D, D), stride_bias.reshape(1, D)
    framed = jnp.concatenate([tile, west, east], axis=1)
    top, bottom = framed[:3], framed[TLAT - 3 :]
    lower = lat % 2 == 1
    pairs = [(i, i + 1) for i in range(0, lat_count - 1, 2)]
    others = [(i, (i + 1) % lat_count) for i in range(1, lat_count, 2)]
    other = lax.ppermute(
        jnp.where(lower, bottom, top), "lat", others + [(j, i) for i, j in others]
    )
    paired = lax.ppermute(
        jnp.where(lower, top, bottom), "lat", pairs + [(j, i) for i, j in pairs]
    )
    gain = norm_gain.reshape(1, D)
    place = jnp.stack([lower, lat > 0, lat < lat_count - 1]).astype(jnp.float32)
    place = jnp.broadcast_to(place[:, None], (3, D))
    inside = inner(tile, west, east, weight, bias, depth_weight, gain)
    return outer(
        place, *inside, tile, west, east, paired, other, weight, bias, depth_weight, gain
    )


def solution(mesh):
    placed = (
        P(("lon", "lat"), None, None),
        P(("lon", "lat"), None, None),
        P(("lon", "lat"), None),
        P(("lon", "lat"), None),
        P(("lon", "lat"), None),
        P(),
        P(),
        P(),
        P(),
        P(),
        P(),
    )
    return jax.shard_map(
        on_device, mesh=mesh, in_specs=placed, out_specs=P("lat", "lon", None), check_vma=False
    )
```

```python
import functools

import jax
import jax.numpy as jnp
from jax import lax
from jax.experimental import pallas as pl
from jax.experimental.pallas import tpu as pltpu
from jax.sharding import PartitionSpec as P

D = 256
OBS_VARS = 31
WIDTH = OBS_VARS + 1
SLOTS = 12
BINS = SLOTS * WIDTH
TLAT = 16
TLON = 32
HALF = TLON // 2
ROWS = TLAT // 2
LANES = 128
GROUP = 16
TILE = 4
CHUNK = 32
SPAN = 24
FRAME = TLON + 5

ANY = pl.BlockSpec(memory_space=pl.ANY)
VMEM = pl.BlockSpec(memory_space=pltpu.VMEM)


def pack_kernel(
    count_hbm,
    values_hbm,
    offset_hbm,
    cell_hbm,
    slot_hbm,
    out,
    count,
    values,
    offset,
    cell,
    slot,
    rows,
    here,
):
    tiles, capacity = cell.shape
    halves = capacity // LANES
    used = out.shape[1] * TILE
    stride = rows.shape[0] // tiles
    groups = tiles // GROUP

    def at(j):
        return pl.ds(j * GROUP, GROUP)

    pairs = ((count_hbm, count), (offset_hbm, offset), (cell_hbm, cell), (slot_hbm, slot))
    small = [
        pltpu.make_async_copy(a, b, here.at[groups + i]) for i, (a, b) in enumerate(pairs)
    ]
    large = [
        pltpu.make_async_copy(values_hbm.at[:, at(j)], values.at[:, at(j)], here.at[j])
        for j in range(groups)
    ]
    for copy in small + large:
        copy.start()
    for copy in small:
        copy.wait()
    square = (tiles, tiles)
    diagonal = lax.broadcasted_iota(jnp.int32, square, 0) == lax.broadcasted_iota(
        jnp.int32, square, 1
    )
    counts = jnp.sum(jnp.where(diagonal, count[...], 0), axis=1, keepdims=True)
    position = lax.broadcasted_iota(jnp.int32, (tiles, capacity), 1)
    dy, dx = offset[:, 0, :], offset[:, 1, :]
    weight = jnp.where(position < counts, jnp.exp(-2.0 * (dy * dy + dx * dx)), 0.0)
    column = cell[...] % TLON
    pair = column // 2
    middle = (pair >= ROWS // 2) & (pair < 3 * ROWS // 2)
    within = pair - jnp.where(pair < ROWS // 2, 0, jnp.where(middle, ROWS // 2, ROWS))
    codes = (
        (slot[...] * TLAT + cell[...] // TLON).astype(jnp.float32),
        (jnp.where(middle, HALF, 0) + (column % 2) * ROWS + within).astype(jnp.float32),
    )
    base = halves * WIDTH
    for j in range(groups):
        own = slice(j * GROUP, (j + 1) * GROUP)

        def put(row, value, h, first=j * GROUP * stride):
            rows[pl.ds(first + row, GROUP, stride=stride), :] = value[
                :, h * LANES : (h + 1) * LANES
            ]

        for h in range(halves):
            put(h * WIDTH + OBS_VARS, weight[own], h)
            for i, code in enumerate(codes):
                put(base + i * halves + h, code[own], h)
        large[j].wait()
        for k in range(OBS_VARS):
            scaled = values[k, own, :].astype(jnp.float32) * weight[own]
            for h in range(halves):
                put(h * WIDTH + k, scaled, h)
        for d in range(j * GROUP, (j + 1) * GROUP):
            for i in range(used // TILE):
                first = d * stride + i * TILE
                out[d, i] = rows[first : first + TILE, :].astype(jnp.bfloat16)


def pack(obs_values, obs_offset, obs_cell, obs_slot, obs_count):
    tiles, _, capacity = obs_values.shape
    used = capacity // LANES * (WIDTH + 2)
    stride = -(-used // 8) * 8
    values = jnp.transpose(obs_values, (1, 0, 2))
    shape = (tiles, used // TILE, TILE, LANES)
    arrays = (obs_count, values, obs_offset, obs_cell, obs_slot)
    return pl.pallas_call(
        pack_kernel,
        in_specs=[ANY] * len(arrays),
        out_specs=VMEM,
        out_shape=pltpu.VMEM(shape, jnp.bfloat16),
        scratch_shapes=[pltpu.VMEM(a.shape, a.dtype) for a in arrays]
        + [
            pltpu.VMEM((tiles * stride, LANES), jnp.float32),
            pltpu.SemaphoreType.DMA((tiles // GROUP + 4,)),
        ],
        compiler_params=pltpu.CompilerParams(vmem_limit_bytes=24 << 20),
    )(*(pltpu.with_memory_space_constraint(a, pltpu.HBM) for a in arrays))


def embedded_cells(x_ref, weight_ref, bias_ref, total, middle):
    tiles, blocks, _, _ = x_ref.shape
    halves = blocks * TILE // WIDTH
    step = WIDTH // TILE
    iota = lax.broadcasted_iota(jnp.int32, (HALF, LANES), 0).astype(jnp.float32)
    none = jnp.zeros((HALF, LANES), jnp.bfloat16)
    zero = jnp.zeros((WIDTH, LANES), jnp.bfloat16)

    def operands(source):
        codes = x_ref[source, halves * step].astype(jnp.float32)
        spread, hot = [], []
        for h in range(halves):
            value = x_ref[source, h * step : (h + 1) * step].reshape(WIDTH, LANES)
            code = codes[h : h + 1]
            slot = jnp.floor(code * (1.0 / TLAT))
            row = jnp.broadcast_to(code - slot * TLAT, (HALF, LANES)).astype(jnp.bfloat16)
            column = codes[halves + h : halves + h + 1]
            group = jnp.where(column >= HALF, 1.0, 0.0)
            slot = jnp.where(group == middle, slot, SLOTS)
            slot = jnp.broadcast_to(slot, (WIDTH, LANES)).astype(jnp.bfloat16)
            column = jnp.where(iota == column - group * HALF, 1.0, 0.0).astype(jnp.bfloat16)
            by_slot = [jnp.where(slot == jnp.bfloat16(s), value, zero) for s in range(SLOTS)]
            by_row = [jnp.where(row == jnp.bfloat16(r), column, none) for r in range(TLAT)]
            spread.append(jnp.concatenate(by_slot, axis=0))
            hot.append(jnp.concatenate(by_row, axis=0))
        return jnp.concatenate(spread, axis=1), jnp.concatenate(hot, axis=1)

    def summed(first, count):
        spread, hot = zip(*(operands(first + g) for g in range(count)))
        return lax.dot_general(
            jnp.concatenate(spread, axis=1),
            jnp.concatenate(hot, axis=1),
            (((1,), (1,)), ((), ())),
            preferred_element_type=jnp.float32,
        )

    count = min(tiles, CHUNK)
    total[...] = summed(0, count)

    @pl.loop(1, tiles // count)
    def _(step):
        total[...] += summed(step * count, count)

    groups = []
    for s in range(SLOTS):
        block = total[s * WIDTH : (s + 1) * WIDTH, :]
        inverse = 1.0 / (1.0 + block[OBS_VARS:WIDTH, :])
        channel = lax.broadcasted_iota(jnp.int32, block.shape, 0)
        ratio = jnp.where(channel == OBS_VARS, block, block * inverse)
        groups.append(ratio.astype(jnp.bfloat16))
    projected = lax.dot_general(
        jnp.concatenate(groups, axis=0),
        weight_ref[...],
        (((0,), (0,)), ((), ())),
        preferred_element_type=jnp.float32,
    )
    return jax.nn.gelu(projected + bias_ref[...]).reshape(TLAT, HALF, D)


def sides_kernel(x_ref, weight_ref, bias_ref, sides_ref, last_ref, first_ref, total):
    sides = embedded_cells(x_ref, weight_ref, bias_ref, total, 0.0)
    sides_ref[...] = sides
    last = [sides[:, c : c + 1] for c in (HALF - 2, ROWS - 1, HALF - 1)]
    first = [sides[:, c : c + 1] for c in (0, ROWS)]
    last_ref[...] = jnp.concatenate(last, axis=1).astype(jnp.bfloat16)
    first_ref[...] = jnp.concatenate(first, axis=1).astype(jnp.bfloat16)


def middle_kernel(x_ref, weight_ref, bias_ref, sides_ref, tile_ref, total):
    middle = embedded_cells(x_ref, weight_ref, bias_ref, total, 1.0)
    sides = sides_ref[...]
    quarter = ROWS // 2
    whole = []
    for parity in range(2):
        at = parity * ROWS
        whole += [
            sides[:, at : at + quarter],
            middle[:, at : at + ROWS],
            sides[:, at + quarter : at + ROWS],
        ]
    tile_ref[...] = jnp.concatenate(whole, axis=1).astype(jnp.bfloat16)


def scatter(kernel, arrived, embed_weight, embed_bias, *more, outs):
    tiles = arrived.shape[0]
    return pl.pallas_call(
        kernel,
        in_specs=[VMEM] * (3 + len(more)),
        out_specs=[VMEM] * len(outs),
        out_shape=outs,
        scratch_shapes=[pltpu.VMEM((BINS, TLAT * HALF), jnp.float32)],
        compiler_params=pltpu.CompilerParams(vmem_limit_bytes=32 << 20),
        cost_estimate=pl.CostEstimate(
            flops=2 * tiles * 256 * BINS * TLAT * HALF, bytes_accessed=4 << 20, transcendentals=0
        ),
    )(arrived, embed_weight, embed_bias.reshape(1, D), *more)


def put_rows(even, odd, rows, tile, west, east):
    even[rows, 0:1] = west[:, 1:2]
    even[rows, 1 : HALF + 1] = tile[:, :HALF]
    even[rows, HALF + 1 : HALF + 2] = east[:, 0:1]
    odd[rows, 0:1] = west[:, 0:1]
    odd[rows, 1:2] = west[:, 2:3]
    odd[rows, 2 : HALF + 2] = tile[:, HALF:]
    odd[rows, HALF + 2 : HALF + 3] = east[:, 1:2]


def strided_rows(even, odd, starts, weight_ref, bias_ref):
    pieces = []
    for a in range(3):
        for source, at in ((odd, 0), (even, 0), (odd, 1)):
            rows = [source[start + a, at : at + SPAN, :] for start in starts]
            pieces.append(jnp.concatenate(rows, axis=0).astype(jnp.bfloat16))
    strided = jnp.dot(
        jnp.concatenate(pieces, axis=1), weight_ref[...], preferred_element_type=jnp.float32
    )
    coarse = jax.nn.gelu(strided + bias_ref[...]).astype(jnp.bfloat16)
    return coarse.astype(jnp.float32).reshape(len(starts), SPAN, D)


def finished(coarse, first, count, depth_ref, gain_ref):
    mixed = coarse[first + 1 : first + count + 1, 1 : HALF + 1]
    for a in range(3):
        for c in range(3):
            tap = depth_ref[3 * a + c : 3 * a + c + 1, :]
            mixed = mixed + coarse[first + a : first + a + count, c : c + HALF] * tap
    centre = mixed - jnp.mean(mixed, axis=-1, keepdims=True)
    variance = jnp.mean(centre * centre, axis=-1, keepdims=True)
    return (centre * lax.rsqrt(variance + 1e-05) * gain_ref[...]).astype(jnp.bfloat16)


def inner_kernel(
    tile_ref,
    west_ref,
    east_ref,
    weight_ref,
    bias_ref,
    depth_ref,
    gain_ref,
    _,
    upper_ref,
    lower_ref,
    out_ref,
    even,
    odd,
    coarse,
):
    tile, west, east = (r[...].astype(jnp.float32) for r in (tile_ref, west_ref, east_ref))
    put_rows(even, odd, slice(0, TLAT), tile, west, east)
    coarse[...] = strided_rows(even, odd, range(1, TLAT - 2, 2), weight_ref, bias_ref)
    upper_ref[...] = coarse[0:2]
    lower_ref[...] = coarse[ROWS - 3 : ROWS - 1]
    out_ref[...] = finished(coarse, 0, ROWS - 3, depth_ref, gain_ref)


def inner(*arrays):
    pair = jax.ShapeDtypeStruct((2, SPAN, D), jnp.float32)
    return pl.pallas_call(
        inner_kernel,
        in_specs=[VMEM] * len(arrays),
        out_specs=[VMEM] * 3,
        out_shape=[pair, pair, jax.ShapeDtypeStruct((ROWS - 3, HALF, D), jnp.bfloat16)],
        scratch_shapes=[
            pltpu.VMEM((TLAT, SPAN, D), jnp.float32),
            pltpu.VMEM((TLAT, SPAN + 8, D), jnp.float32),
            pltpu.VMEM((ROWS - 1, SPAN, D), jnp.float32),
        ],
        compiler_params=pltpu.CompilerParams(vmem_limit_bytes=16 << 20),
        cost_estimate=pl.CostEstimate(
            flops=2 * 7 * SPAN * 9 * D * D, bytes_accessed=2 << 20, transcendentals=0
        ),
    )(*arrays)


def outer_kernel(
    place_ref,
    upper_ref,
    lower_ref,
    done_ref,
    tile_ref,
    west_ref,
    east_ref,
    pair_ref,
    other_ref,
    weight_ref,
    bias_ref,
    depth_ref,
    gain_ref,
    out_hbm,
    even,
    odd,
    coarse,
    top,
    bottom,
    sent,
):
    inner_copy = pltpu.make_async_copy(done_ref, out_hbm.at[2 : ROWS - 1], sent.at[0])
    inner_copy.start()
    paired, other = (r[...].astype(jnp.float32) for r in (pair_ref, other_ref))
    lower, above, below = (place_ref[i : i + 1] for i in range(3))
    upper = 1.0 - lower
    north = paired * (lower * above) + other * (upper * above)
    south = paired * upper + other * lower
    for at, source, rows in ((0, north, slice(0, 3)), (6, south, slice(0, 2))):
        part = source[rows]
        put_rows(
            even,
            odd,
            slice(at, at + rows.stop),
            part[:, :TLON],
            part[:, TLON : TLON + 3],
            part[:, TLON + 3 :],
        )
    for at, rows in ((3, slice(0, 2)), (5, slice(TLAT - 1, TLAT))):
        put_rows(
            even,
            odd,
            slice(at, at + rows.stop - rows.start),
            tile_ref[rows].astype(jnp.float32),
            west_ref[rows].astype(jnp.float32),
            east_ref[rows].astype(jnp.float32),
        )
    edge = strided_rows(even, odd, (0, 2, 5), weight_ref, bias_ref)
    coarse[0] = edge[0] * above
    coarse[1] = edge[1]
    coarse[2:4] = upper_ref[...]
    coarse[4:6] = lower_ref[...]
    coarse[6] = edge[2] * below
    top[...] = finished(coarse, 0, 2, depth_ref, gain_ref)
    bottom[...] = finished(coarse, 4, 1, depth_ref, gain_ref)
    copies = [
        inner_copy,
        pltpu.make_async_copy(top, out_hbm.at[0:2], sent.at[1]),
        pltpu.make_async_copy(bottom, out_hbm.at[ROWS - 1 : ROWS], sent.at[2]),
    ]
    for copy in copies[1:]:
        copy.start()
    for copy in copies:
        copy.wait()


def outer(*arrays):
    return pl.pallas_call(
        outer_kernel,
        in_specs=[VMEM] * len(arrays),
        out_specs=ANY,
        out_shape=jax.ShapeDtypeStruct((ROWS, HALF, D), jnp.bfloat16),
        scratch_shapes=[
            pltpu.VMEM((8, SPAN, D), jnp.float32),
            pltpu.VMEM((8, SPAN + 8, D), jnp.float32),
            pltpu.VMEM((7, SPAN, D), jnp.float32),
            pltpu.VMEM((2, HALF, D), jnp.bfloat16),
            pltpu.VMEM((1, HALF, D), jnp.bfloat16),
            pltpu.SemaphoreType.DMA((3,)),
        ],
        compiler_params=pltpu.CompilerParams(vmem_limit_bytes=16 << 20),
    )(*arrays)


def on_device(
    obs_values,
    obs_offset,
    obs_cell,
    obs_slot,
    obs_count,
    embed_weight,
    embed_bias,
    stride_weight,
    stride_bias,
    depth_weight,
    norm_gain,
):
    lon_count, lat_count = lax.axis_size("lon"), lax.axis_size("lat")
    lat = lax.axis_index("lat")
    packed = pack(obs_values, obs_offset, obs_cell, obs_slot, obs_count)
    lower, above, below = lat % 2 == 1, lat > 0, lat < lat_count - 1
    packed, lower, above, below = lax.optimization_barrier((packed, lower, above, below))
    arrived = lax.all_to_all(packed, ("lon", "lat"), split_axis=0, concat_axis=0, tiled=True)
    held = jax.ShapeDtypeStruct((TLAT, HALF, D), jnp.float32)
    edges = [jax.ShapeDtypeStruct((TLAT, n, D), jnp.bfloat16) for n in (3, 2)]
    sides, last, first = scatter(
        sides_kernel, arrived, embed_weight, embed_bias, outs=[held] + edges
    )
    ring = [(i, (i + 1) % lon_count) for i in range(lon_count)]
    west = lax.ppermute(last, "lon", ring)
    east = lax.ppermute(first, "lon", [(j, i) for i, j in ring])
    cells = jax.ShapeDtypeStruct((TLAT, TLON, D), jnp.bfloat16)
    (tile,) = scatter(middle_kernel, arrived, embed_weight, embed_bias, sides, outs=[cells])
    weight, bias = stride_weight.reshape(9 * D, D), stride_bias.reshape(1, D)
    framed = jnp.concatenate([tile, west, east], axis=1)
    top, bottom = framed[:3], framed[TLAT - 3 :]
    pairs = [(i, i + 1) for i in range(0, lat_count - 1, 2)]
    others = [(i, (i + 1) % lat_count) for i in range(1, lat_count, 2)]
    paired = lax.ppermute(
        jnp.where(lower, top, bottom), "lat", pairs + [(j, i) for i, j in pairs]
    )
    other = lax.ppermute(
        jnp.where(lower, bottom, top), "lat", others + [(j, i) for i, j in others]
    )
    gain = norm_gain.reshape(1, D)
    place = jnp.stack([lower, above, below]).astype(jnp.float32)
    place = jnp.broadcast_to(place[:, None], (3, D))
    inside = inner(tile, west, east, weight, bias, depth_weight, gain, place)
    return outer(
        place, *inside, tile, west, east, paired, other, weight, bias, depth_weight, gain
    )


def solution(mesh):
    placed = (
        P(("lon", "lat"), None, None),
        P(("lon", "lat"), None, None),
        P(("lon", "lat"), None),
        P(("lon", "lat"), None),
        P(("lon", "lat"), None),
        P(),
        P(),
        P(),
        P(),
        P(),
        P(),
    )
    return jax.shard_map(
        on_device, mesh=mesh, in_specs=placed, out_specs=P("lat", "lon", None), check_vma=False
    )
```

```python
import functools

import jax
import jax.numpy as jnp
from jax import lax
from jax.experimental import pallas as pl
from jax.experimental.pallas import tpu as pltpu
from jax.sharding import PartitionSpec as P

D = 256
OBS_VARS = 31
WIDTH = OBS_VARS + 1
SLOTS = 12
BINS = SLOTS * WIDTH
TLAT = 16
TLON = 32
HALF = TLON // 2
ROWS = TLAT // 2
LANES = 128
GROUP = 16
TILE = 4
CHUNK = 32
SPAN = 24
CELLS = TLAT * TLON
MID = 12
EXTRA = 4
SIDES = TLAT * 8
FRAME = TLON + 5

ANY = pl.BlockSpec(memory_space=pl.ANY)
VMEM = pl.BlockSpec(memory_space=pltpu.VMEM)


def placed_cells(cell):
    row, column = cell // TLON, cell % TLON
    pair, parity = column // 2, column % 2
    side = (pair < 1) | (pair > MID)
    edge = (row < 2) | (row >= TLAT - 3)
    corner = (row == 2) & (pair <= EXTRA)
    at_side = row * 8 + parity * 4 + jnp.where(pair < 1, 0, pair - MID)
    at_edge = SIDES + jnp.where(row < 2, row, row - TLAT + 5) * 2 * MID + parity * MID + pair - 1
    at_corner = SIDES + 10 * MID + parity * EXTRA + pair - 1
    at_row = CELLS // 2 - 2 * (MID - EXTRA) + parity * (MID - EXTRA) + pair - 1 - EXTRA
    at_inside = (row - 3) * 2 * MID + parity * MID + pair - 1
    rim = side | edge | corner
    in_rim = jnp.where(side, at_side, jnp.where(edge, at_edge, at_corner))
    return rim, jnp.where(rim, in_rim, jnp.where(row == 2, at_row, at_inside))


def pack_kernel(
    count_hbm,
    values_hbm,
    offset_hbm,
    cell_hbm,
    slot_hbm,
    out,
    count,
    values,
    offset,
    cell,
    slot,
    rows,
    here,
):
    tiles, capacity = cell.shape
    halves = capacity // LANES
    used = out.shape[1] * TILE
    stride = rows.shape[0] // tiles
    groups = tiles // GROUP

    def at(j):
        return pl.ds(j * GROUP, GROUP)

    pairs = ((count_hbm, count), (offset_hbm, offset), (cell_hbm, cell), (slot_hbm, slot))
    small = [
        pltpu.make_async_copy(a, b, here.at[groups + i]) for i, (a, b) in enumerate(pairs)
    ]
    large = [
        pltpu.make_async_copy(values_hbm.at[:, at(j)], values.at[:, at(j)], here.at[j])
        for j in range(groups)
    ]
    for copy in small + large:
        copy.start()
    for copy in small:
        copy.wait()
    square = (tiles, tiles)
    diagonal = lax.broadcasted_iota(jnp.int32, square, 0) == lax.broadcasted_iota(
        jnp.int32, square, 1
    )
    counts = jnp.sum(jnp.where(diagonal, count[...], 0), axis=1, keepdims=True)
    position = lax.broadcasted_iota(jnp.int32, (tiles, capacity), 1)
    dy, dx = offset[:, 0, :], offset[:, 1, :]
    weight = jnp.where(position < counts, jnp.exp(-2.0 * (dy * dy + dx * dx)), 0.0)
    rim, place = placed_cells(cell[...])
    codes = (
        (slot[...] + jnp.where(rim, 0, SLOTS)).astype(jnp.float32),
        place.astype(jnp.float32),
    )
    base = halves * WIDTH
    for j in range(groups):
        own = slice(j * GROUP, (j + 1) * GROUP)

        def put(row, value, h, first=j * GROUP * stride):
            rows[pl.ds(first + row, GROUP, stride=stride), :] = value[
                :, h * LANES : (h + 1) * LANES
            ]

        for h in range(halves):
            put(h * WIDTH + OBS_VARS, weight[own], h)
            for i, code in enumerate(codes):
                put(base + i * halves + h, code[own], h)
        large[j].wait()
        for k in range(OBS_VARS):
            scaled = values[k, own, :].astype(jnp.float32) * weight[own]
            for h in range(halves):
                put(h * WIDTH + k, scaled, h)
        for d in range(j * GROUP, (j + 1) * GROUP):
            for i in range(used // TILE):
                first = d * stride + i * TILE
                out[d, i] = rows[first : first + TILE, :].astype(jnp.bfloat16)


def pack(obs_values, obs_offset, obs_cell, obs_slot, obs_count):
    tiles, _, capacity = obs_values.shape
    used = capacity // LANES * (WIDTH + 2)
    stride = -(-used // 8) * 8
    values = jnp.transpose(obs_values, (1, 0, 2))
    shape = (tiles, used // TILE, TILE, LANES)
    arrays = (obs_count, values, obs_offset, obs_cell, obs_slot)
    return pl.pallas_call(
        pack_kernel,
        in_specs=[ANY] * len(arrays),
        out_specs=VMEM,
        out_shape=pltpu.VMEM(shape, jnp.bfloat16),
        scratch_shapes=[pltpu.VMEM(a.shape, a.dtype) for a in arrays]
        + [
            pltpu.VMEM((tiles * stride, LANES), jnp.float32),
            pltpu.SemaphoreType.DMA((tiles // GROUP + 4,)),
        ],
        compiler_params=pltpu.CompilerParams(vmem_limit_bytes=24 << 20),
    )(*(pltpu.with_memory_space_constraint(a, pltpu.HBM) for a in arrays))


def add_sums(x_ref, total, first_slot, begin, end, held=None):
    blocks = x_ref.shape[1]
    halves = blocks * TILE // WIDTH
    step = WIDTH // TILE
    tall = 16
    iota = lax.broadcasted_iota(jnp.int32, (tall, LANES), 0).astype(jnp.float32)
    one = jnp.ones((tall, LANES), jnp.bfloat16)
    none = jnp.zeros((tall, LANES), jnp.bfloat16)
    zero = jnp.zeros((WIDTH, LANES), jnp.bfloat16)
    cells = [(iota + r).astype(jnp.bfloat16) for r in range(0, CELLS // 2, tall)]

    def operands(source):
        codes = x_ref[source, halves * step].astype(jnp.float32)
        spread, hot = [], []
        for h in range(halves):
            value = x_ref[source, h * step : (h + 1) * step].reshape(WIDTH, LANES)
            slot = jnp.broadcast_to(codes[h : h + 1], (WIDTH, LANES)).astype(jnp.bfloat16)
            place = codes[halves + h : halves + h + 1]
            place = jnp.broadcast_to(place, (tall, LANES)).astype(jnp.bfloat16)
            slots = range(first_slot, first_slot + SLOTS)
            by_slot = [jnp.where(slot == jnp.bfloat16(s), value, zero) for s in slots]
            by_cell = [jnp.where(place == c, one, none) for c in cells]
            spread.append(jnp.concatenate(by_slot, axis=0))
            hot.append(jnp.concatenate(by_cell, axis=0))
        return jnp.concatenate(spread, axis=1), jnp.concatenate(hot, axis=1)

    def summed(first, count):
        spread, hot = zip(*(operands(first + g) for g in range(count)))
        return lax.dot_general(
            jnp.concatenate(spread, axis=1),
            jnp.concatenate(hot, axis=1),
            (((1,), (1,)), ((), ())),
            preferred_element_type=jnp.float32,
        )

    count = min(end - begin, CHUNK)
    total[...] = summed(begin, count) if held is None else held + summed(begin, count)

    @pl.loop(1, (end - begin) // count)
    def _(step):
        total[...] += summed(begin + step * count, count)


def embedded_cells(total, weight_ref, bias_ref):
    groups = []
    for s in range(SLOTS):
        block = total[s * WIDTH : (s + 1) * WIDTH, :]
        inverse = 1.0 / (1.0 + block[OBS_VARS:WIDTH, :])
        channel = lax.broadcasted_iota(jnp.int32, block.shape, 0)
        ratio = jnp.where(channel == OBS_VARS, block, block * inverse)
        groups.append(ratio.astype(jnp.bfloat16))
    projected = lax.dot_general(
        jnp.concatenate(groups, axis=0),
        weight_ref[...],
        (((0,), (0,)), ((), ())),
        preferred_element_type=jnp.float32,
    )
    return jax.nn.gelu(projected + bias_ref[...])


def rim_kernel(x_ref, weight_ref, bias_ref, rim_ref, rows_ref, last_ref, first_ref, total):
    add_sums(x_ref, total, 0, 0, x_ref.shape[0])
    rim = embedded_cells(total, weight_ref, bias_ref)
    rim_ref[...] = rim
    sides = rim[:SIDES].reshape(TLAT, 8, D)
    middle = rim[SIDES : SIDES + 10 * MID].reshape(5, 2 * MID, D)
    ends = jnp.concatenate([sides[:2], sides[TLAT - 3 :]], axis=0)
    parts = []
    for parity in range(2):
        at = 4 * parity
        parts += [
            ends[:, at : at + 1],
            middle[:, parity * MID : (parity + 1) * MID],
            ends[:, at + 1 : at + 4],
        ]
    rows_ref[...] = jnp.concatenate(parts, axis=1).astype(jnp.bfloat16)
    last = [sides[:, c : c + 1] for c in (6, 3, 7)]
    first = [sides[:, c : c + 1] for c in (0, 4)]
    last_ref[...] = jnp.concatenate(last, axis=1).astype(jnp.bfloat16)
    first_ref[...] = jnp.concatenate(first, axis=1).astype(jnp.bfloat16)


def scatter_cost(tiles):
    return pl.CostEstimate(
        flops=2 * tiles * 256 * BINS * CELLS // 2, bytes_accessed=4 << 20, transcendentals=0
    )


def rim_cells(arrived, embed_weight, embed_bias):
    outs = [
        jax.ShapeDtypeStruct((CELLS // 2, D), jnp.float32),
        jax.ShapeDtypeStruct((5, TLON, D), jnp.bfloat16),
        jax.ShapeDtypeStruct((TLAT, 3, D), jnp.bfloat16),
        jax.ShapeDtypeStruct((TLAT, 2, D), jnp.bfloat16),
    ]
    return pl.pallas_call(
        rim_kernel,
        in_specs=[VMEM] * 3,
        out_specs=[VMEM] * len(outs),
        out_shape=outs,
        scratch_shapes=[pltpu.VMEM((BINS, CELLS // 2), jnp.float32)],
        compiler_params=pltpu.CompilerParams(vmem_limit_bytes=32 << 20),
        cost_estimate=scatter_cost(arrived.shape[0]),
    )(arrived, embed_weight, embed_bias)


def put_rows(even, odd, rows, tile, west, east):
    even[rows, 0:1] = west[:, 1:2]
    even[rows, 1 : HALF + 1] = tile[:, :HALF]
    even[rows, HALF + 1 : HALF + 2] = east[:, 0:1]
    odd[rows, 0:1] = west[:, 0:1]
    odd[rows, 1:2] = west[:, 2:3]
    odd[rows, 2 : HALF + 2] = tile[:, HALF:]
    odd[rows, HALF + 2 : HALF + 3] = east[:, 1:2]


def strided_rows(even, odd, starts, weight_ref, bias_ref):
    pieces = []
    for a in range(3):
        for source, at in ((odd, 0), (even, 0), (odd, 1)):
            rows = [source[start + a, at : at + SPAN, :] for start in starts]
            pieces.append(jnp.concatenate(rows, axis=0).astype(jnp.bfloat16))
    strided = jnp.dot(
        jnp.concatenate(pieces, axis=1), weight_ref[...], preferred_element_type=jnp.float32
    )
    coarse = jax.nn.gelu(strided + bias_ref[...]).astype(jnp.bfloat16)
    return coarse.astype(jnp.float32).reshape(len(starts), SPAN, D)


def finished(coarse, first, count, depth_ref, gain_ref):
    mixed = coarse[first + 1 : first + count + 1, 1 : HALF + 1]
    for a in range(3):
        for c in range(3):
            tap = depth_ref[3 * a + c : 3 * a + c + 1, :]
            mixed = mixed + coarse[first + a : first + a + count, c : c + HALF] * tap
    centre = mixed - jnp.mean(mixed, axis=-1, keepdims=True)
    variance = jnp.mean(centre * centre, axis=-1, keepdims=True)
    return (centre * lax.rsqrt(variance + 1e-05) * gain_ref[...]).astype(jnp.bfloat16)


def half_kernel(x_ref, half_ref):
    add_sums(x_ref, half_ref, SLOTS, 0, x_ref.shape[0] // 2)


def half_sums(arrived):
    return pl.pallas_call(
        half_kernel,
        in_specs=[VMEM],
        out_specs=VMEM,
        out_shape=jax.ShapeDtypeStruct((BINS, CELLS // 2), jnp.float32),
        compiler_params=pltpu.CompilerParams(vmem_limit_bytes=32 << 20),
        cost_estimate=scatter_cost(arrived.shape[0]),
    )(arrived)


def inner_kernel(
    x_ref,
    half_ref,
    embed_ref,
    embed_bias_ref,
    rim_ref,
    west_ref,
    east_ref,
    weight_ref,
    bias_ref,
    depth_ref,
    gain_ref,
    _,
    upper_ref,
    lower_ref,
    out_ref,
    total,
    even,
    odd,
    coarse,
):
    tiles = x_ref.shape[0]
    add_sums(x_ref, total, SLOTS, tiles // 2, tiles, half_ref[...])
    inside = embedded_cells(total, embed_ref, embed_bias_ref)
    west, east = (r[...].astype(jnp.float32) for r in (west_ref, east_ref))
    sides = rim_ref[:SIDES].reshape(TLAT, 8, D)
    edges = rim_ref[SIDES : SIDES + 10 * MID].reshape(5, 2 * MID, D)
    corner = rim_ref[SIDES + 10 * MID :].reshape(1, 2 * EXTRA, D)
    bulk = inside[: 20 * MID].reshape(TLAT - 6, 2 * MID, D)
    rest = inside[20 * MID :].reshape(1, 2 * (MID - EXTRA), D)
    even[:, 0:1] = west[:, 1:2]
    odd[:, 0:1] = west[:, 0:1]
    odd[:, 1:2] = west[:, 2:3]
    for parity, held in ((0, even), (1, odd)):
        at = 1 + parity
        mid = slice(at + 1, at + 1 + MID)
        cut = at + 1 + EXTRA
        own = slice(parity * MID, (parity + 1) * MID)
        held[:, at : at + 1] = sides[:, 4 * parity : 4 * parity + 1]
        held[:, at + 1 + MID : at + HALF] = sides[:, 4 * parity + 1 : 4 * parity + 4]
        held[:, at + HALF : at + HALF + 1] = east[:, parity : parity + 1]
        held[0:2, mid] = edges[0:2, own]
        held[TLAT - 3 :, mid] = edges[2:5, own]
        held[3 : TLAT - 3, mid] = bulk[:, own]
        held[2:3, at + 1 : cut] = corner[:, EXTRA * parity : EXTRA * (parity + 1)]
        span = MID - EXTRA
        held[2:3, cut : cut + span] = rest[:, span * parity : span * (parity + 1)]
    coarse[...] = strided_rows(even, odd, range(1, TLAT - 2, 2), weight_ref, bias_ref)
    upper_ref[...] = coarse[0:2]
    lower_ref[...] = coarse[ROWS - 3 : ROWS - 1]
    out_ref[...] = finished(coarse, 0, ROWS - 3, depth_ref, gain_ref)


def inner(arrived, *arrays):
    pair = jax.ShapeDtypeStruct((2, SPAN, D), jnp.float32)
    return pl.pallas_call(
        inner_kernel,
        in_specs=[VMEM] * (1 + len(arrays)),
        out_specs=[VMEM] * 3,
        out_shape=[pair, pair, jax.ShapeDtypeStruct((ROWS - 3, HALF, D), jnp.bfloat16)],
        scratch_shapes=[
            pltpu.VMEM((BINS, CELLS // 2), jnp.float32),
            pltpu.VMEM((TLAT, SPAN, D), jnp.float32),
            pltpu.VMEM((TLAT, SPAN + 8, D), jnp.float32),
            pltpu.VMEM((ROWS - 1, SPAN, D), jnp.float32),
        ],
        compiler_params=pltpu.CompilerParams(vmem_limit_bytes=32 << 20),
        cost_estimate=scatter_cost(arrived.shape[0]),
    )(arrived, *arrays)


def outer_kernel(
    place_ref,
    upper_ref,
    lower_ref,
    done_ref,
    rows_ref,
    west_ref,
    east_ref,
    pair_ref,
    other_ref,
    weight_ref,
    bias_ref,
    depth_ref,
    gain_ref,
    out_hbm,
    even,
    odd,
    coarse,
    top,
    bottom,
    sent,
):
    inner_copy = pltpu.make_async_copy(done_ref, out_hbm.at[2 : ROWS - 1], sent.at[0])
    inner_copy.start()
    paired, other = (r[...].astype(jnp.float32) for r in (pair_ref, other_ref))
    lower, above, below = (place_ref[i : i + 1] for i in range(3))
    upper = 1.0 - lower
    north = paired * (lower * above) + other * (upper * above)
    south = paired * upper + other * lower
    for at, source, rows in ((0, north, slice(0, 3)), (6, south, slice(0, 2))):
        part = source[rows]
        put_rows(
            even,
            odd,
            slice(at, at + rows.stop),
            part[:, :TLON],
            part[:, TLON : TLON + 3],
            part[:, TLON + 3 :],
        )
    for at, rows, own in ((3, slice(0, 2), slice(0, 2)), (5, slice(TLAT - 1, TLAT), slice(4, 5))):
        put_rows(
            even,
            odd,
            slice(at, at + rows.stop - rows.start),
            rows_ref[own].astype(jnp.float32),
            west_ref[rows].astype(jnp.float32),
            east_ref[rows].astype(jnp.float32),
        )
    edge = strided_rows(even, odd, (0, 2, 5), weight_ref, bias_ref)
    coarse[0] = edge[0] * above
    coarse[1] = edge[1]
    coarse[2:4] = upper_ref[...]
    coarse[4:6] = lower_ref[...]
    coarse[6] = edge[2] * below
    top[...] = finished(coarse, 0, 2, depth_ref, gain_ref)
    bottom[...] = finished(coarse, 4, 1, depth_ref, gain_ref)
    copies = [
        inner_copy,
        pltpu.make_async_copy(top, out_hbm.at[0:2], sent.at[1]),
        pltpu.make_async_copy(bottom, out_hbm.at[ROWS - 1 : ROWS], sent.at[2]),
    ]
    for copy in copies[1:]:
        copy.start()
    for copy in copies:
        copy.wait()


def outer(*arrays):
    return pl.pallas_call(
        outer_kernel,
        in_specs=[VMEM] * len(arrays),
        out_specs=ANY,
        out_shape=jax.ShapeDtypeStruct((ROWS, HALF, D), jnp.bfloat16),
        scratch_shapes=[
            pltpu.VMEM((8, SPAN, D), jnp.float32),
            pltpu.VMEM((8, SPAN + 8, D), jnp.float32),
            pltpu.VMEM((7, SPAN, D), jnp.float32),
            pltpu.VMEM((2, HALF, D), jnp.bfloat16),
            pltpu.VMEM((1, HALF, D), jnp.bfloat16),
            pltpu.SemaphoreType.DMA((3,)),
        ],
        compiler_params=pltpu.CompilerParams(vmem_limit_bytes=16 << 20),
    )(*arrays)


def on_device(
    obs_values,
    obs_offset,
    obs_cell,
    obs_slot,
    obs_count,
    embed_weight,
    embed_bias,
    stride_weight,
    stride_bias,
    depth_weight,
    norm_gain,
):
    lon_count, lat_count = lax.axis_size("lon"), lax.axis_size("lat")
    lat = lax.axis_index("lat")
    packed = pack(obs_values, obs_offset, obs_cell, obs_slot, obs_count)
    lower, above, below = lat % 2 == 1, lat > 0, lat < lat_count - 1
    packed, lower, above, below = lax.optimization_barrier((packed, lower, above, below))
    arrived = lax.all_to_all(packed, ("lon", "lat"), split_axis=0, concat_axis=0, tiled=True)
    embed = embed_bias.reshape(1, D)
    rim, rows, last, first = rim_cells(arrived, embed_weight, embed)
    rows, lower, above, below = lax.optimization_barrier((rows, lower, above, below))
    ring = [(i, (i + 1) % lon_count) for i in range(lon_count)]
    west = lax.ppermute(last, "lon", ring)
    east = lax.ppermute(first, "lon", [(j, i) for i, j in ring])
    half = half_sums(arrived)
    weight, bias = stride_weight.reshape(9 * D, D), stride_bias.reshape(1, D)
    top = jnp.concatenate([rows[:3], west[:3], east[:3]], axis=1)
    bottom = jnp.concatenate([rows[2:], west[TLAT - 3 :], east[TLAT - 3 :]], axis=1)
    pairs = [(i, i + 1) for i in range(0, lat_count - 1, 2)]
    others = [(i, (i + 1) % lat_count) for i in range(1, lat_count, 2)]
    paired = lax.ppermute(
        jnp.where(lower, top, bottom), "lat", pairs + [(j, i) for i, j in pairs]
    )
    other = lax.ppermute(
        jnp.where(lower, bottom, top), "lat", others + [(j, i) for i, j in others]
    )
    gain = norm_gain.reshape(1, D)
    index = lax.broadcasted_iota(jnp.int32, (3, D), 0)
    flags = jnp.where(index == 0, lower, jnp.where(index == 1, above, below))
    place = flags.astype(jnp.float32)
    inside = inner(
        arrived, half, embed_weight, embed, rim, west, east, weight, bias, depth_weight, gain, place
    )
    return outer(
        place, *inside, rows, west, east, paired, other, weight, bias, depth_weight, gain
    )


def solution(mesh):
    placed = (
        P(("lon", "lat"), None, None),
        P(("lon", "lat"), None, None),
        P(("lon", "lat"), None),
        P(("lon", "lat"), None),
        P(("lon", "lat"), None),
        P(),
        P(),
        P(),
        P(),
        P(),
        P(),
    )
    return jax.shard_map(
        on_device, mesh=mesh, in_specs=placed, out_specs=P("lat", "lon", None), check_vma=False
    )
```

```python
import functools

import jax
import jax.numpy as jnp
from jax import lax
from jax.experimental import pallas as pl
from jax.experimental.pallas import tpu as pltpu
from jax.sharding import PartitionSpec as P

D = 256
OBS_VARS = 31
WIDTH = OBS_VARS + 1
SLOTS = 12
BINS = SLOTS * WIDTH
TLAT = 16
TLON = 32
HALF = TLON // 2
ROWS = TLAT // 2
LANES = 128
GROUP = 16
TILE = 4
CHUNK = 32
EARLY = 20
SPAN = 24
CELLS = TLAT * TLON
MID = 12
EXTRA = 4
SIDES = TLAT * 8
FRAME = TLON + 5

ANY = pl.BlockSpec(memory_space=pl.ANY)
VMEM = pl.BlockSpec(memory_space=pltpu.VMEM)


def placed_cells(cell):
    row, column = cell // TLON, cell % TLON
    pair, parity = column // 2, column % 2
    side = (pair < 1) | (pair > MID)
    edge = (row < 2) | (row >= TLAT - 3)
    corner = (row == 2) & (pair <= EXTRA)
    at_side = row * 8 + parity * 4 + jnp.where(pair < 1, 0, pair - MID)
    at_edge = SIDES + jnp.where(row < 2, row, row - TLAT + 5) * 2 * MID + parity * MID + pair - 1
    at_corner = SIDES + 10 * MID + parity * EXTRA + pair - 1
    at_row = CELLS // 2 - 2 * (MID - EXTRA) + parity * (MID - EXTRA) + pair - 1 - EXTRA
    at_inside = (row - 3) * 2 * MID + parity * MID + pair - 1
    rim = side | edge | corner
    in_rim = jnp.where(side, at_side, jnp.where(edge, at_edge, at_corner))
    return rim, jnp.where(rim, in_rim, jnp.where(row == 2, at_row, at_inside))


def pack_kernel(
    count_hbm,
    values_hbm,
    offset_hbm,
    cell_hbm,
    slot_hbm,
    out,
    count,
    values,
    offset,
    cell,
    slot,
    rows,
    here,
):
    tiles, capacity = cell.shape
    halves = capacity // LANES
    used = out.shape[1] * TILE
    stride = rows.shape[0] // tiles
    groups = tiles // GROUP

    def at(j):
        return pl.ds(j * GROUP, GROUP)

    pairs = ((count_hbm, count), (offset_hbm, offset), (cell_hbm, cell), (slot_hbm, slot))
    small = [
        pltpu.make_async_copy(a, b, here.at[groups + i]) for i, (a, b) in enumerate(pairs)
    ]
    large = [
        pltpu.make_async_copy(values_hbm.at[:, at(j)], values.at[:, at(j)], here.at[j])
        for j in range(groups)
    ]
    for copy in small + large:
        copy.start()
    for copy in small:
        copy.wait()
    square = (tiles, tiles)
    diagonal = lax.broadcasted_iota(jnp.int32, square, 0) == lax.broadcasted_iota(
        jnp.int32, square, 1
    )
    counts = jnp.sum(jnp.where(diagonal, count[...], 0), axis=1, keepdims=True)
    position = lax.broadcasted_iota(jnp.int32, (tiles, capacity), 1)
    dy, dx = offset[:, 0, :], offset[:, 1, :]
    weight = jnp.where(position < counts, jnp.exp(-2.0 * (dy * dy + dx * dx)), 0.0)
    rim, place = placed_cells(cell[...])
    codes = (
        (slot[...] + jnp.where(rim, 0, SLOTS)).astype(jnp.float32),
        place.astype(jnp.float32),
    )
    base = halves * WIDTH
    for j in range(groups):
        own = slice(j * GROUP, (j + 1) * GROUP)

        def put(row, value, h, first=j * GROUP * stride):
            rows[pl.ds(first + row, GROUP, stride=stride), :] = value[
                :, h * LANES : (h + 1) * LANES
            ]

        for h in range(halves):
            put(h * WIDTH + OBS_VARS, weight[own], h)
            for i, code in enumerate(codes):
                put(base + i * halves + h, code[own], h)
        large[j].wait()
        for k in range(OBS_VARS):
            scaled = values[k, own, :].astype(jnp.float32) * weight[own]
            for h in range(halves):
                put(h * WIDTH + k, scaled, h)
        for d in range(j * GROUP, (j + 1) * GROUP):
            block = rows[d * stride : (d + 1) * stride, :].astype(jnp.bfloat16)
            out[d] = block.reshape(stride // TILE, TILE, LANES)[: used // TILE]


def pack(obs_values, obs_offset, obs_cell, obs_slot, obs_count):
    tiles, _, capacity = obs_values.shape
    used = capacity // LANES * (WIDTH + 2)
    stride = -(-used // 8) * 8
    values = jnp.transpose(obs_values, (1, 0, 2))
    shape = (tiles, used // TILE, TILE, LANES)
    arrays = (obs_count, values, obs_offset, obs_cell, obs_slot)
    return pl.pallas_call(
        pack_kernel,
        in_specs=[ANY] * len(arrays),
        out_specs=VMEM,
        out_shape=pltpu.VMEM(shape, jnp.bfloat16),
        scratch_shapes=[pltpu.VMEM(a.shape, a.dtype) for a in arrays]
        + [
            pltpu.VMEM((tiles * stride, LANES), jnp.float32),
            pltpu.SemaphoreType.DMA((tiles // GROUP + 4,)),
        ],
        compiler_params=pltpu.CompilerParams(vmem_limit_bytes=24 << 20),
    )(*(pltpu.with_memory_space_constraint(a, pltpu.HBM) for a in arrays))


def add_sums(x_ref, total, first_slot, begin, end, held=None):
    blocks = x_ref.shape[1]
    halves = blocks * TILE // WIDTH
    step = WIDTH // TILE
    tall = 16
    iota = lax.broadcasted_iota(jnp.int32, (tall, LANES), 0).astype(jnp.float32)
    one = jnp.ones((tall, LANES), jnp.bfloat16)
    none = jnp.zeros((tall, LANES), jnp.bfloat16)
    zero = jnp.zeros((WIDTH, LANES), jnp.bfloat16)
    cells = [(iota + r).astype(jnp.bfloat16) for r in range(0, CELLS // 2, tall)]

    def operands(source):
        codes = x_ref[source, halves * step].astype(jnp.float32)
        spread, hot = [], []
        for h in range(halves):
            value = x_ref[source, h * step : (h + 1) * step].reshape(WIDTH, LANES)
            slot = jnp.broadcast_to(codes[h : h + 1], (WIDTH, LANES)).astype(jnp.bfloat16)
            place = codes[halves + h : halves + h + 1]
            place = jnp.broadcast_to(place, (tall, LANES)).astype(jnp.bfloat16)
            slots = range(first_slot, first_slot + SLOTS)
            by_slot = [jnp.where(slot == jnp.bfloat16(s), value, zero) for s in slots]
            by_cell = [jnp.where(place == c, one, none) for c in cells]
            spread.append(jnp.concatenate(by_slot, axis=0))
            hot.append(jnp.concatenate(by_cell, axis=0))
        return jnp.concatenate(spread, axis=1), jnp.concatenate(hot, axis=1)

    def summed(first, count):
        spread, hot = zip(*(operands(first + g) for g in range(count)))
        return lax.dot_general(
            jnp.concatenate(spread, axis=1),
            jnp.concatenate(hot, axis=1),
            (((1,), (1,)), ((), ())),
            preferred_element_type=jnp.float32,
        )

    count = end - begin if end - begin <= CHUNK else CHUNK // 2
    total[...] = summed(begin, count) if held is None else held + summed(begin, count)

    @pl.loop(1, (end - begin) // count)
    def _(step):
        total[...] += summed(begin + step * count, count)


def embedded_cells(total, weight_ref, bias_ref):
    groups = []
    for s in range(SLOTS):
        block = total[s * WIDTH : (s + 1) * WIDTH, :]
        inverse = 1.0 / (1.0 + block[OBS_VARS:WIDTH, :])
        channel = lax.broadcasted_iota(jnp.int32, block.shape, 0)
        ratio = jnp.where(channel == OBS_VARS, block, block * inverse)
        groups.append(ratio.astype(jnp.bfloat16))
    projected = lax.dot_general(
        jnp.concatenate(groups, axis=0),
        weight_ref[...],
        (((0,), (0,)), ((), ())),
        preferred_element_type=jnp.float32,
    )
    return jax.nn.gelu(projected + bias_ref[...])


def sides_kernel(x_ref, weight_ref, bias_ref, sides_ref, sums_ref, last_ref, first_ref, total):
    add_sums(x_ref, total, 0, 0, x_ref.shape[0])
    sums_ref[...] = total[:, SIDES:]
    embedded = embedded_cells(total.at[:, :SIDES], weight_ref, bias_ref)
    sides_ref[...] = embedded
    sides = embedded.reshape(TLAT, 8, D)
    last = [sides[:, c : c + 1] for c in (6, 3, 7)]
    first = [sides[:, c : c + 1] for c in (0, 4)]
    last_ref[...] = jnp.concatenate(last, axis=1).astype(jnp.bfloat16)
    first_ref[...] = jnp.concatenate(first, axis=1).astype(jnp.bfloat16)


def edges_kernel(
    x_ref, weight_ref, bias_ref, sides_ref, sums_ref, half_ref, edges_ref, rows_ref
):
    add_sums(x_ref, half_ref, SLOTS, 0, x_ref.shape[0] * EARLY // 32)
    embedded = embedded_cells(sums_ref, weight_ref, bias_ref)
    edges_ref[...] = embedded
    middle = embedded[: 10 * MID].reshape(5, 2 * MID, D)
    sides = sides_ref[...].reshape(TLAT, 8, D)
    ends = jnp.concatenate([sides[:2], sides[TLAT - 3 :]], axis=0)
    parts = []
    for parity in range(2):
        at = 4 * parity
        parts += [
            ends[:, at : at + 1],
            middle[:, parity * MID : (parity + 1) * MID],
            ends[:, at + 1 : at + 4],
        ]
    rows_ref[...] = jnp.concatenate(parts, axis=1).astype(jnp.bfloat16)


def scatter_cost(tiles):
    return pl.CostEstimate(
        flops=2 * tiles * 256 * BINS * CELLS // 2, bytes_accessed=4 << 20, transcendentals=0
    )


def sides(arrived, embed_weight, embed_bias):
    outs = [
        jax.ShapeDtypeStruct((SIDES, D), jnp.float32),
        jax.ShapeDtypeStruct((BINS, CELLS // 2 - SIDES), jnp.float32),
        jax.ShapeDtypeStruct((TLAT, 3, D), jnp.bfloat16),
        jax.ShapeDtypeStruct((TLAT, 2, D), jnp.bfloat16),
    ]
    return pl.pallas_call(
        sides_kernel,
        in_specs=[VMEM] * 3,
        out_specs=[VMEM] * len(outs),
        out_shape=outs,
        scratch_shapes=[pltpu.VMEM((BINS, CELLS // 2), jnp.float32)],
        compiler_params=pltpu.CompilerParams(vmem_limit_bytes=32 << 20),
        cost_estimate=scatter_cost(arrived.shape[0]),
    )(arrived, embed_weight, embed_bias)


def edges(arrived, *arrays):
    outs = [
        jax.ShapeDtypeStruct((BINS, CELLS // 2), jnp.float32),
        jax.ShapeDtypeStruct((CELLS // 2 - SIDES, D), jnp.float32),
        jax.ShapeDtypeStruct((5, TLON, D), jnp.bfloat16),
    ]
    return pl.pallas_call(
        edges_kernel,
        in_specs=[VMEM] * (1 + len(arrays)),
        out_specs=[VMEM] * len(outs),
        out_shape=outs,
        compiler_params=pltpu.CompilerParams(vmem_limit_bytes=32 << 20),
        cost_estimate=scatter_cost(arrived.shape[0]),
    )(arrived, *arrays)


def put_rows(even, odd, rows, tile, west, east):
    even[rows, 0:1] = west[:, 1:2]
    even[rows, 1 : HALF + 1] = tile[:, :HALF]
    even[rows, HALF + 1 : HALF + 2] = east[:, 0:1]
    odd[rows, 0:1] = west[:, 0:1]
    odd[rows, 1:2] = west[:, 2:3]
    odd[rows, 2 : HALF + 2] = tile[:, HALF:]
    odd[rows, HALF + 2 : HALF + 3] = east[:, 1:2]


def strided_rows(even, odd, starts, weight_ref, bias_ref):
    pieces = []
    for a in range(3):
        for source, at in ((odd, 0), (even, 0), (odd, 1)):
            rows = [source(start + a, at) for start in starts]
            pieces.append(jnp.concatenate(rows, axis=0).astype(jnp.bfloat16))
    strided = jnp.dot(
        jnp.concatenate(pieces, axis=1), weight_ref[...], preferred_element_type=jnp.float32
    )
    coarse = jax.nn.gelu(strided + bias_ref[...]).astype(jnp.bfloat16)
    return coarse.astype(jnp.float32).reshape(len(starts), SPAN, D)


def spans(*refs):
    rows = [(ref, i) for ref in refs for i in range(ref.shape[0])]
    return lambda i, at: rows[i][0][rows[i][1], at : at + SPAN, :]


def finished(coarse, first, count, depth_ref, gain_ref):
    mixed = coarse[first + 1 : first + count + 1, 1 : HALF + 1]
    for a in range(3):
        for c in range(3):
            tap = depth_ref[3 * a + c : 3 * a + c + 1, :]
            mixed = mixed + coarse[first + a : first + a + count, c : c + HALF] * tap
    centre = mixed - jnp.mean(mixed, axis=-1, keepdims=True)
    variance = jnp.mean(centre * centre, axis=-1, keepdims=True)
    return (centre * lax.rsqrt(variance + 1e-05) * gain_ref[...]).astype(jnp.bfloat16)


def inner_kernel(
    x_ref,
    half_ref,
    embed_ref,
    embed_bias_ref,
    sides_ref,
    edges_ref,
    west_ref,
    east_ref,
    weight_ref,
    bias_ref,
    depth_ref,
    gain_ref,
    _,
    own_even_ref,
    own_odd_ref,
    upper_ref,
    lower_ref,
    out_ref,
    total,
    even,
    odd,
    coarse,
):
    tiles = x_ref.shape[0]
    add_sums(x_ref, total, SLOTS, tiles * EARLY // 32, tiles, half_ref[...])
    inside = embedded_cells(total, embed_ref, embed_bias_ref)
    west, east = (r[...].astype(jnp.float32) for r in (west_ref, east_ref))
    sides = sides_ref[...].reshape(TLAT, 8, D)
    edges = edges_ref[: 10 * MID].reshape(5, 2 * MID, D)
    corner = edges_ref[10 * MID :].reshape(1, 2 * EXTRA, D)
    bulk = inside[: 20 * MID].reshape(TLAT - 6, 2 * MID, D)
    rest = inside[20 * MID :].reshape(1, 2 * (MID - EXTRA), D)
    even[:, 0:1] = west[:, 1:2]
    odd[:, 0:1] = west[:, 0:1]
    odd[:, 1:2] = west[:, 2:3]
    for parity, held in ((0, even), (1, odd)):
        at = 1 + parity
        mid = slice(at + 1, at + 1 + MID)
        cut = at + 1 + EXTRA
        own = slice(parity * MID, (parity + 1) * MID)
        held[:, at : at + 1] = sides[:, 4 * parity : 4 * parity + 1]
        held[:, at + 1 + MID : at + HALF] = sides[:, 4 * parity + 1 : 4 * parity + 4]
        held[:, at + HALF : at + HALF + 1] = east[:, parity : parity + 1]
        held[0:2, mid] = edges[0:2, own]
        held[TLAT - 3 :, mid] = edges[2:5, own]
        held[3 : TLAT - 3, mid] = bulk[:, own]
        held[2:3, at + 1 : cut] = corner[:, EXTRA * parity : EXTRA * (parity + 1)]
        span = MID - EXTRA
        held[2:3, cut : cut + span] = rest[:, span * parity : span * (parity + 1)]
    starts = range(1, TLAT - 2, 2)
    coarse[...] = strided_rows(spans(even), spans(odd), starts, weight_ref, bias_ref)
    for held, own_ref in ((even, own_even_ref), (odd, own_odd_ref)):
        own_ref[0:2] = held[0:2]
        own_ref[2:3] = held[TLAT - 1 :]
    upper_ref[...] = coarse[0:2]
    lower_ref[...] = coarse[ROWS - 3 : ROWS - 1]
    out_ref[...] = finished(coarse, 0, ROWS - 3, depth_ref, gain_ref)


def inner(arrived, *arrays):
    pair = jax.ShapeDtypeStruct((2, SPAN, D), jnp.float32)
    owns = [jax.ShapeDtypeStruct((3, n, D), jnp.float32) for n in (SPAN, SPAN + 8)]
    return pl.pallas_call(
        inner_kernel,
        in_specs=[VMEM] * (1 + len(arrays)),
        out_specs=[VMEM] * 5,
        out_shape=owns + [pair, pair, jax.ShapeDtypeStruct((ROWS - 3, HALF, D), jnp.bfloat16)],
        scratch_shapes=[
            pltpu.VMEM((BINS, CELLS // 2), jnp.float32),
            pltpu.VMEM((TLAT, SPAN, D), jnp.float32),
            pltpu.VMEM((TLAT, SPAN + 8, D), jnp.float32),
            pltpu.VMEM((ROWS - 1, SPAN, D), jnp.float32),
        ],
        compiler_params=pltpu.CompilerParams(vmem_limit_bytes=32 << 20),
        cost_estimate=scatter_cost(arrived.shape[0]),
    )(arrived, *arrays)


def outer_kernel(
    place_ref,
    own_even_ref,
    own_odd_ref,
    upper_ref,
    lower_ref,
    done_ref,
    pair_ref,
    other_ref,
    weight_ref,
    bias_ref,
    depth_ref,
    gain_ref,
    out_hbm,
    north_even,
    north_odd,
    south_even,
    south_odd,
    coarse,
    top,
    bottom,
    sent,
):
    inner_copy = pltpu.make_async_copy(done_ref, out_hbm.at[2 : ROWS - 1], sent.at[0])
    inner_copy.start()
    paired, other = (r[...].astype(jnp.float32) for r in (pair_ref, other_ref))
    lower, above, below = (place_ref[i : i + 1] for i in range(3))
    upper = 1.0 - lower
    north = paired * (lower * above) + other * (upper * above)
    south = (paired * upper + other * lower)[:2]
    for even, odd, part in ((north_even, north_odd, north), (south_even, south_odd, south)):
        west, east = part[:, TLON : TLON + 3], part[:, TLON + 3 :]
        put_rows(even, odd, slice(0, part.shape[0]), part[:, :TLON], west, east)
    edge = strided_rows(
        spans(north_even, own_even_ref, south_even),
        spans(north_odd, own_odd_ref, south_odd),
        (0, 2, 5),
        weight_ref,
        bias_ref,
    )
    coarse[0] = edge[0] * above
    coarse[1] = edge[1]
    coarse[2:4] = upper_ref[...]
    coarse[4:6] = lower_ref[...]
    coarse[6] = edge[2] * below
    top[...] = finished(coarse, 0, 2, depth_ref, gain_ref)
    bottom[...] = finished(coarse, 4, 1, depth_ref, gain_ref)
    copies = [
        inner_copy,
        pltpu.make_async_copy(top, out_hbm.at[0:2], sent.at[1]),
        pltpu.make_async_copy(bottom, out_hbm.at[ROWS - 1 : ROWS], sent.at[2]),
    ]
    for copy in copies[1:]:
        copy.start()
    for copy in copies:
        copy.wait()


def outer(*arrays):
    return pl.pallas_call(
        outer_kernel,
        in_specs=[VMEM] * len(arrays),
        out_specs=ANY,
        out_shape=jax.ShapeDtypeStruct((ROWS, HALF, D), jnp.bfloat16),
        scratch_shapes=[
            pltpu.VMEM((3, SPAN, D), jnp.float32),
            pltpu.VMEM((3, SPAN + 8, D), jnp.float32),
            pltpu.VMEM((2, SPAN, D), jnp.float32),
            pltpu.VMEM((2, SPAN + 8, D), jnp.float32),
            pltpu.VMEM((7, SPAN, D), jnp.float32),
            pltpu.VMEM((2, HALF, D), jnp.bfloat16),
            pltpu.VMEM((1, HALF, D), jnp.bfloat16),
            pltpu.SemaphoreType.DMA((3,)),
        ],
        compiler_params=pltpu.CompilerParams(vmem_limit_bytes=16 << 20),
    )(*arrays)


def on_device(
    obs_values,
    obs_offset,
    obs_cell,
    obs_slot,
    obs_count,
    embed_weight,
    embed_bias,
    stride_weight,
    stride_bias,
    depth_weight,
    norm_gain,
):
    lon_count, lat_count = lax.axis_size("lon"), lax.axis_size("lat")
    lat = lax.axis_index("lat")
    packed = pack(obs_values, obs_offset, obs_cell, obs_slot, obs_count)
    lower, above, below = lat % 2 == 1, lat > 0, lat < lat_count - 1
    packed, lower, above, below = lax.optimization_barrier((packed, lower, above, below))
    arrived = lax.all_to_all(packed, ("lon", "lat"), split_axis=0, concat_axis=0, tiled=True)
    embed = embed_bias.reshape(1, D)
    side_cells, sums, last, first = sides(arrived, embed_weight, embed)
    sums, lower, above, below = lax.optimization_barrier((sums, lower, above, below))
    half, edge_cells, rows = edges(arrived, embed_weight, embed, side_cells, sums)
    ring = [(i, (i + 1) % lon_count) for i in range(lon_count)]
    west = lax.ppermute(last, "lon", ring)
    east = lax.ppermute(first, "lon", [(j, i) for i, j in ring])
    weight, bias = stride_weight.reshape(9 * D, D), stride_bias.reshape(1, D)
    top = jnp.concatenate([rows[:3], west[:3], east[:3]], axis=1)
    bottom = jnp.concatenate([rows[2:], west[TLAT - 3 :], east[TLAT - 3 :]], axis=1)
    pairs = [(i, i + 1) for i in range(0, lat_count - 1, 2)]
    others = [(i, (i + 1) % lat_count) for i in range(1, lat_count, 2)]
    paired = lax.ppermute(
        jnp.where(lower, top, bottom), "lat", pairs + [(j, i) for i, j in pairs]
    )
    other = lax.ppermute(
        jnp.where(lower, bottom, top), "lat", others + [(j, i) for i, j in others]
    )
    gain = norm_gain.reshape(1, D)
    index = lax.broadcasted_iota(jnp.int32, (3, D), 0)
    flags = jnp.where(index == 0, lower, jnp.where(index == 1, above, below))
    place = flags.astype(jnp.float32)
    inside = inner(
        arrived,
        half,
        embed_weight,
        embed,
        side_cells,
        edge_cells,
        west,
        east,
        weight,
        bias,
        depth_weight,
        gain,
        place,
    )
    return outer(place, *inside, paired, other, weight, bias, depth_weight, gain)


def solution(mesh):
    placed = (
        P(("lon", "lat"), None, None),
        P(("lon", "lat"), None, None),
        P(("lon", "lat"), None),
        P(("lon", "lat"), None),
        P(("lon", "lat"), None),
        P(),
        P(),
        P(),
        P(),
        P(),
        P(),
    )
    return jax.shard_map(
        on_device, mesh=mesh, in_specs=placed, out_specs=P("lat", "lon", None), check_vma=False
    )
```

```python
import functools

import jax
import jax.numpy as jnp
from jax import lax
from jax.experimental import pallas as pl
from jax.experimental.pallas import tpu as pltpu
from jax.sharding import PartitionSpec as P

D = 256
OBS_VARS = 31
WIDTH = OBS_VARS + 1
SLOTS = 12
BINS = SLOTS * WIDTH
TLAT = 16
TLON = 32
HALF = TLON // 2
ROWS = TLAT // 2
LANES = 128
GROUP = 16
TILE = 4
CHUNK = 32
EARLY = 18
SPAN = 24
CELLS = TLAT * TLON
MID = 12
EXTRA = 4
SIDES = TLAT * 8
FRAME = TLON + 5

ANY = pl.BlockSpec(memory_space=pl.ANY)
VMEM = pl.BlockSpec(memory_space=pltpu.VMEM)


def placed_cells(cell):
    row, column = cell // TLON, cell % TLON
    pair, parity = column // 2, column % 2
    side = (pair < 1) | (pair > MID)
    edge = (row < 2) | (row >= TLAT - 3)
    corner = (row == 2) & (pair <= EXTRA)
    at_side = row * 8 + parity * 4 + jnp.where(pair < 1, 0, pair - MID)
    at_edge = SIDES + jnp.where(row < 2, row, row - TLAT + 5) * 2 * MID + parity * MID + pair - 1
    at_corner = SIDES + 10 * MID + parity * EXTRA + pair - 1
    at_row = CELLS // 2 - 2 * (MID - EXTRA) + parity * (MID - EXTRA) + pair - 1 - EXTRA
    at_inside = (row - 3) * 2 * MID + parity * MID + pair - 1
    rim = side | edge | corner
    in_rim = jnp.where(side, at_side, jnp.where(edge, at_edge, at_corner))
    return rim, jnp.where(rim, in_rim, jnp.where(row == 2, at_row, at_inside))


def pack_kernel(
    count_hbm,
    values_hbm,
    offset_hbm,
    cell_hbm,
    slot_hbm,
    out,
    count,
    values,
    offset,
    cell,
    slot,
    rows,
    here,
):
    tiles, capacity = cell.shape
    halves = capacity // LANES
    used = out.shape[1] * TILE
    stride = rows.shape[0] // (tiles + 1)
    groups = tiles // GROUP

    def at(j):
        return pl.ds(j * GROUP, GROUP)

    pairs = ((count_hbm, count), (offset_hbm, offset), (cell_hbm, cell), (slot_hbm, slot))
    small = [
        pltpu.make_async_copy(a, b, here.at[groups + i]) for i, (a, b) in enumerate(pairs)
    ]
    large = [
        pltpu.make_async_copy(values_hbm.at[:, at(j)], values.at[:, at(j)], here.at[j])
        for j in range(groups)
    ]
    for copy in small + large:
        copy.start()
    for copy in small:
        copy.wait()
    square = (tiles, tiles)
    diagonal = lax.broadcasted_iota(jnp.int32, square, 0) == lax.broadcasted_iota(
        jnp.int32, square, 1
    )
    counts = jnp.sum(jnp.where(diagonal, count[...], 0), axis=1, keepdims=True)
    position = lax.broadcasted_iota(jnp.int32, (tiles, capacity), 1)
    dy, dx = offset[:, 0, :], offset[:, 1, :]
    weight = jnp.where(position < counts, jnp.exp(-2.0 * (dy * dy + dx * dx)), 0.0)
    rim, place = placed_cells(cell[...])
    codes = (
        (slot[...] + jnp.where(rim, 0, SLOTS)).astype(jnp.float32),
        place.astype(jnp.float32),
    )
    base = halves * WIDTH
    for j in range(groups):
        own = slice(j * GROUP, (j + 1) * GROUP)

        def put(row, value, h, first=j * GROUP * stride):
            rows[pl.ds(first + row, GROUP, stride=stride), :] = value[
                :, h * LANES : (h + 1) * LANES
            ]

        for h in range(halves):
            put(h * WIDTH + OBS_VARS, weight[own], h)
            for i, code in enumerate(codes):
                put(base + i * halves + h, code[own], h)
        large[j].wait()
        for k in range(OBS_VARS):
            scaled = values[k, own, :].astype(jnp.float32) * weight[own]
            for h in range(halves):
                put(h * WIDTH + k, scaled, h)
        for d in range(j * GROUP, (j + 1) * GROUP):
            block = rows[d * stride : (d + 1) * stride, :].astype(jnp.bfloat16)
            out[d] = block.reshape(stride // TILE, TILE, LANES)[: used // TILE]


def pack(obs_values, obs_offset, obs_cell, obs_slot, obs_count):
    tiles, _, capacity = obs_values.shape
    used = capacity // LANES * (WIDTH + 2)
    stride = -(-used // 8) * 8
    values = jnp.transpose(obs_values, (1, 0, 2))
    shape = (tiles, used // TILE, TILE, LANES)
    arrays = (obs_count, values, obs_offset, obs_cell, obs_slot)
    return pl.pallas_call(
        pack_kernel,
        in_specs=[ANY] * len(arrays),
        out_specs=VMEM,
        out_shape=pltpu.VMEM(shape, jnp.bfloat16),
        scratch_shapes=[pltpu.VMEM(a.shape, a.dtype) for a in arrays]
        + [
            pltpu.VMEM(((tiles + 1) * stride, LANES), jnp.float32),
            pltpu.SemaphoreType.DMA((tiles // GROUP + 4,)),
        ],
        compiler_params=pltpu.CompilerParams(vmem_limit_bytes=24 << 20),
    )(*(pltpu.with_memory_space_constraint(a, pltpu.HBM) for a in arrays))


def add_sums(x_ref, total, first_slot, begin, end, held=None):
    blocks = x_ref.shape[1]
    halves = blocks * TILE // WIDTH
    step = WIDTH // TILE
    tall = 16
    iota = lax.broadcasted_iota(jnp.int32, (tall, LANES), 0).astype(jnp.float32)
    one = jnp.ones((tall, LANES), jnp.bfloat16)
    none = jnp.zeros((tall, LANES), jnp.bfloat16)
    zero = jnp.zeros((WIDTH, LANES), jnp.bfloat16)
    cells = [(iota + r).astype(jnp.bfloat16) for r in range(0, CELLS // 2, tall)]

    def operands(source):
        codes = x_ref[source, halves * step].astype(jnp.float32)
        spread, hot = [], []
        for h in range(halves):
            value = x_ref[source, h * step : (h + 1) * step].reshape(WIDTH, LANES)
            slot = jnp.broadcast_to(codes[h : h + 1], (WIDTH, LANES)).astype(jnp.bfloat16)
            place = codes[halves + h : halves + h + 1]
            place = jnp.broadcast_to(place, (tall, LANES)).astype(jnp.bfloat16)
            slots = range(first_slot, first_slot + SLOTS)
            by_slot = [jnp.where(slot == jnp.bfloat16(s), value, zero) for s in slots]
            by_cell = [jnp.where(place == c, one, none) for c in cells]
            spread.append(jnp.concatenate(by_slot, axis=0))
            hot.append(jnp.concatenate(by_cell, axis=0))
        return jnp.concatenate(spread, axis=1), jnp.concatenate(hot, axis=1)

    def summed(first, count):
        spread, hot = zip(*(operands(first + g) for g in range(count)))
        return lax.dot_general(
            jnp.concatenate(spread, axis=1),
            jnp.concatenate(hot, axis=1),
            (((1,), (1,)), ((), ())),
            preferred_element_type=jnp.float32,
        )

    count = end - begin if end - begin <= CHUNK else CHUNK // 2
    total[...] = summed(begin, count) if held is None else held + summed(begin, count)

    @pl.loop(1, (end - begin) // count)
    def _(step):
        total[...] += summed(begin + step * count, count)


def embedded_cells(total, weight_ref, bias_ref):
    groups = []
    for s in range(SLOTS):
        block = total[s * WIDTH : (s + 1) * WIDTH, :]
        inverse = 1.0 / (1.0 + block[OBS_VARS:WIDTH, :])
        channel = lax.broadcasted_iota(jnp.int32, block.shape, 0)
        ratio = jnp.where(channel == OBS_VARS, block, block * inverse)
        groups.append(ratio.astype(jnp.bfloat16))
    projected = lax.dot_general(
        jnp.concatenate(groups, axis=0),
        weight_ref[...],
        (((0,), (0,)), ((), ())),
        preferred_element_type=jnp.float32,
    )
    return jax.nn.gelu(projected + bias_ref[...])


def sides_kernel(x_ref, weight_ref, bias_ref, sides_ref, sums_ref, last_ref, first_ref, total):
    add_sums(x_ref, total, 0, 0, x_ref.shape[0])
    sums_ref[...] = total[:, SIDES:]
    embedded = embedded_cells(total.at[:, :SIDES], weight_ref, bias_ref)
    sides_ref[...] = embedded
    sides = embedded.reshape(TLAT, 8, D)
    last = [sides[:, c : c + 1] for c in (6, 3, 7)]
    first = [sides[:, c : c + 1] for c in (0, 4)]
    last_ref[...] = jnp.concatenate(last, axis=1).astype(jnp.bfloat16)
    first_ref[...] = jnp.concatenate(first, axis=1).astype(jnp.bfloat16)


def edges_kernel(
    x_ref, weight_ref, bias_ref, sides_ref, sums_ref, half_ref, edges_ref, rows_ref
):
    add_sums(x_ref, half_ref, SLOTS, 0, x_ref.shape[0] * EARLY // 32)
    embedded = embedded_cells(sums_ref, weight_ref, bias_ref)
    edges_ref[...] = embedded
    middle = embedded[: 10 * MID].reshape(5, 2 * MID, D)
    sides = sides_ref[...].reshape(TLAT, 8, D)
    ends = jnp.concatenate([sides[:2], sides[TLAT - 3 :]], axis=0)
    parts = []
    for parity in range(2):
        at = 4 * parity
        parts += [
            ends[:, at : at + 1],
            middle[:, parity * MID : (parity + 1) * MID],
            ends[:, at + 1 : at + 4],
        ]
    rows_ref[...] = jnp.concatenate(parts, axis=1).astype(jnp.bfloat16)


def scatter_cost(tiles):
    return pl.CostEstimate(
        flops=2 * tiles * 256 * BINS * CELLS // 2, bytes_accessed=4 << 20, transcendentals=0
    )


def sides(arrived, embed_weight, embed_bias):
    outs = [
        jax.ShapeDtypeStruct((SIDES, D), jnp.float32),
        jax.ShapeDtypeStruct((BINS, CELLS // 2 - SIDES), jnp.float32),
        jax.ShapeDtypeStruct((TLAT, 3, D), jnp.bfloat16),
        jax.ShapeDtypeStruct((TLAT, 2, D), jnp.bfloat16),
    ]
    return pl.pallas_call(
        sides_kernel,
        in_specs=[VMEM] * 3,
        out_specs=[VMEM] * len(outs),
        out_shape=outs,
        scratch_shapes=[pltpu.VMEM((BINS, CELLS // 2), jnp.float32)],
        compiler_params=pltpu.CompilerParams(vmem_limit_bytes=32 << 20),
        cost_estimate=scatter_cost(arrived.shape[0]),
    )(arrived, embed_weight, embed_bias)


def edges(arrived, *arrays):
    outs = [
        jax.ShapeDtypeStruct((BINS, CELLS // 2), jnp.float32),
        jax.ShapeDtypeStruct((CELLS // 2 - SIDES, D), jnp.float32),
        jax.ShapeDtypeStruct((5, TLON, D), jnp.bfloat16),
    ]
    return pl.pallas_call(
        edges_kernel,
        in_specs=[VMEM] * (1 + len(arrays)),
        out_specs=[VMEM] * len(outs),
        out_shape=outs,
        compiler_params=pltpu.CompilerParams(vmem_limit_bytes=32 << 20),
        cost_estimate=scatter_cost(arrived.shape[0]),
    )(arrived, *arrays)


def put_rows(even, odd, rows, tile, west, east):
    even[rows, 0:1] = west[:, 1:2]
    even[rows, 1 : HALF + 1] = tile[:, :HALF]
    even[rows, HALF + 1 : HALF + 2] = east[:, 0:1]
    odd[rows, 0:1] = west[:, 0:1]
    odd[rows, 1:2] = west[:, 2:3]
    odd[rows, 2 : HALF + 2] = tile[:, HALF:]
    odd[rows, HALF + 2 : HALF + 3] = east[:, 1:2]


def strided_rows(even, odd, starts, weight_ref, bias_ref):
    pieces = []
    for a in range(3):
        for source, at in ((odd, 0), (even, 0), (odd, 1)):
            rows = [source(start + a, at) for start in starts]
            pieces.append(jnp.concatenate(rows, axis=0).astype(jnp.bfloat16))
    strided = jnp.dot(
        jnp.concatenate(pieces, axis=1), weight_ref[...], preferred_element_type=jnp.float32
    )
    coarse = jax.nn.gelu(strided + bias_ref[...]).astype(jnp.bfloat16)
    return coarse.astype(jnp.float32).reshape(len(starts), SPAN, D)


def spans(*refs):
    rows = [(ref, i) for ref in refs for i in range(ref.shape[0])]
    return lambda i, at: rows[i][0][rows[i][1], at : at + SPAN, :]


def finished(coarse, first, count, depth_ref, gain_ref):
    mixed = coarse[first + 1 : first + count + 1, 1 : HALF + 1]
    for a in range(3):
        for c in range(3):
            tap = depth_ref[3 * a + c : 3 * a + c + 1, :]
            mixed = mixed + coarse[first + a : first + a + count, c : c + HALF] * tap
    centre = mixed - jnp.mean(mixed, axis=-1, keepdims=True)
    variance = jnp.mean(centre * centre, axis=-1, keepdims=True)
    return (centre * lax.rsqrt(variance + 1e-05) * gain_ref[...]).astype(jnp.bfloat16)


def inner_kernel(
    x_ref,
    half_ref,
    embed_ref,
    embed_bias_ref,
    sides_ref,
    edges_ref,
    west_ref,
    east_ref,
    weight_ref,
    bias_ref,
    depth_ref,
    gain_ref,
    _,
    own_even_ref,
    own_odd_ref,
    upper_ref,
    lower_ref,
    out_ref,
    total,
    even,
    odd,
    coarse,
):
    tiles = x_ref.shape[0]
    add_sums(x_ref, total, SLOTS, tiles * EARLY // 32, tiles, half_ref[...])
    inside = embedded_cells(total, embed_ref, embed_bias_ref)
    west, east = (r[...].astype(jnp.float32) for r in (west_ref, east_ref))
    sides = sides_ref[...].reshape(TLAT, 8, D)
    edges = edges_ref[: 10 * MID].reshape(5, 2 * MID, D)
    corner = edges_ref[10 * MID :].reshape(1, 2 * EXTRA, D)
    bulk = inside[: 20 * MID].reshape(TLAT - 6, 2 * MID, D)
    rest = inside[20 * MID :].reshape(1, 2 * (MID - EXTRA), D)
    even[:, 0:1] = west[:, 1:2]
    odd[:, 0:1] = west[:, 0:1]
    odd[:, 1:2] = west[:, 2:3]
    for parity, held in ((0, even), (1, odd)):
        at = 1 + parity
        mid = slice(at + 1, at + 1 + MID)
        cut = at + 1 + EXTRA
        own = slice(parity * MID, (parity + 1) * MID)
        held[:, at : at + 1] = sides[:, 4 * parity : 4 * parity + 1]
        held[:, at + 1 + MID : at + HALF] = sides[:, 4 * parity + 1 : 4 * parity + 4]
        held[:, at + HALF : at + HALF + 1] = east[:, parity : parity + 1]
        held[0:2, mid] = edges[0:2, own]
        held[TLAT - 3 :, mid] = edges[2:5, own]
        held[3 : TLAT - 3, mid] = bulk[:, own]
        held[2:3, at + 1 : cut] = corner[:, EXTRA * parity : EXTRA * (parity + 1)]
        span = MID - EXTRA
        held[2:3, cut : cut + span] = rest[:, span * parity : span * (parity + 1)]
    starts = range(1, TLAT - 2, 2)
    coarse[...] = strided_rows(spans(even), spans(odd), starts, weight_ref, bias_ref)
    for held, own_ref in ((even, own_even_ref), (odd, own_odd_ref)):
        own_ref[0:2] = held[0:2]
        own_ref[2:3] = held[TLAT - 1 :]
    upper_ref[...] = coarse[0:2]
    lower_ref[...] = coarse[ROWS - 3 : ROWS - 1]
    out_ref[...] = finished(coarse, 0, ROWS - 3, depth_ref, gain_ref)


def inner(arrived, *arrays):
    pair = jax.ShapeDtypeStruct((2, SPAN, D), jnp.float32)
    owns = [jax.ShapeDtypeStruct((3, n, D), jnp.float32) for n in (SPAN, SPAN + 8)]
    return pl.pallas_call(
        inner_kernel,
        in_specs=[VMEM] * (1 + len(arrays)),
        out_specs=[VMEM] * 5,
        out_shape=owns + [pair, pair, jax.ShapeDtypeStruct((ROWS - 3, HALF, D), jnp.bfloat16)],
        scratch_shapes=[
            pltpu.VMEM((BINS, CELLS // 2), jnp.float32),
            pltpu.VMEM((TLAT, SPAN, D), jnp.float32),
            pltpu.VMEM((TLAT, SPAN + 8, D), jnp.float32),
            pltpu.VMEM((ROWS - 1, SPAN, D), jnp.float32),
        ],
        compiler_params=pltpu.CompilerParams(vmem_limit_bytes=32 << 20),
        cost_estimate=scatter_cost(arrived.shape[0]),
    )(arrived, *arrays)


def outer_kernel(
    place_ref,
    own_even_ref,
    own_odd_ref,
    upper_ref,
    lower_ref,
    done_ref,
    other_ref,
    pair_ref,
    weight_ref,
    bias_ref,
    depth_ref,
    gain_ref,
    out_hbm,
    north_even,
    north_odd,
    south_even,
    south_odd,
    coarse,
    top,
    bottom,
    sent,
):
    inner_copy = pltpu.make_async_copy(done_ref, out_hbm.at[2 : ROWS - 1], sent.at[0])
    inner_copy.start()
    paired, other = (r[...].astype(jnp.float32) for r in (pair_ref, other_ref))
    lower, above, below = (place_ref[i : i + 1] for i in range(3))
    upper = 1.0 - lower
    north = paired * (lower * above) + other * (upper * above)
    south = (paired * upper + other * lower)[:2]
    for even, odd, part in ((north_even, north_odd, north), (south_even, south_odd, south)):
        west, east = part[:, TLON : TLON + 3], part[:, TLON + 3 :]
        put_rows(even, odd, slice(0, part.shape[0]), part[:, :TLON], west, east)
    edge = strided_rows(
        spans(north_even, own_even_ref, south_even),
        spans(north_odd, own_odd_ref, south_odd),
        (0, 2, 5),
        weight_ref,
        bias_ref,
    )
    coarse[0] = edge[0] * above
    coarse[1] = edge[1]
    coarse[2:4] = upper_ref[...]
    coarse[4:6] = lower_ref[...]
    coarse[6] = edge[2] * below
    top[...] = finished(coarse, 0, 2, depth_ref, gain_ref)
    bottom[...] = finished(coarse, 4, 1, depth_ref, gain_ref)
    copies = [
        inner_copy,
        pltpu.make_async_copy(top, out_hbm.at[0:2], sent.at[1]),
        pltpu.make_async_copy(bottom, out_hbm.at[ROWS - 1 : ROWS], sent.at[2]),
    ]
    for copy in copies[1:]:
        copy.start()
    for copy in copies:
        copy.wait()


def outer(*arrays):
    return pl.pallas_call(
        outer_kernel,
        in_specs=[VMEM] * len(arrays),
        out_specs=ANY,
        out_shape=jax.ShapeDtypeStruct((ROWS, HALF, D), jnp.bfloat16),
        scratch_shapes=[
            pltpu.VMEM((3, SPAN, D), jnp.float32),
            pltpu.VMEM((3, SPAN + 8, D), jnp.float32),
            pltpu.VMEM((2, SPAN, D), jnp.float32),
            pltpu.VMEM((2, SPAN + 8, D), jnp.float32),
            pltpu.VMEM((7, SPAN, D), jnp.float32),
            pltpu.VMEM((2, HALF, D), jnp.bfloat16),
            pltpu.VMEM((1, HALF, D), jnp.bfloat16),
            pltpu.SemaphoreType.DMA((3,)),
        ],
        compiler_params=pltpu.CompilerParams(vmem_limit_bytes=16 << 20),
    )(*arrays)


def on_device(
    obs_values,
    obs_offset,
    obs_cell,
    obs_slot,
    obs_count,
    embed_weight,
    embed_bias,
    stride_weight,
    stride_bias,
    depth_weight,
    norm_gain,
):
    lon_count, lat_count = lax.axis_size("lon"), lax.axis_size("lat")
    lat = lax.axis_index("lat")
    packed = pack(obs_values, obs_offset, obs_cell, obs_slot, obs_count)
    lower, above, below = lat % 2 == 1, lat > 0, lat < lat_count - 1
    packed, lower, above, below = lax.optimization_barrier((packed, lower, above, below))
    arrived = lax.all_to_all(packed, ("lon", "lat"), split_axis=0, concat_axis=0, tiled=True)
    embed = embed_bias.reshape(1, D)
    side_cells, sums, last, first = sides(arrived, embed_weight, embed)
    sums, lower, above, below = lax.optimization_barrier((sums, lower, above, below))
    half, edge_cells, rows = edges(arrived, embed_weight, embed, side_cells, sums)
    ring = [(i, (i + 1) % lon_count) for i in range(lon_count)]
    west = lax.ppermute(last, "lon", ring)
    east = lax.ppermute(first, "lon", [(j, i) for i, j in ring])
    weight, bias = stride_weight.reshape(9 * D, D), stride_bias.reshape(1, D)
    top = jnp.concatenate([rows[:3], west[:3], east[:3]], axis=1)
    bottom = jnp.concatenate([rows[2:], west[TLAT - 3 :], east[TLAT - 3 :]], axis=1)
    pairs = [(i, i + 1) for i in range(0, lat_count - 1, 2)]
    others = [(i, (i + 1) % lat_count) for i in range(1, lat_count, 2)]
    paired = lax.ppermute(
        jnp.where(lower, top, bottom), "lat", pairs + [(j, i) for i, j in pairs]
    )
    other = lax.ppermute(
        jnp.where(lower, bottom, top), "lat", others + [(j, i) for i, j in others]
    )
    gain = norm_gain.reshape(1, D)
    index = lax.broadcasted_iota(jnp.int32, (3, D), 0)
    flags = jnp.where(index == 0, lower, jnp.where(index == 1, above, below))
    place = flags.astype(jnp.float32)
    inside = inner(
        arrived,
        half,
        embed_weight,
        embed,
        side_cells,
        edge_cells,
        west,
        east,
        weight,
        bias,
        depth_weight,
        gain,
        place,
    )
    return outer(place, *inside, other, paired, weight, bias, depth_weight, gain)


def solution(mesh):
    placed = (
        P(("lon", "lat"), None, None),
        P(("lon", "lat"), None, None),
        P(("lon", "lat"), None),
        P(("lon", "lat"), None),
        P(("lon", "lat"), None),
        P(),
        P(),
        P(),
        P(),
        P(),
        P(),
    )
    return jax.shard_map(
        on_device, mesh=mesh, in_specs=placed, out_specs=P("lat", "lon", None), check_vma=False
    )
```

```python
import functools

import jax
import jax.numpy as jnp
from jax import lax
from jax.experimental import pallas as pl
from jax.experimental.pallas import tpu as pltpu
from jax.sharding import PartitionSpec as P

D = 256
OBS_VARS = 31
WIDTH = OBS_VARS + 1
SLOTS = 12
BINS = SLOTS * WIDTH
TLAT = 16
TLON = 32
HALF = TLON // 2
ROWS = TLAT // 2
LANES = 128
GROUP = 16
TILE = 4
CHUNK = 32
EARLY = 18
SPAN = 24
CELLS = TLAT * TLON
MID = 12
EXTRA = 4
SIDES = TLAT * 8
FRAME = TLON + 5

ANY = pl.BlockSpec(memory_space=pl.ANY)
VMEM = pl.BlockSpec(memory_space=pltpu.VMEM)


def placed_cells(cell):
    row, column = cell // TLON, cell % TLON
    pair, parity = column // 2, column % 2
    side = (pair < 1) | (pair > MID)
    edge = (row < 2) | (row >= TLAT - 3)
    corner = (row == 2) & (pair <= EXTRA)
    at_side = row * 8 + parity * 4 + jnp.where(pair < 1, 0, pair - MID)
    at_edge = SIDES + jnp.where(row < 2, row, row - TLAT + 5) * 2 * MID + parity * MID + pair - 1
    at_corner = SIDES + 10 * MID + parity * EXTRA + pair - 1
    at_row = CELLS // 2 - 2 * (MID - EXTRA) + parity * (MID - EXTRA) + pair - 1 - EXTRA
    at_inside = (row - 3) * 2 * MID + parity * MID + pair - 1
    rim = side | edge | corner
    in_rim = jnp.where(side, at_side, jnp.where(edge, at_edge, at_corner))
    return rim, jnp.where(rim, in_rim, jnp.where(row == 2, at_row, at_inside))


def pack_kernel(
    count_hbm,
    values_hbm,
    offset_hbm,
    cell_hbm,
    slot_hbm,
    out,
    count,
    values,
    offset,
    cell,
    slot,
    rows,
    here,
):
    tiles, capacity = cell.shape
    halves = capacity // LANES
    used = out.shape[1] * TILE
    stride = rows.shape[0] // (tiles + 1)
    groups = tiles // GROUP

    def at(j):
        return pl.ds(j * GROUP, GROUP)

    pairs = ((count_hbm, count), (offset_hbm, offset), (cell_hbm, cell), (slot_hbm, slot))
    small = [
        pltpu.make_async_copy(a, b, here.at[groups + i]) for i, (a, b) in enumerate(pairs)
    ]
    large = [
        pltpu.make_async_copy(values_hbm.at[:, at(j)], values.at[:, at(j)], here.at[j])
        for j in range(groups)
    ]
    for copy in small + large:
        copy.start()
    for copy in small:
        copy.wait()
    square = (tiles, tiles)
    diagonal = lax.broadcasted_iota(jnp.int32, square, 0) == lax.broadcasted_iota(
        jnp.int32, square, 1
    )
    counts = jnp.sum(jnp.where(diagonal, count[...], 0), axis=1, keepdims=True)
    position = lax.broadcasted_iota(jnp.int32, (tiles, capacity), 1)
    dy, dx = offset[:, 0, :], offset[:, 1, :]
    weight = jnp.where(position < counts, jnp.exp(-2.0 * (dy * dy + dx * dx)), 0.0)
    rim, place = placed_cells(cell[...])
    codes = (
        (slot[...] + jnp.where(rim, 0, SLOTS)).astype(jnp.float32),
        place.astype(jnp.float32),
    )
    base = halves * WIDTH
    for j in range(groups):
        own = slice(j * GROUP, (j + 1) * GROUP)

        def put(row, value, h, first=j * GROUP * stride):
            rows[pl.ds(first + row, GROUP, stride=stride), :] = value[
                :, h * LANES : (h + 1) * LANES
            ]

        for h in range(halves):
            put(h * WIDTH + OBS_VARS, weight[own], h)
            for i, code in enumerate(codes):
                put(base + i * halves + h, code[own], h)
        large[j].wait()
        for k in range(OBS_VARS):
            scaled = values[k, own, :].astype(jnp.float32) * weight[own]
            for h in range(halves):
                put(h * WIDTH + k, scaled, h)
        for d in range(j * GROUP, (j + 1) * GROUP):
            block = rows[d * stride : (d + 1) * stride, :].astype(jnp.bfloat16)
            out[d] = block.reshape(stride // TILE, TILE, LANES)[: used // TILE]


def pack(obs_values, obs_offset, obs_cell, obs_slot, obs_count):
    tiles, _, capacity = obs_values.shape
    used = capacity // LANES * (WIDTH + 2)
    stride = -(-used // 8) * 8
    values = jnp.transpose(obs_values, (1, 0, 2))
    shape = (tiles, used // TILE, TILE, LANES)
    arrays = (obs_count, values, obs_offset, obs_cell, obs_slot)
    return pl.pallas_call(
        pack_kernel,
        in_specs=[ANY] * len(arrays),
        out_specs=VMEM,
        out_shape=pltpu.VMEM(shape, jnp.bfloat16),
        scratch_shapes=[pltpu.VMEM(a.shape, a.dtype) for a in arrays]
        + [
            pltpu.VMEM(((tiles + 1) * stride, LANES), jnp.float32),
            pltpu.SemaphoreType.DMA((tiles // GROUP + 4,)),
        ],
        compiler_params=pltpu.CompilerParams(vmem_limit_bytes=24 << 20),
    )(*(pltpu.with_memory_space_constraint(a, pltpu.HBM) for a in arrays))


def add_sums(x_ref, total, first_slot, begin, end, held=None):
    blocks = x_ref.shape[1]
    halves = blocks * TILE // WIDTH
    step = WIDTH // TILE
    tall = 16
    iota = lax.broadcasted_iota(jnp.int32, (tall, LANES), 0).astype(jnp.float32)
    one = jnp.ones((tall, LANES), jnp.bfloat16)
    none = jnp.zeros((tall, LANES), jnp.bfloat16)
    zero = jnp.zeros((WIDTH, LANES), jnp.bfloat16)
    cells = [(iota + r).astype(jnp.bfloat16) for r in range(0, CELLS // 2, tall)]

    def operands(source):
        codes = x_ref[source, halves * step].astype(jnp.float32)
        spread, hot = [], []
        for h in range(halves):
            value = x_ref[source, h * step : (h + 1) * step].reshape(WIDTH, LANES)
            slot = jnp.broadcast_to(codes[h : h + 1], (WIDTH, LANES)).astype(jnp.bfloat16)
            place = codes[halves + h : halves + h + 1]
            place = jnp.broadcast_to(place, (tall, LANES)).astype(jnp.bfloat16)
            slots = range(first_slot, first_slot + SLOTS)
            by_slot = [jnp.where(slot == jnp.bfloat16(s), value, zero) for s in slots]
            by_cell = [jnp.where(place == c, one, none) for c in cells]
            spread.append(jnp.concatenate(by_slot, axis=0))
            hot.append(jnp.concatenate(by_cell, axis=0))
        return jnp.concatenate(spread, axis=1), jnp.concatenate(hot, axis=1)

    def summed(first, count):
        spread, hot = zip(*(operands(first + g) for g in range(count)))
        return lax.dot_general(
            jnp.concatenate(spread, axis=1),
            jnp.concatenate(hot, axis=1),
            (((1,), (1,)), ((), ())),
            preferred_element_type=jnp.float32,
        )

    count = end - begin if end - begin <= CHUNK else CHUNK // 2
    total[...] = summed(begin, count) if held is None else held + summed(begin, count)

    @pl.loop(1, (end - begin) // count)
    def _(step):
        total[...] += summed(begin + step * count, count)


def embedded_cells(total, weight_ref, bias_ref):
    groups = []
    for s in range(SLOTS):
        block = total[s * WIDTH : (s + 1) * WIDTH, :]
        inverse = 1.0 / (1.0 + block[OBS_VARS:WIDTH, :])
        channel = lax.broadcasted_iota(jnp.int32, block.shape, 0)
        ratio = jnp.where(channel == OBS_VARS, block, block * inverse)
        groups.append(ratio.astype(jnp.bfloat16))
    projected = lax.dot_general(
        jnp.concatenate(groups, axis=0),
        weight_ref[...],
        (((0,), (0,)), ((), ())),
        preferred_element_type=jnp.float32,
    )
    return jax.nn.gelu(projected + bias_ref[...])


def sides_kernel(x_ref, weight_ref, bias_ref, sides_ref, sums_ref, last_ref, first_ref, total):
    add_sums(x_ref, total, 0, 0, x_ref.shape[0])
    sums_ref[...] = total[:, SIDES:]
    embedded = embedded_cells(total.at[:, :SIDES], weight_ref, bias_ref)
    sides_ref[...] = embedded
    sides = embedded.reshape(TLAT, 8, D)
    for i, c in enumerate((6, 3, 7)):
        last_ref[i] = sides[:, c, :].astype(jnp.bfloat16)
    for i, c in enumerate((0, 4)):
        first_ref[i] = sides[:, c, :].astype(jnp.bfloat16)


def edges_kernel(
    x_ref, weight_ref, bias_ref, sides_ref, sums_ref, half_ref, edges_ref, rows_ref
):
    add_sums(x_ref, half_ref, SLOTS, 0, x_ref.shape[0] * EARLY // 32)
    embedded = embedded_cells(sums_ref, weight_ref, bias_ref)
    edges_ref[...] = embedded
    middle = embedded[: 10 * MID].reshape(5, 2 * MID, D)
    sides = sides_ref[...].reshape(TLAT, 8, D)
    ends = jnp.concatenate([sides[:2], sides[TLAT - 3 :]], axis=0)
    parts = []
    for parity in range(2):
        at = 4 * parity
        parts += [
            ends[:, at : at + 1],
            middle[:, parity * MID : (parity + 1) * MID],
            ends[:, at + 1 : at + 4],
        ]
    rows_ref[...] = jnp.concatenate(parts, axis=1).astype(jnp.bfloat16)


def scatter_cost(tiles):
    return pl.CostEstimate(
        flops=2 * tiles * 256 * BINS * CELLS // 2, bytes_accessed=4 << 20, transcendentals=0
    )


def sides(arrived, embed_weight, embed_bias):
    outs = [
        jax.ShapeDtypeStruct((SIDES, D), jnp.float32),
        jax.ShapeDtypeStruct((BINS, CELLS // 2 - SIDES), jnp.float32),
        jax.ShapeDtypeStruct((3, TLAT, D), jnp.bfloat16),
        jax.ShapeDtypeStruct((2, TLAT, D), jnp.bfloat16),
    ]
    return pl.pallas_call(
        sides_kernel,
        in_specs=[VMEM] * 3,
        out_specs=[VMEM] * len(outs),
        out_shape=outs,
        scratch_shapes=[pltpu.VMEM((BINS, CELLS // 2), jnp.float32)],
        compiler_params=pltpu.CompilerParams(vmem_limit_bytes=32 << 20),
        cost_estimate=scatter_cost(arrived.shape[0]),
    )(arrived, embed_weight, embed_bias)


def edges(arrived, *arrays):
    outs = [
        jax.ShapeDtypeStruct((BINS, CELLS // 2), jnp.float32),
        jax.ShapeDtypeStruct((CELLS // 2 - SIDES, D), jnp.float32),
        jax.ShapeDtypeStruct((5, TLON, D), jnp.bfloat16),
    ]
    return pl.pallas_call(
        edges_kernel,
        in_specs=[VMEM] * (1 + len(arrays)),
        out_specs=[VMEM] * len(outs),
        out_shape=outs,
        compiler_params=pltpu.CompilerParams(vmem_limit_bytes=32 << 20),
        cost_estimate=scatter_cost(arrived.shape[0]),
    )(arrived, *arrays)


def put_rows(even, odd, rows, tile, west, east):
    even[rows, 0:1] = west[:, 1:2]
    even[rows, 1 : HALF + 1] = tile[:, :HALF]
    even[rows, HALF + 1 : HALF + 2] = east[:, 0:1]
    odd[rows, 0:1] = west[:, 0:1]
    odd[rows, 1:2] = west[:, 2:3]
    odd[rows, 2 : HALF + 2] = tile[:, HALF:]
    odd[rows, HALF + 2 : HALF + 3] = east[:, 1:2]


def strided_rows(even, odd, starts, weight_ref, bias_ref):
    pieces = []
    for a in range(3):
        for source, at in ((odd, 0), (even, 0), (odd, 1)):
            rows = [source(start + a, at) for start in starts]
            pieces.append(jnp.concatenate(rows, axis=0).astype(jnp.bfloat16))
    strided = jnp.dot(
        jnp.concatenate(pieces, axis=1), weight_ref[...], preferred_element_type=jnp.float32
    )
    coarse = jax.nn.gelu(strided + bias_ref[...]).astype(jnp.bfloat16)
    return coarse.astype(jnp.float32).reshape(len(starts), SPAN, D)


def spans(*refs):
    rows = [(ref, i) for ref in refs for i in range(ref.shape[0])]
    return lambda i, at: rows[i][0][rows[i][1], at : at + SPAN, :]


def finished(coarse, first, count, depth_ref, gain_ref):
    mixed = coarse[first + 1 : first + count + 1, 1 : HALF + 1]
    for a in range(3):
        for c in range(3):
            tap = depth_ref[3 * a + c : 3 * a + c + 1, :]
            mixed = mixed + coarse[first + a : first + a + count, c : c + HALF] * tap
    centre = mixed - jnp.mean(mixed, axis=-1, keepdims=True)
    variance = jnp.mean(centre * centre, axis=-1, keepdims=True)
    return (centre * lax.rsqrt(variance + 1e-05) * gain_ref[...]).astype(jnp.bfloat16)


def inner_kernel(
    x_ref,
    half_ref,
    embed_ref,
    embed_bias_ref,
    sides_ref,
    edges_ref,
    west_ref,
    east_ref,
    weight_ref,
    bias_ref,
    depth_ref,
    gain_ref,
    _,
    own_even_ref,
    own_odd_ref,
    upper_ref,
    lower_ref,
    out_ref,
    total,
    even,
    odd,
    coarse,
):
    tiles = x_ref.shape[0]
    add_sums(x_ref, total, SLOTS, tiles * EARLY // 32, tiles, half_ref[...])
    inside = embedded_cells(total, embed_ref, embed_bias_ref)
    west, east = (r[...].astype(jnp.float32) for r in (west_ref, east_ref))
    sides = sides_ref[...].reshape(TLAT, 8, D)
    edges = edges_ref[: 10 * MID].reshape(5, 2 * MID, D)
    corner = edges_ref[10 * MID :].reshape(1, 2 * EXTRA, D)
    bulk = inside[: 20 * MID].reshape(TLAT - 6, 2 * MID, D)
    rest = inside[20 * MID :].reshape(1, 2 * (MID - EXTRA), D)
    even[:, 0:1] = west[1].reshape(TLAT, 1, D)
    odd[:, 0:1] = west[0].reshape(TLAT, 1, D)
    odd[:, 1:2] = west[2].reshape(TLAT, 1, D)
    for parity, held in ((0, even), (1, odd)):
        at = 1 + parity
        mid = slice(at + 1, at + 1 + MID)
        cut = at + 1 + EXTRA
        own = slice(parity * MID, (parity + 1) * MID)
        held[:, at : at + 1] = sides[:, 4 * parity : 4 * parity + 1]
        held[:, at + 1 + MID : at + HALF] = sides[:, 4 * parity + 1 : 4 * parity + 4]
        held[:, at + HALF : at + HALF + 1] = east[parity].reshape(TLAT, 1, D)
        held[0:2, mid] = edges[0:2, own]
        held[TLAT - 3 :, mid] = edges[2:5, own]
        held[3 : TLAT - 3, mid] = bulk[:, own]
        held[2:3, at + 1 : cut] = corner[:, EXTRA * parity : EXTRA * (parity + 1)]
        span = MID - EXTRA
        held[2:3, cut : cut + span] = rest[:, span * parity : span * (parity + 1)]
    starts = range(1, TLAT - 2, 2)
    coarse[...] = strided_rows(spans(even), spans(odd), starts, weight_ref, bias_ref)
    for held, own_ref in ((even, own_even_ref), (odd, own_odd_ref)):
        own_ref[0:2] = held[0:2]
        own_ref[2:3] = held[TLAT - 1 :]
    upper_ref[...] = coarse[0:2]
    lower_ref[...] = coarse[ROWS - 3 : ROWS - 1]
    out_ref[...] = finished(coarse, 0, ROWS - 3, depth_ref, gain_ref)


def inner(arrived, *arrays):
    pair = jax.ShapeDtypeStruct((2, SPAN, D), jnp.float32)
    owns = [jax.ShapeDtypeStruct((3, n, D), jnp.float32) for n in (SPAN, SPAN + 8)]
    return pl.pallas_call(
        inner_kernel,
        in_specs=[VMEM] * (1 + len(arrays)),
        out_specs=[VMEM] * 5,
        out_shape=owns + [pair, pair, jax.ShapeDtypeStruct((ROWS - 3, HALF, D), jnp.bfloat16)],
        scratch_shapes=[
            pltpu.VMEM((BINS, CELLS // 2), jnp.float32),
            pltpu.VMEM((TLAT, SPAN, D), jnp.float32),
            pltpu.VMEM((TLAT, SPAN + 8, D), jnp.float32),
            pltpu.VMEM((ROWS - 1, SPAN, D), jnp.float32),
        ],
        compiler_params=pltpu.CompilerParams(vmem_limit_bytes=32 << 20),
        cost_estimate=scatter_cost(arrived.shape[0]),
    )(arrived, *arrays)


def outer_kernel(
    place_ref,
    own_even_ref,
    own_odd_ref,
    upper_ref,
    lower_ref,
    done_ref,
    other_ref,
    pair_ref,
    weight_ref,
    bias_ref,
    depth_ref,
    gain_ref,
    out_hbm,
    north_even,
    north_odd,
    south_even,
    south_odd,
    coarse,
    top,
    bottom,
    sent,
):
    inner_copy = pltpu.make_async_copy(done_ref, out_hbm.at[2 : ROWS - 1], sent.at[0])
    inner_copy.start()
    paired, other = (r[...].astype(jnp.float32) for r in (pair_ref, other_ref))
    lower, above, below = (place_ref[i : i + 1] for i in range(3))
    upper = 1.0 - lower
    north = paired * (lower * above) + other * (upper * above)
    south = paired * upper + other * lower
    for even, odd, part in ((north_even, north_odd, north), (south_even, south_odd, south)):
        count = even.shape[0]
        tile = part[: 3 * TLON].reshape(3, TLON, D)[:count]
        sides = [
            part[at : at + count].reshape(count, 1, D)
            for at in range(3 * TLON, 3 * FRAME, 3)
        ]
        west = jnp.concatenate(sides[:3], axis=1)
        east = jnp.concatenate(sides[3:], axis=1)
        put_rows(even, odd, slice(0, count), tile, west, east)
    edge = strided_rows(
        spans(north_even, own_even_ref, south_even),
        spans(north_odd, own_odd_ref, south_odd),
        (0, 2, 5),
        weight_ref,
        bias_ref,
    )
    coarse[0] = edge[0] * above
    coarse[1] = edge[1]
    coarse[2:4] = upper_ref[...]
    coarse[4:6] = lower_ref[...]
    coarse[6] = edge[2] * below
    top[...] = finished(coarse, 0, 2, depth_ref, gain_ref)
    bottom[...] = finished(coarse, 4, 1, depth_ref, gain_ref)
    copies = [
        inner_copy,
        pltpu.make_async_copy(top, out_hbm.at[0:2], sent.at[1]),
        pltpu.make_async_copy(bottom, out_hbm.at[ROWS - 1 : ROWS], sent.at[2]),
    ]
    for copy in copies[1:]:
        copy.start()
    for copy in copies:
        copy.wait()


def outer(*arrays):
    return pl.pallas_call(
        outer_kernel,
        in_specs=[VMEM] * len(arrays),
        out_specs=ANY,
        out_shape=jax.ShapeDtypeStruct((ROWS, HALF, D), jnp.bfloat16),
        scratch_shapes=[
            pltpu.VMEM((3, SPAN, D), jnp.float32),
            pltpu.VMEM((3, SPAN + 8, D), jnp.float32),
            pltpu.VMEM((2, SPAN, D), jnp.float32),
            pltpu.VMEM((2, SPAN + 8, D), jnp.float32),
            pltpu.VMEM((7, SPAN, D), jnp.float32),
            pltpu.VMEM((2, HALF, D), jnp.bfloat16),
            pltpu.VMEM((1, HALF, D), jnp.bfloat16),
            pltpu.SemaphoreType.DMA((3,)),
        ],
        compiler_params=pltpu.CompilerParams(vmem_limit_bytes=16 << 20),
    )(*arrays)


def on_device(
    obs_values,
    obs_offset,
    obs_cell,
    obs_slot,
    obs_count,
    embed_weight,
    embed_bias,
    stride_weight,
    stride_bias,
    depth_weight,
    norm_gain,
):
    lon_count, lat_count = lax.axis_size("lon"), lax.axis_size("lat")
    lat = lax.axis_index("lat")
    packed = pack(obs_values, obs_offset, obs_cell, obs_slot, obs_count)
    lower, above, below = lat % 2 == 1, lat > 0, lat < lat_count - 1
    packed, lower, above, below = lax.optimization_barrier((packed, lower, above, below))
    arrived = lax.all_to_all(packed, ("lon", "lat"), split_axis=0, concat_axis=0, tiled=True)
    embed = embed_bias.reshape(1, D)
    side_cells, sums, last, first = sides(arrived, embed_weight, embed)
    sums, lower, above, below = lax.optimization_barrier((sums, lower, above, below))
    half, edge_cells, rows = edges(arrived, embed_weight, embed, side_cells, sums)
    ring = [(i, (i + 1) % lon_count) for i in range(lon_count)]
    west = lax.ppermute(last, "lon", ring)
    east = lax.ppermute(first, "lon", [(j, i) for i, j in ring])
    weight, bias = stride_weight.reshape(9 * D, D), stride_bias.reshape(1, D)
    ends = [slice(0, 3), slice(TLAT - 3, TLAT)]
    top, bottom = (
        jnp.concatenate([part.reshape(-1, D) for part in (rows[own], west[:, end], east[:, end])])
        for own, end in zip((slice(0, 3), slice(2, 5)), ends)
    )
    pairs = [(i, i + 1) for i in range(0, lat_count - 1, 2)]
    others = [(i, (i + 1) % lat_count) for i in range(1, lat_count, 2)]
    paired = lax.ppermute(
        jnp.where(lower, top, bottom), "lat", pairs + [(j, i) for i, j in pairs]
    )
    other = lax.ppermute(
        jnp.where(lower, bottom, top), "lat", others + [(j, i) for i, j in others]
    )
    gain = norm_gain.reshape(1, D)
    index = lax.broadcasted_iota(jnp.int32, (3, D), 0)
    flags = jnp.where(index == 0, lower, jnp.where(index == 1, above, below))
    place = flags.astype(jnp.float32)
    inside = inner(
        arrived,
        half,
        embed_weight,
        embed,
        side_cells,
        edge_cells,
        west,
        east,
        weight,
        bias,
        depth_weight,
        gain,
        place,
    )
    return outer(place, *inside, other, paired, weight, bias, depth_weight, gain)


def solution(mesh):
    placed = (
        P(("lon", "lat"), None, None),
        P(("lon", "lat"), None, None),
        P(("lon", "lat"), None),
        P(("lon", "lat"), None),
        P(("lon", "lat"), None),
        P(),
        P(),
        P(),
        P(),
        P(),
        P(),
    )
    return jax.shard_map(
        on_device, mesh=mesh, in_specs=placed, out_specs=P("lat", "lon", None), check_vma=False
    )
```

```python
import functools

import jax
import jax.numpy as jnp
from jax import lax
from jax.experimental import pallas as pl
from jax.experimental.pallas import tpu as pltpu
from jax.sharding import PartitionSpec as P

D = 256
OBS_VARS = 31
WIDTH = OBS_VARS + 1
SLOTS = 12
BINS = SLOTS * WIDTH
TLAT = 16
TLON = 32
HALF = TLON // 2
ROWS = TLAT // 2
LANES = 128
GROUP = 16
TILE = 4
CHUNK = 32
EARLY = 22
SPAN = 24
CELLS = TLAT * TLON
MID = 12
EXTRA = 4
SIDES = TLAT * 8
FRAME = TLON + 5

ANY = pl.BlockSpec(memory_space=pl.ANY)
VMEM = pl.BlockSpec(memory_space=pltpu.VMEM)


def placed_cells(cell):
    row, column = cell // TLON, cell % TLON
    pair, parity = column // 2, column % 2
    side = (pair < 1) | (pair > MID)
    edge = (row < 2) | (row >= TLAT - 3)
    corner = (row == 2) & (pair <= EXTRA)
    at_side = row * 8 + parity * 4 + jnp.where(pair < 1, 0, pair - MID)
    at_edge = SIDES + jnp.where(row < 2, row, row - TLAT + 5) * 2 * MID + parity * MID + pair - 1
    at_corner = SIDES + 10 * MID + parity * EXTRA + pair - 1
    at_row = CELLS // 2 - 2 * (MID - EXTRA) + parity * (MID - EXTRA) + pair - 1 - EXTRA
    at_inside = (row - 3) * 2 * MID + parity * MID + pair - 1
    rim = side | edge | corner
    in_rim = jnp.where(side, at_side, jnp.where(edge, at_edge, at_corner))
    return rim, jnp.where(rim, in_rim, jnp.where(row == 2, at_row, at_inside))


def pack_kernel(
    count_hbm,
    values_hbm,
    offset_hbm,
    cell_hbm,
    slot_hbm,
    out,
    count,
    values,
    offset,
    cell,
    slot,
    rows,
    here,
):
    tiles, capacity = cell.shape
    halves = capacity // LANES
    used = out.shape[1] * TILE
    stride = rows.shape[0] // (tiles + 1)
    groups = tiles // GROUP

    def at(j):
        return pl.ds(j * GROUP, GROUP)

    pairs = ((count_hbm, count), (offset_hbm, offset), (cell_hbm, cell), (slot_hbm, slot))
    small = [
        pltpu.make_async_copy(a, b, here.at[groups + i]) for i, (a, b) in enumerate(pairs)
    ]
    large = [
        pltpu.make_async_copy(values_hbm.at[:, at(j)], values.at[:, at(j)], here.at[j])
        for j in range(groups)
    ]
    for copy in small + large:
        copy.start()
    for copy in small:
        copy.wait()
    square = (tiles, tiles)
    diagonal = lax.broadcasted_iota(jnp.int32, square, 0) == lax.broadcasted_iota(
        jnp.int32, square, 1
    )
    counts = jnp.sum(jnp.where(diagonal, count[...], 0), axis=1, keepdims=True)
    position = lax.broadcasted_iota(jnp.int32, (tiles, capacity), 1)
    dy, dx = offset[:, 0, :], offset[:, 1, :]
    weight = jnp.where(position < counts, jnp.exp(-2.0 * (dy * dy + dx * dx)), 0.0)
    rim, place = placed_cells(cell[...])
    codes = (
        (slot[...] + jnp.where(rim, 0, SLOTS)).astype(jnp.float32),
        place.astype(jnp.float32),
    )
    base = halves * WIDTH
    for j in range(groups):
        own = slice(j * GROUP, (j + 1) * GROUP)

        def put(row, value, h, first=j * GROUP * stride):
            rows[pl.ds(first + row, GROUP, stride=stride), :] = value[
                :, h * LANES : (h + 1) * LANES
            ]

        for h in range(halves):
            put(h * WIDTH + OBS_VARS, weight[own], h)
            for i, code in enumerate(codes):
                put(base + i * halves + h, code[own], h)
        large[j].wait()
        for k in range(OBS_VARS):
            scaled = values[k, own, :].astype(jnp.float32) * weight[own]
            for h in range(halves):
                put(h * WIDTH + k, scaled, h)
        for d in range(j * GROUP, (j + 1) * GROUP):
            block = rows[d * stride : (d + 1) * stride, :].astype(jnp.bfloat16)
            out[d] = block.reshape(stride // TILE, TILE, LANES)[: used // TILE]


def pack(obs_values, obs_offset, obs_cell, obs_slot, obs_count):
    tiles, _, capacity = obs_values.shape
    used = capacity // LANES * (WIDTH + 2)
    stride = -(-used // 8) * 8
    values = jnp.transpose(obs_values, (1, 0, 2))
    shape = (tiles, used // TILE, TILE, LANES)
    arrays = (obs_count, values, obs_offset, obs_cell, obs_slot)
    return pl.pallas_call(
        pack_kernel,
        in_specs=[ANY] * len(arrays),
        out_specs=VMEM,
        out_shape=pltpu.VMEM(shape, jnp.bfloat16),
        scratch_shapes=[pltpu.VMEM(a.shape, a.dtype) for a in arrays]
        + [
            pltpu.VMEM(((tiles + 1) * stride, LANES), jnp.float32),
            pltpu.SemaphoreType.DMA((tiles // GROUP + 4,)),
        ],
        compiler_params=pltpu.CompilerParams(vmem_limit_bytes=24 << 20),
    )(*(pltpu.with_memory_space_constraint(a, pltpu.HBM) for a in arrays))


def add_sums(x_ref, total, first_slot, begin, end, held=None):
    blocks = x_ref.shape[1]
    halves = blocks * TILE // WIDTH
    step = WIDTH // TILE
    tall = 16
    iota = lax.broadcasted_iota(jnp.int32, (tall, LANES), 0).astype(jnp.float32)
    one = jnp.ones((tall, LANES), jnp.bfloat16)
    none = jnp.zeros((tall, LANES), jnp.bfloat16)
    zero = jnp.zeros((WIDTH, LANES), jnp.bfloat16)
    cells = [(iota + r).astype(jnp.bfloat16) for r in range(0, CELLS // 2, tall)]

    def operands(source):
        codes = x_ref[source, halves * step].astype(jnp.float32)
        spread, hot = [], []
        for h in range(halves):
            value = x_ref[source, h * step : (h + 1) * step].reshape(WIDTH, LANES)
            slot = jnp.broadcast_to(codes[h : h + 1], (WIDTH, LANES)).astype(jnp.bfloat16)
            place = codes[halves + h : halves + h + 1]
            place = jnp.broadcast_to(place, (tall, LANES)).astype(jnp.bfloat16)
            slots = range(first_slot, first_slot + SLOTS)
            by_slot = [jnp.where(slot == jnp.bfloat16(s), value, zero) for s in slots]
            by_cell = [jnp.where(place == c, one, none) for c in cells]
            spread.append(jnp.concatenate(by_slot, axis=0))
            hot.append(jnp.concatenate(by_cell, axis=0))
        return jnp.concatenate(spread, axis=1), jnp.concatenate(hot, axis=1)

    def summed(first, count):
        spread, hot = zip(*(operands(first + g) for g in range(count)))
        return lax.dot_general(
            jnp.concatenate(spread, axis=1),
            jnp.concatenate(hot, axis=1),
            (((1,), (1,)), ((), ())),
            preferred_element_type=jnp.float32,
        )

    count = end - begin if end - begin <= CHUNK else CHUNK // 2
    total[...] = summed(begin, count) if held is None else held + summed(begin, count)

    @pl.loop(1, (end - begin) // count)
    def _(step):
        total[...] += summed(begin + step * count, count)


def embedded_cells(total, weight_ref, bias_ref):
    groups = []
    for s in range(SLOTS):
        block = total[s * WIDTH : (s + 1) * WIDTH, :]
        inverse = 1.0 / (1.0 + block[OBS_VARS:WIDTH, :])
        channel = lax.broadcasted_iota(jnp.int32, block.shape, 0)
        ratio = jnp.where(channel == OBS_VARS, block, block * inverse)
        groups.append(ratio.astype(jnp.bfloat16))
    projected = lax.dot_general(
        jnp.concatenate(groups, axis=0),
        weight_ref[...],
        (((0,), (0,)), ((), ())),
        preferred_element_type=jnp.float32,
    )
    return jax.nn.gelu(projected + bias_ref[...])


def sides_kernel(x_ref, weight_ref, bias_ref, sides_ref, sums_ref, last_ref, first_ref, total):
    add_sums(x_ref, total, 0, 0, x_ref.shape[0])
    sums_ref[...] = total[:, SIDES:]
    embedded = embedded_cells(total.at[:, :SIDES], weight_ref, bias_ref)
    sides_ref[...] = embedded
    sides = embedded.reshape(TLAT, 8, D)
    for i, c in enumerate((6, 3, 7)):
        last_ref[i] = sides[:, c, :].astype(jnp.bfloat16)
    for i, c in enumerate((0, 4)):
        first_ref[i] = sides[:, c, :].astype(jnp.bfloat16)


def edges_kernel(
    x_ref, weight_ref, bias_ref, sides_ref, sums_ref, half_ref, edges_ref, rows_ref
):
    add_sums(x_ref, half_ref, SLOTS, 0, x_ref.shape[0] * EARLY // 32)
    embedded = embedded_cells(sums_ref, weight_ref, bias_ref)
    edges_ref[...] = embedded
    middle = embedded[: 10 * MID].reshape(5, 2 * MID, D)
    sides = sides_ref[...].reshape(TLAT, 8, D)
    ends = jnp.concatenate([sides[:2], sides[TLAT - 3 :]], axis=0)
    parts = []
    for parity in range(2):
        at = 4 * parity
        parts += [
            ends[:, at : at + 1],
            middle[:, parity * MID : (parity + 1) * MID],
            ends[:, at + 1 : at + 4],
        ]
    rows_ref[...] = jnp.concatenate(parts, axis=1).astype(jnp.bfloat16)


def scatter_cost(tiles):
    return pl.CostEstimate(
        flops=2 * tiles * 256 * BINS * CELLS // 2, bytes_accessed=4 << 20, transcendentals=0
    )


def sides(arrived, embed_weight, embed_bias):
    outs = [
        jax.ShapeDtypeStruct((SIDES, D), jnp.float32),
        jax.ShapeDtypeStruct((BINS, CELLS // 2 - SIDES), jnp.float32),
        jax.ShapeDtypeStruct((3, TLAT, D), jnp.bfloat16),
        jax.ShapeDtypeStruct((2, TLAT, D), jnp.bfloat16),
    ]
    return pl.pallas_call(
        sides_kernel,
        in_specs=[VMEM] * 3,
        out_specs=[VMEM] * len(outs),
        out_shape=outs,
        scratch_shapes=[pltpu.VMEM((BINS, CELLS // 2), jnp.float32)],
        compiler_params=pltpu.CompilerParams(vmem_limit_bytes=32 << 20),
        cost_estimate=scatter_cost(arrived.shape[0]),
    )(arrived, embed_weight, embed_bias)


def edges(arrived, *arrays):
    outs = [
        jax.ShapeDtypeStruct((BINS, CELLS // 2), jnp.float32),
        jax.ShapeDtypeStruct((CELLS // 2 - SIDES, D), jnp.float32),
        jax.ShapeDtypeStruct((5, TLON, D), jnp.bfloat16),
    ]
    return pl.pallas_call(
        edges_kernel,
        in_specs=[VMEM] * (1 + len(arrays)),
        out_specs=[VMEM] * len(outs),
        out_shape=outs,
        compiler_params=pltpu.CompilerParams(vmem_limit_bytes=32 << 20),
        cost_estimate=scatter_cost(arrived.shape[0]),
    )(arrived, *arrays)


def put_rows(even, odd, rows, tile, west, east):
    even[rows, 0:1] = west[:, 1:2]
    even[rows, 1 : HALF + 1] = tile[:, :HALF]
    even[rows, HALF + 1 : HALF + 2] = east[:, 0:1]
    odd[rows, 0:1] = west[:, 0:1]
    odd[rows, 1:2] = west[:, 2:3]
    odd[rows, 2 : HALF + 2] = tile[:, HALF:]
    odd[rows, HALF + 2 : HALF + 3] = east[:, 1:2]


def strided_rows(even, odd, starts, weight_ref, bias_ref):
    pieces = []
    for a in range(3):
        for source, at in ((odd, 0), (even, 0), (odd, 1)):
            rows = [source(start + a, at) for start in starts]
            pieces.append(jnp.concatenate(rows, axis=0).astype(jnp.bfloat16))
    strided = jnp.dot(
        jnp.concatenate(pieces, axis=1), weight_ref[...], preferred_element_type=jnp.float32
    )
    coarse = jax.nn.gelu(strided + bias_ref[...]).astype(jnp.bfloat16)
    return coarse.astype(jnp.float32).reshape(len(starts), SPAN, D)


def spans(*refs):
    rows = [(ref, i) for ref in refs for i in range(ref.shape[0])]
    return lambda i, at: rows[i][0][rows[i][1], at : at + SPAN, :]


def finished(coarse, first, count, depth_ref, gain_ref):
    mixed = coarse[first + 1 : first + count + 1, 1 : HALF + 1]
    for a in range(3):
        for c in range(3):
            tap = depth_ref[3 * a + c : 3 * a + c + 1, :]
            mixed = mixed + coarse[first + a : first + a + count, c : c + HALF] * tap
    centre = mixed - jnp.mean(mixed, axis=-1, keepdims=True)
    variance = jnp.mean(centre * centre, axis=-1, keepdims=True)
    return (centre * lax.rsqrt(variance + 1e-05) * gain_ref[...]).astype(jnp.bfloat16)


def inner_kernel(
    x_ref,
    half_ref,
    embed_ref,
    embed_bias_ref,
    sides_ref,
    edges_ref,
    west_ref,
    east_ref,
    weight_ref,
    bias_ref,
    depth_ref,
    gain_ref,
    _,
    own_even_ref,
    own_odd_ref,
    upper_ref,
    lower_ref,
    out_ref,
    total,
    even,
    odd,
    coarse,
):
    tiles = x_ref.shape[0]
    add_sums(x_ref, total, SLOTS, tiles * EARLY // 32, tiles, half_ref[...])
    inside = embedded_cells(total, embed_ref, embed_bias_ref)
    west, east = (r[...].astype(jnp.float32) for r in (west_ref, east_ref))
    sides = sides_ref[...].reshape(TLAT, 8, D)
    edges = edges_ref[: 10 * MID].reshape(5, 2 * MID, D)
    corner = edges_ref[10 * MID :].reshape(1, 2 * EXTRA, D)
    bulk = inside[: 20 * MID].reshape(TLAT - 6, 2 * MID, D)
    rest = inside[20 * MID :].reshape(1, 2 * (MID - EXTRA), D)
    even[:, 0:1] = west[1].reshape(TLAT, 1, D)
    odd[:, 0:1] = west[0].reshape(TLAT, 1, D)
    odd[:, 1:2] = west[2].reshape(TLAT, 1, D)
    for parity, held in ((0, even), (1, odd)):
        at = 1 + parity
        mid = slice(at + 1, at + 1 + MID)
        cut = at + 1 + EXTRA
        own = slice(parity * MID, (parity + 1) * MID)
        held[:, at : at + 1] = sides[:, 4 * parity : 4 * parity + 1]
        held[:, at + 1 + MID : at + HALF] = sides[:, 4 * parity + 1 : 4 * parity + 4]
        held[:, at + HALF : at + HALF + 1] = east[parity].reshape(TLAT, 1, D)
        held[0:2, mid] = edges[0:2, own]
        held[TLAT - 3 :, mid] = edges[2:5, own]
        held[3 : TLAT - 3, mid] = bulk[:, own]
        held[2:3, at + 1 : cut] = corner[:, EXTRA * parity : EXTRA * (parity + 1)]
        span = MID - EXTRA
        held[2:3, cut : cut + span] = rest[:, span * parity : span * (parity + 1)]
    starts = range(1, TLAT - 2, 2)
    coarse[...] = strided_rows(spans(even), spans(odd), starts, weight_ref, bias_ref)
    for held, own_ref in ((even, own_even_ref), (odd, own_odd_ref)):
        own_ref[0:2] = held[0:2]
        own_ref[2:3] = held[TLAT - 1 :]
    upper_ref[...] = coarse[0:2]
    lower_ref[...] = coarse[ROWS - 3 : ROWS - 1]
    out_ref[...] = finished(coarse, 0, ROWS - 3, depth_ref, gain_ref)


def inner(arrived, *arrays):
    pair = jax.ShapeDtypeStruct((2, SPAN, D), jnp.float32)
    owns = [jax.ShapeDtypeStruct((3, n, D), jnp.float32) for n in (SPAN, SPAN + 8)]
    return pl.pallas_call(
        inner_kernel,
        in_specs=[VMEM] * (1 + len(arrays)),
        out_specs=[VMEM] * 5,
        out_shape=owns + [pair, pair, jax.ShapeDtypeStruct((ROWS - 3, HALF, D), jnp.bfloat16)],
        scratch_shapes=[
            pltpu.VMEM((BINS, CELLS // 2), jnp.float32),
            pltpu.VMEM((TLAT, SPAN, D), jnp.float32),
            pltpu.VMEM((TLAT, SPAN + 8, D), jnp.float32),
            pltpu.VMEM((ROWS - 1, SPAN, D), jnp.float32),
        ],
        compiler_params=pltpu.CompilerParams(vmem_limit_bytes=32 << 20),
        cost_estimate=scatter_cost(arrived.shape[0]),
    )(arrived, *arrays)


def outer_kernel(
    place_ref,
    own_even_ref,
    own_odd_ref,
    upper_ref,
    lower_ref,
    done_ref,
    other_ref,
    pair_ref,
    weight_ref,
    bias_ref,
    depth_ref,
    gain_ref,
    out_hbm,
    north_even,
    north_odd,
    south_even,
    south_odd,
    coarse,
    top,
    bottom,
    sent,
):
    inner_copy = pltpu.make_async_copy(done_ref, out_hbm.at[2 : ROWS - 1], sent.at[0])
    inner_copy.start()
    paired, other = (r[...].astype(jnp.float32) for r in (pair_ref, other_ref))
    lower, above, below = (place_ref[i : i + 1] for i in range(3))
    upper = 1.0 - lower
    north = paired * (lower * above) + other * (upper * above)
    south = paired * upper + other * lower
    for even, odd, part in ((north_even, north_odd, north), (south_even, south_odd, south)):
        count = even.shape[0]
        tile = part[: 3 * TLON].reshape(3, TLON, D)[:count]
        sides = [
            part[at : at + count].reshape(count, 1, D)
            for at in range(3 * TLON, 3 * FRAME, 3)
        ]
        west = jnp.concatenate(sides[:3], axis=1)
        east = jnp.concatenate(sides[3:], axis=1)
        put_rows(even, odd, slice(0, count), tile, west, east)
    edge = strided_rows(
        spans(north_even, own_even_ref, south_even),
        spans(north_odd, own_odd_ref, south_odd),
        (0, 2, 5),
        weight_ref,
        bias_ref,
    )
    coarse[0] = edge[0] * above
    coarse[1] = edge[1]
    coarse[2:4] = upper_ref[...]
    coarse[4:6] = lower_ref[...]
    coarse[6] = edge[2] * below
    top[...] = finished(coarse, 0, 2, depth_ref, gain_ref)
    bottom[...] = finished(coarse, 4, 1, depth_ref, gain_ref)
    copies = [
        inner_copy,
        pltpu.make_async_copy(top, out_hbm.at[0:2], sent.at[1]),
        pltpu.make_async_copy(bottom, out_hbm.at[ROWS - 1 : ROWS], sent.at[2]),
    ]
    for copy in copies[1:]:
        copy.start()
    for copy in copies:
        copy.wait()


def outer(*arrays):
    return pl.pallas_call(
        outer_kernel,
        in_specs=[VMEM] * len(arrays),
        out_specs=ANY,
        out_shape=jax.ShapeDtypeStruct((ROWS, HALF, D), jnp.bfloat16),
        scratch_shapes=[
            pltpu.VMEM((3, SPAN, D), jnp.float32),
            pltpu.VMEM((3, SPAN + 8, D), jnp.float32),
            pltpu.VMEM((2, SPAN, D), jnp.float32),
            pltpu.VMEM((2, SPAN + 8, D), jnp.float32),
            pltpu.VMEM((7, SPAN, D), jnp.float32),
            pltpu.VMEM((2, HALF, D), jnp.bfloat16),
            pltpu.VMEM((1, HALF, D), jnp.bfloat16),
            pltpu.SemaphoreType.DMA((3,)),
        ],
        compiler_params=pltpu.CompilerParams(vmem_limit_bytes=16 << 20),
    )(*arrays)


def on_device(
    obs_values,
    obs_offset,
    obs_cell,
    obs_slot,
    obs_count,
    embed_weight,
    embed_bias,
    stride_weight,
    stride_bias,
    depth_weight,
    norm_gain,
):
    lon_count, lat_count = lax.axis_size("lon"), lax.axis_size("lat")
    lat = lax.axis_index("lat")
    packed = pack(obs_values, obs_offset, obs_cell, obs_slot, obs_count)
    lower, above, below = lat % 2 == 1, lat > 0, lat < lat_count - 1
    packed, lower, above, below = lax.optimization_barrier((packed, lower, above, below))
    arrived = lax.all_to_all(packed, ("lon", "lat"), split_axis=0, concat_axis=0, tiled=True)
    embed = embed_bias.reshape(1, D)
    side_cells, sums, last, first = sides(arrived, embed_weight, embed)
    sums, lower, above, below = lax.optimization_barrier((sums, lower, above, below))
    half, edge_cells, rows = edges(arrived, embed_weight, embed, side_cells, sums)
    ring = [(i, (i + 1) % lon_count) for i in range(lon_count)]
    west = lax.ppermute(last, "lon", ring)
    east = lax.ppermute(first, "lon", [(j, i) for i, j in ring])
    weight, bias = stride_weight.reshape(9 * D, D), stride_bias.reshape(1, D)
    ends = [slice(0, 3), slice(TLAT - 3, TLAT)]
    top, bottom = (
        jnp.concatenate([part.reshape(-1, D) for part in (rows[own], west[:, end], east[:, end])])
        for own, end in zip((slice(0, 3), slice(2, 5)), ends)
    )
    pairs = [(i, i + 1) for i in range(0, lat_count - 1, 2)]
    others = [(i, (i + 1) % lat_count) for i in range(1, lat_count, 2)]
    paired = lax.ppermute(
        jnp.where(lower, top, bottom), "lat", pairs + [(j, i) for i, j in pairs]
    )
    other = lax.ppermute(
        jnp.where(lower, bottom, top), "lat", others + [(j, i) for i, j in others]
    )
    gain = norm_gain.reshape(1, D)
    index = lax.broadcasted_iota(jnp.int32, (3, D), 0)
    flags = jnp.where(index == 0, lower, jnp.where(index == 1, above, below))
    place = flags.astype(jnp.float32)
    inside = inner(
        arrived,
        half,
        embed_weight,
        embed,
        side_cells,
        edge_cells,
        west,
        east,
        weight,
        bias,
        depth_weight,
        gain,
        place,
    )
    return outer(place, *inside, other, paired, weight, bias, depth_weight, gain)


def solution(mesh):
    placed = (
        P(("lon", "lat"), None, None),
        P(("lon", "lat"), None, None),
        P(("lon", "lat"), None),
        P(("lon", "lat"), None),
        P(("lon", "lat"), None),
        P(),
        P(),
        P(),
        P(),
        P(),
        P(),
    )
    return jax.shard_map(
        on_device, mesh=mesh, in_specs=placed, out_specs=P("lat", "lon", None), check_vma=False
    )
```

```python
import functools

import jax
import jax.numpy as jnp
from jax import lax
from jax.experimental import pallas as pl
from jax.experimental.pallas import tpu as pltpu
from jax.sharding import PartitionSpec as P

D = 256
OBS_VARS = 31
WIDTH = OBS_VARS + 1
SLOTS = 12
BINS = SLOTS * WIDTH
TLAT = 16
TLON = 32
HALF = TLON // 2
ROWS = TLAT // 2
LANES = 128
GROUP = 16
TILE = 4
CHUNK = 32
EARLY = 22
SPAN = 24
CELLS = TLAT * TLON
MID = 12
EXTRA = 4
SIDES = TLAT * 8
FRAME = TLON + 5

ANY = pl.BlockSpec(memory_space=pl.ANY)
VMEM = pl.BlockSpec(memory_space=pltpu.VMEM)


def placed_cells(cell):
    row, column = cell // TLON, cell % TLON
    pair, parity = column // 2, column % 2
    side = (pair < 1) | (pair > MID)
    edge = (row < 2) | (row >= TLAT - 3)
    corner = (row == 2) & (pair <= EXTRA)
    at_side = row * 8 + parity * 4 + jnp.where(pair < 1, 0, pair - MID)
    at_edge = SIDES + jnp.where(row < 2, row, row - TLAT + 5) * 2 * MID + parity * MID + pair - 1
    at_corner = SIDES + 10 * MID + parity * EXTRA + pair - 1
    at_row = CELLS // 2 - 2 * (MID - EXTRA) + parity * (MID - EXTRA) + pair - 1 - EXTRA
    at_inside = (row - 3) * 2 * MID + parity * MID + pair - 1
    rim = side | edge | corner
    in_rim = jnp.where(side, at_side, jnp.where(edge, at_edge, at_corner))
    return rim, jnp.where(rim, in_rim, jnp.where(row == 2, at_row, at_inside))


def pack_kernel(
    count_hbm,
    values_hbm,
    offset_hbm,
    cell_hbm,
    slot_hbm,
    out,
    count,
    values,
    offset,
    cell,
    slot,
    rows,
    here,
):
    tiles, capacity = cell.shape
    halves = capacity // LANES
    used = out.shape[1] * TILE
    stride = rows.shape[0] // (tiles + 1)
    groups = tiles // GROUP

    def at(j):
        return pl.ds(j * GROUP, GROUP)

    pairs = ((count_hbm, count), (offset_hbm, offset), (cell_hbm, cell), (slot_hbm, slot))
    small = [
        pltpu.make_async_copy(a, b, here.at[groups + i]) for i, (a, b) in enumerate(pairs)
    ]
    large = [
        pltpu.make_async_copy(values_hbm.at[:, at(j)], values.at[:, at(j)], here.at[j])
        for j in range(groups)
    ]
    for copy in small + large:
        copy.start()
    for copy in small:
        copy.wait()
    square = (tiles, tiles)
    diagonal = lax.broadcasted_iota(jnp.int32, square, 0) == lax.broadcasted_iota(
        jnp.int32, square, 1
    )
    counts = jnp.sum(jnp.where(diagonal, count[...], 0), axis=1, keepdims=True)
    position = lax.broadcasted_iota(jnp.int32, (tiles, capacity), 1)
    dy, dx = offset[:, 0, :], offset[:, 1, :]
    weight = jnp.where(position < counts, jnp.exp(-2.0 * (dy * dy + dx * dx)), 0.0)
    rim, place = placed_cells(cell[...])
    codes = (
        (slot[...] + jnp.where(rim, 0, SLOTS)).astype(jnp.float32),
        place.astype(jnp.float32),
    )
    base = halves * WIDTH
    for j in range(groups):
        own = slice(j * GROUP, (j + 1) * GROUP)

        def put(row, value, h, first=j * GROUP * stride):
            rows[pl.ds(first + row, GROUP, stride=stride), :] = value[
                :, h * LANES : (h + 1) * LANES
            ]

        for h in range(halves):
            put(h * WIDTH + OBS_VARS, weight[own], h)
            for i, code in enumerate(codes):
                put(base + i * halves + h, code[own], h)
        large[j].wait()
        for k in range(OBS_VARS):
            scaled = values[k, own, :].astype(jnp.float32) * weight[own]
            for h in range(halves):
                put(h * WIDTH + k, scaled, h)
        for d in range(j * GROUP, (j + 1) * GROUP):
            block = rows[d * stride : (d + 1) * stride, :].astype(jnp.bfloat16)
            out[d] = block.reshape(stride // TILE, TILE, LANES)[: used // TILE]


def pack(obs_values, obs_offset, obs_cell, obs_slot, obs_count):
    tiles, _, capacity = obs_values.shape
    used = capacity // LANES * (WIDTH + 2)
    stride = -(-used // 8) * 8
    values = jnp.transpose(obs_values, (1, 0, 2))
    shape = (tiles, used // TILE, TILE, LANES)
    arrays = (obs_count, values, obs_offset, obs_cell, obs_slot)
    return pl.pallas_call(
        pack_kernel,
        in_specs=[ANY] * len(arrays),
        out_specs=VMEM,
        out_shape=pltpu.VMEM(shape, jnp.bfloat16),
        scratch_shapes=[pltpu.VMEM(a.shape, a.dtype) for a in arrays]
        + [
            pltpu.VMEM(((tiles + 1) * stride, LANES), jnp.float32),
            pltpu.SemaphoreType.DMA((tiles // GROUP + 4,)),
        ],
        compiler_params=pltpu.CompilerParams(vmem_limit_bytes=24 << 20),
    )(*(pltpu.with_memory_space_constraint(a, pltpu.HBM) for a in arrays))


def add_sums(x_ref, total, first_slot, begin, end, held=None):
    blocks = x_ref.shape[1]
    halves = blocks * TILE // WIDTH
    step = WIDTH // TILE
    tall = 16
    iota = lax.broadcasted_iota(jnp.int32, (tall, LANES), 0).astype(jnp.float32)
    one = jnp.ones((tall, LANES), jnp.bfloat16)
    none = jnp.zeros((tall, LANES), jnp.bfloat16)
    zero = jnp.zeros((WIDTH, LANES), jnp.bfloat16)
    cells = [(iota + r).astype(jnp.bfloat16) for r in range(0, CELLS // 2, tall)]

    def operands(source):
        codes = x_ref[source, halves * step].astype(jnp.float32)
        spread, hot = [], []
        for h in range(halves):
            value = x_ref[source, h * step : (h + 1) * step].reshape(WIDTH, LANES)
            slot = jnp.broadcast_to(codes[h : h + 1], (WIDTH, LANES)).astype(jnp.bfloat16)
            place = codes[halves + h : halves + h + 1]
            place = jnp.broadcast_to(place, (tall, LANES)).astype(jnp.bfloat16)
            slots = range(first_slot, first_slot + SLOTS)
            by_slot = [jnp.where(slot == jnp.bfloat16(s), value, zero) for s in slots]
            by_cell = [jnp.where(place == c, one, none) for c in cells]
            spread.append(jnp.concatenate(by_slot, axis=0))
            hot.append(jnp.concatenate(by_cell, axis=0))
        return jnp.concatenate(spread, axis=1), jnp.concatenate(hot, axis=1)

    def summed(first, count):
        spread, hot = zip(*(operands(first + g) for g in range(count)))
        return lax.dot_general(
            jnp.concatenate(spread, axis=1),
            jnp.concatenate(hot, axis=1),
            (((1,), (1,)), ((), ())),
            preferred_element_type=jnp.float32,
        )

    parts = -(-(end - begin) // CHUNK)
    while (end - begin) % parts:
        parts += 1
    count = (end - begin) // parts
    total[...] = summed(begin, count) if held is None else held + summed(begin, count)

    @pl.loop(1, parts)
    def _(step):
        total[...] += summed(begin + step * count, count)


def embedded_cells(total, weight_ref, bias_ref):
    groups = []
    for s in range(SLOTS):
        block = total[s * WIDTH : (s + 1) * WIDTH, :]
        inverse = 1.0 / (1.0 + block[OBS_VARS:WIDTH, :])
        channel = lax.broadcasted_iota(jnp.int32, block.shape, 0)
        ratio = jnp.where(channel == OBS_VARS, block, block * inverse)
        groups.append(ratio.astype(jnp.bfloat16))
    projected = lax.dot_general(
        jnp.concatenate(groups, axis=0),
        weight_ref[...],
        (((0,), (0,)), ((), ())),
        preferred_element_type=jnp.float32,
    )
    return jax.nn.gelu(projected + bias_ref[...])


def sides_kernel(x_ref, weight_ref, bias_ref, sides_ref, sums_ref, last_ref, first_ref, total):
    add_sums(x_ref, total, 0, 0, x_ref.shape[0])
    sums_ref[...] = total[:, SIDES:]
    embedded = embedded_cells(total.at[:, :SIDES], weight_ref, bias_ref)
    sides_ref[...] = embedded
    sides = embedded.reshape(TLAT, 8, D)
    for i, c in enumerate((6, 3, 7)):
        last_ref[i] = sides[:, c, :].astype(jnp.bfloat16)
    for i, c in enumerate((0, 4)):
        first_ref[i] = sides[:, c, :].astype(jnp.bfloat16)


def edges_kernel(
    x_ref, weight_ref, bias_ref, sides_ref, sums_ref, half_ref, edges_ref, rows_ref
):
    add_sums(x_ref, half_ref, SLOTS, 0, x_ref.shape[0] * EARLY // 32)
    embedded = embedded_cells(sums_ref, weight_ref, bias_ref)
    edges_ref[...] = embedded
    middle = embedded[: 10 * MID].reshape(5, 2 * MID, D)
    sides = sides_ref[...].reshape(TLAT, 8, D)
    ends = jnp.concatenate([sides[:2], sides[TLAT - 3 :]], axis=0)
    parts = []
    for parity in range(2):
        at = 4 * parity
        parts += [
            ends[:, at : at + 1],
            middle[:, parity * MID : (parity + 1) * MID],
            ends[:, at + 1 : at + 4],
        ]
    rows_ref[...] = jnp.concatenate(parts, axis=1).astype(jnp.bfloat16)


def scatter_cost(tiles):
    return pl.CostEstimate(
        flops=2 * tiles * 256 * BINS * CELLS // 2, bytes_accessed=4 << 20, transcendentals=0
    )


def sides(arrived, embed_weight, embed_bias):
    outs = [
        jax.ShapeDtypeStruct((SIDES, D), jnp.float32),
        jax.ShapeDtypeStruct((BINS, CELLS // 2 - SIDES), jnp.float32),
        jax.ShapeDtypeStruct((3, TLAT, D), jnp.bfloat16),
        jax.ShapeDtypeStruct((2, TLAT, D), jnp.bfloat16),
    ]
    return pl.pallas_call(
        sides_kernel,
        in_specs=[VMEM] * 3,
        out_specs=[VMEM] * len(outs),
        out_shape=outs,
        scratch_shapes=[pltpu.VMEM((BINS, CELLS // 2), jnp.float32)],
        compiler_params=pltpu.CompilerParams(vmem_limit_bytes=32 << 20),
        cost_estimate=scatter_cost(arrived.shape[0]),
    )(arrived, embed_weight, embed_bias)


def edges(arrived, *arrays):
    outs = [
        jax.ShapeDtypeStruct((BINS, CELLS // 2), jnp.float32),
        jax.ShapeDtypeStruct((CELLS // 2 - SIDES, D), jnp.float32),
        jax.ShapeDtypeStruct((5, TLON, D), jnp.bfloat16),
    ]
    return pl.pallas_call(
        edges_kernel,
        in_specs=[VMEM] * (1 + len(arrays)),
        out_specs=[VMEM] * len(outs),
        out_shape=outs,
        compiler_params=pltpu.CompilerParams(vmem_limit_bytes=32 << 20),
        cost_estimate=scatter_cost(arrived.shape[0]),
    )(arrived, *arrays)


def put_rows(even, odd, rows, tile, west, east):
    even[rows, 0:1] = west[:, 1:2]
    even[rows, 1 : HALF + 1] = tile[:, :HALF]
    even[rows, HALF + 1 : HALF + 2] = east[:, 0:1]
    odd[rows, 0:1] = west[:, 0:1]
    odd[rows, 1:2] = west[:, 2:3]
    odd[rows, 2 : HALF + 2] = tile[:, HALF:]
    odd[rows, HALF + 2 : HALF + 3] = east[:, 1:2]


def strided_rows(even, odd, starts, weight_ref, bias_ref):
    pieces = []
    for a in range(3):
        for source, at in ((odd, 0), (even, 0), (odd, 1)):
            rows = [source(start + a, at) for start in starts]
            pieces.append(jnp.concatenate(rows, axis=0).astype(jnp.bfloat16))
    strided = jnp.dot(
        jnp.concatenate(pieces, axis=1), weight_ref[...], preferred_element_type=jnp.float32
    )
    coarse = jax.nn.gelu(strided + bias_ref[...]).astype(jnp.bfloat16)
    return coarse.astype(jnp.float32).reshape(len(starts), SPAN, D)


def spans(*refs):
    rows = [(ref, i) for ref in refs for i in range(ref.shape[0])]
    return lambda i, at: rows[i][0][rows[i][1], at : at + SPAN, :]


def finished(coarse, first, count, depth_ref, gain_ref):
    mixed = coarse[first + 1 : first + count + 1, 1 : HALF + 1]
    for a in range(3):
        for c in range(3):
            tap = depth_ref[3 * a + c : 3 * a + c + 1, :]
            mixed = mixed + coarse[first + a : first + a + count, c : c + HALF] * tap
    centre = mixed - jnp.mean(mixed, axis=-1, keepdims=True)
    variance = jnp.mean(centre * centre, axis=-1, keepdims=True)
    return (centre * lax.rsqrt(variance + 1e-05) * gain_ref[...]).astype(jnp.bfloat16)


def inner_kernel(
    x_ref,
    half_ref,
    embed_ref,
    embed_bias_ref,
    sides_ref,
    edges_ref,
    west_ref,
    east_ref,
    weight_ref,
    bias_ref,
    depth_ref,
    gain_ref,
    _,
    own_even_ref,
    own_odd_ref,
    upper_ref,
    lower_ref,
    out_ref,
    total,
    even,
    odd,
    coarse,
):
    tiles = x_ref.shape[0]
    add_sums(x_ref, total, SLOTS, tiles * EARLY // 32, tiles, half_ref[...])
    inside = embedded_cells(total, embed_ref, embed_bias_ref)
    west, east = (r[...].astype(jnp.float32) for r in (west_ref, east_ref))
    sides = sides_ref[...].reshape(TLAT, 8, D)
    edges = edges_ref[: 10 * MID].reshape(5, 2 * MID, D)
    corner = edges_ref[10 * MID :].reshape(1, 2 * EXTRA, D)
    bulk = inside[: 20 * MID].reshape(TLAT - 6, 2 * MID, D)
    rest = inside[20 * MID :].reshape(1, 2 * (MID - EXTRA), D)
    even[:, 0:1] = west[1].reshape(TLAT, 1, D)
    odd[:, 0:1] = west[0].reshape(TLAT, 1, D)
    odd[:, 1:2] = west[2].reshape(TLAT, 1, D)
    for parity, held in ((0, even), (1, odd)):
        at = 1 + parity
        mid = slice(at + 1, at + 1 + MID)
        cut = at + 1 + EXTRA
        own = slice(parity * MID, (parity + 1) * MID)
        held[:, at : at + 1] = sides[:, 4 * parity : 4 * parity + 1]
        held[:, at + 1 + MID : at + HALF] = sides[:, 4 * parity + 1 : 4 * parity + 4]
        held[:, at + HALF : at + HALF + 1] = east[parity].reshape(TLAT, 1, D)
        held[0:2, mid] = edges[0:2, own]
        held[TLAT - 3 :, mid] = edges[2:5, own]
        held[3 : TLAT - 3, mid] = bulk[:, own]
        held[2:3, at + 1 : cut] = corner[:, EXTRA * parity : EXTRA * (parity + 1)]
        span = MID - EXTRA
        held[2:3, cut : cut + span] = rest[:, span * parity : span * (parity + 1)]
    starts = range(1, TLAT - 2, 2)
    coarse[...] = strided_rows(spans(even), spans(odd), starts, weight_ref, bias_ref)
    for held, own_ref in ((even, own_even_ref), (odd, own_odd_ref)):
        own_ref[0:2] = held[0:2]
        own_ref[2:3] = held[TLAT - 1 :]
    upper_ref[...] = coarse[0:2]
    lower_ref[...] = coarse[ROWS - 3 : ROWS - 1]
    out_ref[...] = finished(coarse, 0, ROWS - 3, depth_ref, gain_ref)


def inner(arrived, *arrays):
    pair = jax.ShapeDtypeStruct((2, SPAN, D), jnp.float32)
    owns = [jax.ShapeDtypeStruct((3, n, D), jnp.float32) for n in (SPAN, SPAN + 8)]
    return pl.pallas_call(
        inner_kernel,
        in_specs=[VMEM] * (1 + len(arrays)),
        out_specs=[VMEM] * 5,
        out_shape=owns + [pair, pair, jax.ShapeDtypeStruct((ROWS - 3, HALF, D), jnp.bfloat16)],
        scratch_shapes=[
            pltpu.VMEM((BINS, CELLS // 2), jnp.float32),
            pltpu.VMEM((TLAT, SPAN, D), jnp.float32),
            pltpu.VMEM((TLAT, SPAN + 8, D), jnp.float32),
            pltpu.VMEM((ROWS - 1, SPAN, D), jnp.float32),
        ],
        compiler_params=pltpu.CompilerParams(vmem_limit_bytes=32 << 20),
        cost_estimate=scatter_cost(arrived.shape[0]),
    )(arrived, *arrays)


def outer_kernel(
    place_ref,
    own_even_ref,
    own_odd_ref,
    upper_ref,
    lower_ref,
    done_ref,
    other_ref,
    pair_ref,
    weight_ref,
    bias_ref,
    depth_ref,
    gain_ref,
    out_hbm,
    north_even,
    north_odd,
    south_even,
    south_odd,
    coarse,
    top,
    bottom,
    sent,
):
    inner_copy = pltpu.make_async_copy(done_ref, out_hbm.at[2 : ROWS - 1], sent.at[0])
    inner_copy.start()
    paired, other = (r[...].astype(jnp.float32) for r in (pair_ref, other_ref))
    lower, above, below = (place_ref[i : i + 1] for i in range(3))
    upper = 1.0 - lower
    north = paired * (lower * above) + other * (upper * above)
    south = paired * upper + other * lower
    for even, odd, part in ((north_even, north_odd, north), (south_even, south_odd, south)):
        count = even.shape[0]
        tile = part[: 3 * TLON].reshape(3, TLON, D)[:count]
        sides = [
            part[at : at + count].reshape(count, 1, D)
            for at in range(3 * TLON, 3 * FRAME, 3)
        ]
        west = jnp.concatenate(sides[:3], axis=1)
        east = jnp.concatenate(sides[3:], axis=1)
        put_rows(even, odd, slice(0, count), tile, west, east)
    edge = strided_rows(
        spans(north_even, own_even_ref, south_even),
        spans(north_odd, own_odd_ref, south_odd),
        (0, 2, 5),
        weight_ref,
        bias_ref,
    )
    coarse[0] = edge[0] * above
    coarse[1] = edge[1]
    coarse[2:4] = upper_ref[...]
    coarse[4:6] = lower_ref[...]
    coarse[6] = edge[2] * below
    top[...] = finished(coarse, 0, 2, depth_ref, gain_ref)
    bottom[...] = finished(coarse, 4, 1, depth_ref, gain_ref)
    copies = [
        inner_copy,
        pltpu.make_async_copy(top, out_hbm.at[0:2], sent.at[1]),
        pltpu.make_async_copy(bottom, out_hbm.at[ROWS - 1 : ROWS], sent.at[2]),
    ]
    for copy in copies[1:]:
        copy.start()
    for copy in copies:
        copy.wait()


def outer(*arrays):
    return pl.pallas_call(
        outer_kernel,
        in_specs=[VMEM] * len(arrays),
        out_specs=ANY,
        out_shape=jax.ShapeDtypeStruct((ROWS, HALF, D), jnp.bfloat16),
        scratch_shapes=[
            pltpu.VMEM((3, SPAN, D), jnp.float32),
            pltpu.VMEM((3, SPAN + 8, D), jnp.float32),
            pltpu.VMEM((2, SPAN, D), jnp.float32),
            pltpu.VMEM((2, SPAN + 8, D), jnp.float32),
            pltpu.VMEM((7, SPAN, D), jnp.float32),
            pltpu.VMEM((2, HALF, D), jnp.bfloat16),
            pltpu.VMEM((1, HALF, D), jnp.bfloat16),
            pltpu.SemaphoreType.DMA((3,)),
        ],
        compiler_params=pltpu.CompilerParams(vmem_limit_bytes=16 << 20),
    )(*arrays)


def on_device(
    obs_values,
    obs_offset,
    obs_cell,
    obs_slot,
    obs_count,
    embed_weight,
    embed_bias,
    stride_weight,
    stride_bias,
    depth_weight,
    norm_gain,
):
    lon_count, lat_count = lax.axis_size("lon"), lax.axis_size("lat")
    lat = lax.axis_index("lat")
    packed = pack(obs_values, obs_offset, obs_cell, obs_slot, obs_count)
    lower, above, below = lat % 2 == 1, lat > 0, lat < lat_count - 1
    packed, lower, above, below = lax.optimization_barrier((packed, lower, above, below))
    arrived = lax.all_to_all(packed, ("lon", "lat"), split_axis=0, concat_axis=0, tiled=True)
    embed = embed_bias.reshape(1, D)
    side_cells, sums, last, first = sides(arrived, embed_weight, embed)
    sums, lower, above, below = lax.optimization_barrier((sums, lower, above, below))
    half, edge_cells, rows = edges(arrived, embed_weight, embed, side_cells, sums)
    ring = [(i, (i + 1) % lon_count) for i in range(lon_count)]
    west = lax.ppermute(last, "lon", ring)
    east = lax.ppermute(first, "lon", [(j, i) for i, j in ring])
    weight, bias = stride_weight.reshape(9 * D, D), stride_bias.reshape(1, D)
    ends = [slice(0, 3), slice(TLAT - 3, TLAT)]
    top, bottom = (
        jnp.concatenate([part.reshape(-1, D) for part in (rows[own], west[:, end], east[:, end])])
        for own, end in zip((slice(0, 3), slice(2, 5)), ends)
    )
    pairs = [(i, i + 1) for i in range(0, lat_count - 1, 2)]
    others = [(i, (i + 1) % lat_count) for i in range(1, lat_count, 2)]
    paired = lax.ppermute(
        jnp.where(lower, top, bottom), "lat", pairs + [(j, i) for i, j in pairs]
    )
    other = lax.ppermute(
        jnp.where(lower, bottom, top), "lat", others + [(j, i) for i, j in others]
    )
    gain = norm_gain.reshape(1, D)
    index = lax.broadcasted_iota(jnp.int32, (3, D), 0)
    flags = jnp.where(index == 0, lower, jnp.where(index == 1, above, below))
    place = flags.astype(jnp.float32)
    inside = inner(
        arrived,
        half,
        embed_weight,
        embed,
        side_cells,
        edge_cells,
        west,
        east,
        weight,
        bias,
        depth_weight,
        gain,
        place,
    )
    return outer(place, *inside, other, paired, weight, bias, depth_weight, gain)


def solution(mesh):
    placed = (
        P(("lon", "lat"), None, None),
        P(("lon", "lat"), None, None),
        P(("lon", "lat"), None),
        P(("lon", "lat"), None),
        P(("lon", "lat"), None),
        P(),
        P(),
        P(),
        P(),
        P(),
        P(),
    )
    return jax.shard_map(
        on_device, mesh=mesh, in_specs=placed, out_specs=P("lat", "lon", None), check_vma=False
    )
```

```python
import functools

import jax
import jax.numpy as jnp
from jax import lax
from jax.experimental import pallas as pl
from jax.experimental.pallas import tpu as pltpu
from jax.sharding import PartitionSpec as P

D = 256
OBS_VARS = 31
WIDTH = OBS_VARS + 1
SLOTS = 12
BINS = SLOTS * WIDTH
TLAT = 16
TLON = 32
HALF = TLON // 2
ROWS = TLAT // 2
LANES = 128
GROUP = 16
TILE = 4
CHUNK = 32
EARLY = 24
SPAN = 24
CELLS = TLAT * TLON
MID = 12
EXTRA = 4
SIDES = TLAT * 8
FRAME = TLON + 5

ANY = pl.BlockSpec(memory_space=pl.ANY)
VMEM = pl.BlockSpec(memory_space=pltpu.VMEM)


def placed_cells(cell):
    row, column = cell // TLON, cell % TLON
    pair, parity = column // 2, column % 2
    side = (pair < 1) | (pair > MID)
    edge = (row < 2) | (row >= TLAT - 3)
    corner = (row == 2) & (pair <= EXTRA)
    at_side = row * 8 + parity * 4 + jnp.where(pair < 1, 0, pair - MID)
    at_edge = SIDES + jnp.where(row < 2, row, row - TLAT + 5) * 2 * MID + parity * MID + pair - 1
    at_corner = SIDES + 10 * MID + parity * EXTRA + pair - 1
    at_row = CELLS // 2 - 2 * (MID - EXTRA) + parity * (MID - EXTRA) + pair - 1 - EXTRA
    at_inside = (row - 3) * 2 * MID + parity * MID + pair - 1
    rim = side | edge | corner
    in_rim = jnp.where(side, at_side, jnp.where(edge, at_edge, at_corner))
    return rim, jnp.where(rim, in_rim, jnp.where(row == 2, at_row, at_inside))


def pack_kernel(
    count_hbm,
    values_hbm,
    offset_hbm,
    cell_hbm,
    slot_hbm,
    out,
    count,
    values,
    offset,
    cell,
    slot,
    rows,
    here,
):
    tiles, capacity = cell.shape
    halves = capacity // LANES
    used = out.shape[1] * TILE
    stride = rows.shape[0] // (tiles + 1)
    groups = tiles // GROUP

    def at(j):
        return pl.ds(j * GROUP, GROUP)

    pairs = ((count_hbm, count), (offset_hbm, offset), (cell_hbm, cell), (slot_hbm, slot))
    small = [
        pltpu.make_async_copy(a, b, here.at[groups + i]) for i, (a, b) in enumerate(pairs)
    ]
    large = [
        pltpu.make_async_copy(values_hbm.at[:, at(j)], values.at[:, at(j)], here.at[j])
        for j in range(groups)
    ]
    for copy in small + large:
        copy.start()
    for copy in small:
        copy.wait()
    square = (tiles, tiles)
    diagonal = lax.broadcasted_iota(jnp.int32, square, 0) == lax.broadcasted_iota(
        jnp.int32, square, 1
    )
    counts = jnp.sum(jnp.where(diagonal, count[...], 0), axis=1, keepdims=True)
    position = lax.broadcasted_iota(jnp.int32, (tiles, capacity), 1)
    dy, dx = offset[:, 0, :], offset[:, 1, :]
    weight = jnp.where(position < counts, jnp.exp(-2.0 * (dy * dy + dx * dx)), 0.0)
    rim, place = placed_cells(cell[...])
    codes = (
        (slot[...] + jnp.where(rim, 0, SLOTS)).astype(jnp.float32),
        place.astype(jnp.float32),
    )
    base = halves * WIDTH
    for j in range(groups):
        own = slice(j * GROUP, (j + 1) * GROUP)

        def put(row, value, h, first=j * GROUP * stride):
            rows[pl.ds(first + row, GROUP, stride=stride), :] = value[
                :, h * LANES : (h + 1) * LANES
            ]

        for h in range(halves):
            put(h * WIDTH + OBS_VARS, weight[own], h)
            for i, code in enumerate(codes):
                put(base + i * halves + h, code[own], h)
        large[j].wait()
        for k in range(OBS_VARS):
            scaled = values[k, own, :].astype(jnp.float32) * weight[own]
            for h in range(halves):
                put(h * WIDTH + k, scaled, h)
        for d in range(j * GROUP, (j + 1) * GROUP):
            block = rows[d * stride : (d + 1) * stride, :].astype(jnp.bfloat16)
            out[d] = block.reshape(stride // TILE, TILE, LANES)[: used // TILE]


def pack(obs_values, obs_offset, obs_cell, obs_slot, obs_count):
    tiles, _, capacity = obs_values.shape
    used = capacity // LANES * (WIDTH + 2)
    stride = -(-used // 8) * 8
    values = jnp.transpose(obs_values, (1, 0, 2))
    shape = (tiles, used // TILE, TILE, LANES)
    arrays = (obs_count, values, obs_offset, obs_cell, obs_slot)
    return pl.pallas_call(
        pack_kernel,
        in_specs=[ANY] * len(arrays),
        out_specs=VMEM,
        out_shape=pltpu.VMEM(shape, jnp.bfloat16),
        scratch_shapes=[pltpu.VMEM(a.shape, a.dtype) for a in arrays]
        + [
            pltpu.VMEM(((tiles + 1) * stride, LANES), jnp.float32),
            pltpu.SemaphoreType.DMA((tiles // GROUP + 4,)),
        ],
        compiler_params=pltpu.CompilerParams(vmem_limit_bytes=24 << 20),
    )(*(pltpu.with_memory_space_constraint(a, pltpu.HBM) for a in arrays))


def add_sums(x_ref, total, first_slot, begin, end, held=None):
    blocks = x_ref.shape[1]
    halves = blocks * TILE // WIDTH
    step = WIDTH // TILE
    tall = 16
    iota = lax.broadcasted_iota(jnp.int32, (tall, LANES), 0).astype(jnp.float32)
    one = jnp.ones((tall, LANES), jnp.bfloat16)
    none = jnp.zeros((tall, LANES), jnp.bfloat16)
    zero = jnp.zeros((WIDTH, LANES), jnp.bfloat16)
    cells = [(iota + r).astype(jnp.bfloat16) for r in range(0, CELLS // 2, tall)]

    def operands(source):
        codes = x_ref[source, halves * step].astype(jnp.float32)
        spread, hot = [], []
        for h in range(halves):
            value = x_ref[source, h * step : (h + 1) * step].reshape(WIDTH, LANES)
            slot = jnp.broadcast_to(codes[h : h + 1], (WIDTH, LANES)).astype(jnp.bfloat16)
            place = codes[halves + h : halves + h + 1]
            place = jnp.broadcast_to(place, (tall, LANES)).astype(jnp.bfloat16)
            slots = range(first_slot, first_slot + SLOTS)
            by_slot = [jnp.where(slot == jnp.bfloat16(s), value, zero) for s in slots]
            by_cell = [jnp.where(place == c, one, none) for c in cells]
            spread.append(jnp.concatenate(by_slot, axis=0))
            hot.append(jnp.concatenate(by_cell, axis=0))
        return jnp.concatenate(spread, axis=1), jnp.concatenate(hot, axis=1)

    def summed(first, count):
        spread, hot = zip(*(operands(first + g) for g in range(count)))
        return lax.dot_general(
            jnp.concatenate(spread, axis=1),
            jnp.concatenate(hot, axis=1),
            (((1,), (1,)), ((), ())),
            preferred_element_type=jnp.float32,
        )

    parts = -(-(end - begin) // CHUNK)
    while (end - begin) % parts:
        parts += 1
    count = (end - begin) // parts
    total[...] = summed(begin, count) if held is None else held + summed(begin, count)

    @pl.loop(1, parts)
    def _(step):
        total[...] += summed(begin + step * count, count)


def embedded_cells(total, weight_ref, bias_ref):
    groups = []
    for s in range(SLOTS):
        block = total[s * WIDTH : (s + 1) * WIDTH, :]
        inverse = 1.0 / (1.0 + block[OBS_VARS:WIDTH, :])
        channel = lax.broadcasted_iota(jnp.int32, block.shape, 0)
        ratio = jnp.where(channel == OBS_VARS, block, block * inverse)
        groups.append(ratio.astype(jnp.bfloat16))
    projected = lax.dot_general(
        jnp.concatenate(groups, axis=0),
        weight_ref[...],
        (((0,), (0,)), ((), ())),
        preferred_element_type=jnp.float32,
    )
    return jax.nn.gelu(projected + bias_ref[...])


def sides_kernel(x_ref, weight_ref, bias_ref, sides_ref, sums_ref, last_ref, first_ref, total):
    add_sums(x_ref, total, 0, 0, x_ref.shape[0])
    sums_ref[...] = total[:, SIDES:]
    embedded = embedded_cells(total.at[:, :SIDES], weight_ref, bias_ref)
    sides_ref[...] = embedded
    sides = embedded.reshape(TLAT, 8, D)
    for i, c in enumerate((6, 3, 7)):
        last_ref[i] = sides[:, c, :].astype(jnp.bfloat16)
    for i, c in enumerate((0, 4)):
        first_ref[i] = sides[:, c, :].astype(jnp.bfloat16)


def edges_kernel(
    x_ref, weight_ref, bias_ref, sides_ref, sums_ref, half_ref, edges_ref, rows_ref
):
    add_sums(x_ref, half_ref, SLOTS, 0, x_ref.shape[0] * EARLY // 32)
    embedded = embedded_cells(sums_ref, weight_ref, bias_ref)
    edges_ref[...] = embedded
    middle = embedded[: 10 * MID].reshape(5, 2 * MID, D)
    sides = sides_ref[...].reshape(TLAT, 8, D)
    ends = jnp.concatenate([sides[:2], sides[TLAT - 3 :]], axis=0)
    parts = []
    for parity in range(2):
        at = 4 * parity
        parts += [
            ends[:, at : at + 1],
            middle[:, parity * MID : (parity + 1) * MID],
            ends[:, at + 1 : at + 4],
        ]
    rows_ref[...] = jnp.concatenate(parts, axis=1).astype(jnp.bfloat16)


def scatter_cost(tiles):
    return pl.CostEstimate(
        flops=2 * tiles * 256 * BINS * CELLS // 2, bytes_accessed=4 << 20, transcendentals=0
    )


def sides(arrived, embed_weight, embed_bias):
    outs = [
        jax.ShapeDtypeStruct((SIDES, D), jnp.float32),
        jax.ShapeDtypeStruct((BINS, CELLS // 2 - SIDES), jnp.float32),
        jax.ShapeDtypeStruct((3, TLAT, D), jnp.bfloat16),
        jax.ShapeDtypeStruct((2, TLAT, D), jnp.bfloat16),
    ]
    return pl.pallas_call(
        sides_kernel,
        in_specs=[VMEM] * 3,
        out_specs=[VMEM] * len(outs),
        out_shape=outs,
        scratch_shapes=[pltpu.VMEM((BINS, CELLS // 2), jnp.float32)],
        compiler_params=pltpu.CompilerParams(vmem_limit_bytes=32 << 20),
        cost_estimate=scatter_cost(arrived.shape[0]),
    )(arrived, embed_weight, embed_bias)


def edges(arrived, *arrays):
    outs = [
        jax.ShapeDtypeStruct((BINS, CELLS // 2), jnp.float32),
        jax.ShapeDtypeStruct((CELLS // 2 - SIDES, D), jnp.float32),
        jax.ShapeDtypeStruct((5, TLON, D), jnp.bfloat16),
    ]
    return pl.pallas_call(
        edges_kernel,
        in_specs=[VMEM] * (1 + len(arrays)),
        out_specs=[VMEM] * len(outs),
        out_shape=outs,
        compiler_params=pltpu.CompilerParams(vmem_limit_bytes=32 << 20),
        cost_estimate=scatter_cost(arrived.shape[0]),
    )(arrived, *arrays)


def put_rows(even, odd, rows, tile, west, east):
    even[rows, 0:1] = west[:, 1:2]
    even[rows, 1 : HALF + 1] = tile[:, :HALF]
    even[rows, HALF + 1 : HALF + 2] = east[:, 0:1]
    odd[rows, 0:1] = west[:, 0:1]
    odd[rows, 1:2] = west[:, 2:3]
    odd[rows, 2 : HALF + 2] = tile[:, HALF:]
    odd[rows, HALF + 2 : HALF + 3] = east[:, 1:2]


def strided_rows(even, odd, starts, weight_ref, bias_ref):
    pieces = []
    for a in range(3):
        for source, at in ((odd, 0), (even, 0), (odd, 1)):
            rows = [source(start + a, at) for start in starts]
            pieces.append(jnp.concatenate(rows, axis=0).astype(jnp.bfloat16))
    strided = jnp.dot(
        jnp.concatenate(pieces, axis=1), weight_ref[...], preferred_element_type=jnp.float32
    )
    coarse = jax.nn.gelu(strided + bias_ref[...]).astype(jnp.bfloat16)
    return coarse.astype(jnp.float32).reshape(len(starts), SPAN, D)


def spans(*refs):
    rows = [(ref, i) for ref in refs for i in range(ref.shape[0])]
    return lambda i, at: rows[i][0][rows[i][1], at : at + SPAN, :]


def finished(coarse, first, count, depth_ref, gain_ref):
    mixed = coarse[first + 1 : first + count + 1, 1 : HALF + 1]
    for a in range(3):
        for c in range(3):
            tap = depth_ref[3 * a + c : 3 * a + c + 1, :]
            mixed = mixed + coarse[first + a : first + a + count, c : c + HALF] * tap
    centre = mixed - jnp.mean(mixed, axis=-1, keepdims=True)
    variance = jnp.mean(centre * centre, axis=-1, keepdims=True)
    return (centre * lax.rsqrt(variance + 1e-05) * gain_ref[...]).astype(jnp.bfloat16)


def inner_kernel(
    x_ref,
    half_ref,
    embed_ref,
    embed_bias_ref,
    sides_ref,
    edges_ref,
    west_ref,
    east_ref,
    weight_ref,
    bias_ref,
    depth_ref,
    gain_ref,
    _,
    own_even_ref,
    own_odd_ref,
    upper_ref,
    lower_ref,
    out_ref,
    total,
    even,
    odd,
    coarse,
):
    tiles = x_ref.shape[0]
    add_sums(x_ref, total, SLOTS, tiles * EARLY // 32, tiles, half_ref[...])
    inside = embedded_cells(total, embed_ref, embed_bias_ref)
    west, east = (r[...].astype(jnp.float32) for r in (west_ref, east_ref))
    sides = sides_ref[...].reshape(TLAT, 8, D)
    edges = edges_ref[: 10 * MID].reshape(5, 2 * MID, D)
    corner = edges_ref[10 * MID :].reshape(1, 2 * EXTRA, D)
    bulk = inside[: 20 * MID].reshape(TLAT - 6, 2 * MID, D)
    rest = inside[20 * MID :].reshape(1, 2 * (MID - EXTRA), D)
    even[:, 0:1] = west[1].reshape(TLAT, 1, D)
    odd[:, 0:1] = west[0].reshape(TLAT, 1, D)
    odd[:, 1:2] = west[2].reshape(TLAT, 1, D)
    for parity, held in ((0, even), (1, odd)):
        at = 1 + parity
        mid = slice(at + 1, at + 1 + MID)
        cut = at + 1 + EXTRA
        own = slice(parity * MID, (parity + 1) * MID)
        held[:, at : at + 1] = sides[:, 4 * parity : 4 * parity + 1]
        held[:, at + 1 + MID : at + HALF] = sides[:, 4 * parity + 1 : 4 * parity + 4]
        held[:, at + HALF : at + HALF + 1] = east[parity].reshape(TLAT, 1, D)
        held[0:2, mid] = edges[0:2, own]
        held[TLAT - 3 :, mid] = edges[2:5, own]
        held[3 : TLAT - 3, mid] = bulk[:, own]
        held[2:3, at + 1 : cut] = corner[:, EXTRA * parity : EXTRA * (parity + 1)]
        span = MID - EXTRA
        held[2:3, cut : cut + span] = rest[:, span * parity : span * (parity + 1)]
    starts = range(1, TLAT - 2, 2)
    coarse[...] = strided_rows(spans(even), spans(odd), starts, weight_ref, bias_ref)
    for held, own_ref in ((even, own_even_ref), (odd, own_odd_ref)):
        own_ref[0:2] = held[0:2]
        own_ref[2:3] = held[TLAT - 1 :]
    upper_ref[...] = coarse[0:2]
    lower_ref[...] = coarse[ROWS - 3 : ROWS - 1]
    out_ref[...] = finished(coarse, 0, ROWS - 3, depth_ref, gain_ref)


def inner(arrived, *arrays):
    pair = jax.ShapeDtypeStruct((2, SPAN, D), jnp.float32)
    owns = [jax.ShapeDtypeStruct((3, n, D), jnp.float32) for n in (SPAN, SPAN + 8)]
    return pl.pallas_call(
        inner_kernel,
        in_specs=[VMEM] * (1 + len(arrays)),
        out_specs=[VMEM] * 5,
        out_shape=owns + [pair, pair, jax.ShapeDtypeStruct((ROWS - 3, HALF, D), jnp.bfloat16)],
        scratch_shapes=[
            pltpu.VMEM((BINS, CELLS // 2), jnp.float32),
            pltpu.VMEM((TLAT, SPAN, D), jnp.float32),
            pltpu.VMEM((TLAT, SPAN + 8, D), jnp.float32),
            pltpu.VMEM((ROWS - 1, SPAN, D), jnp.float32),
        ],
        compiler_params=pltpu.CompilerParams(vmem_limit_bytes=32 << 20),
        cost_estimate=scatter_cost(arrived.shape[0]),
    )(arrived, *arrays)


def outer_kernel(
    place_ref,
    own_even_ref,
    own_odd_ref,
    upper_ref,
    lower_ref,
    done_ref,
    other_ref,
    pair_ref,
    weight_ref,
    bias_ref,
    depth_ref,
    gain_ref,
    out_hbm,
    north_even,
    north_odd,
    south_even,
    south_odd,
    coarse,
    top,
    bottom,
    sent,
):
    inner_copy = pltpu.make_async_copy(done_ref, out_hbm.at[2 : ROWS - 1], sent.at[0])
    inner_copy.start()
    paired, other = (r[...].astype(jnp.float32) for r in (pair_ref, other_ref))
    lower, above, below = (place_ref[i : i + 1] for i in range(3))
    upper = 1.0 - lower
    north = paired * (lower * above) + other * (upper * above)
    south = paired * upper + other * lower
    for even, odd, part in ((north_even, north_odd, north), (south_even, south_odd, south)):
        count = even.shape[0]
        tile = part[: 3 * TLON].reshape(3, TLON, D)[:count]
        sides = [
            part[at : at + count].reshape(count, 1, D)
            for at in range(3 * TLON, 3 * FRAME, 3)
        ]
        west = jnp.concatenate(sides[:3], axis=1)
        east = jnp.concatenate(sides[3:], axis=1)
        put_rows(even, odd, slice(0, count), tile, west, east)
    edge = strided_rows(
        spans(north_even, own_even_ref, south_even),
        spans(north_odd, own_odd_ref, south_odd),
        (0, 2, 5),
        weight_ref,
        bias_ref,
    )
    coarse[0] = edge[0] * above
    coarse[1] = edge[1]
    coarse[2:4] = upper_ref[...]
    coarse[4:6] = lower_ref[...]
    coarse[6] = edge[2] * below
    top[...] = finished(coarse, 0, 2, depth_ref, gain_ref)
    bottom[...] = finished(coarse, 4, 1, depth_ref, gain_ref)
    copies = [
        inner_copy,
        pltpu.make_async_copy(top, out_hbm.at[0:2], sent.at[1]),
        pltpu.make_async_copy(bottom, out_hbm.at[ROWS - 1 : ROWS], sent.at[2]),
    ]
    for copy in copies[1:]:
        copy.start()
    for copy in copies:
        copy.wait()


def outer(*arrays):
    return pl.pallas_call(
        outer_kernel,
        in_specs=[VMEM] * len(arrays),
        out_specs=ANY,
        out_shape=jax.ShapeDtypeStruct((ROWS, HALF, D), jnp.bfloat16),
        scratch_shapes=[
            pltpu.VMEM((3, SPAN, D), jnp.float32),
            pltpu.VMEM((3, SPAN + 8, D), jnp.float32),
            pltpu.VMEM((2, SPAN, D), jnp.float32),
            pltpu.VMEM((2, SPAN + 8, D), jnp.float32),
            pltpu.VMEM((7, SPAN, D), jnp.float32),
            pltpu.VMEM((2, HALF, D), jnp.bfloat16),
            pltpu.VMEM((1, HALF, D), jnp.bfloat16),
            pltpu.SemaphoreType.DMA((3,)),
        ],
        compiler_params=pltpu.CompilerParams(vmem_limit_bytes=16 << 20),
    )(*arrays)


def on_device(
    obs_values,
    obs_offset,
    obs_cell,
    obs_slot,
    obs_count,
    embed_weight,
    embed_bias,
    stride_weight,
    stride_bias,
    depth_weight,
    norm_gain,
):
    lon_count, lat_count = lax.axis_size("lon"), lax.axis_size("lat")
    lat = lax.axis_index("lat")
    packed = pack(obs_values, obs_offset, obs_cell, obs_slot, obs_count)
    lower, above, below = lat % 2 == 1, lat > 0, lat < lat_count - 1
    packed, lower, above, below = lax.optimization_barrier((packed, lower, above, below))
    arrived = lax.all_to_all(packed, ("lon", "lat"), split_axis=0, concat_axis=0, tiled=True)
    embed = embed_bias.reshape(1, D)
    side_cells, sums, last, first = sides(arrived, embed_weight, embed)
    sums, lower, above, below = lax.optimization_barrier((sums, lower, above, below))
    half, edge_cells, rows = edges(arrived, embed_weight, embed, side_cells, sums)
    ring = [(i, (i + 1) % lon_count) for i in range(lon_count)]
    west = lax.ppermute(last, "lon", ring)
    east = lax.ppermute(first, "lon", [(j, i) for i, j in ring])
    weight, bias = stride_weight.reshape(9 * D, D), stride_bias.reshape(1, D)
    ends = [slice(0, 3), slice(TLAT - 3, TLAT)]
    top, bottom = (
        jnp.concatenate([part.reshape(-1, D) for part in (rows[own], west[:, end], east[:, end])])
        for own, end in zip((slice(0, 3), slice(2, 5)), ends)
    )
    pairs = [(i, i + 1) for i in range(0, lat_count - 1, 2)]
    others = [(i, (i + 1) % lat_count) for i in range(1, lat_count, 2)]
    paired = lax.ppermute(
        jnp.where(lower, top, bottom), "lat", pairs + [(j, i) for i, j in pairs]
    )
    other = lax.ppermute(
        jnp.where(lower, bottom, top), "lat", others + [(j, i) for i, j in others]
    )
    gain = norm_gain.reshape(1, D)
    index = lax.broadcasted_iota(jnp.int32, (3, D), 0)
    flags = jnp.where(index == 0, lower, jnp.where(index == 1, above, below))
    place = flags.astype(jnp.float32)
    inside = inner(
        arrived,
        half,
        embed_weight,
        embed,
        side_cells,
        edge_cells,
        west,
        east,
        weight,
        bias,
        depth_weight,
        gain,
        place,
    )
    return outer(place, *inside, other, paired, weight, bias, depth_weight, gain)


def solution(mesh):
    placed = (
        P(("lon", "lat"), None, None),
        P(("lon", "lat"), None, None),
        P(("lon", "lat"), None),
        P(("lon", "lat"), None),
        P(("lon", "lat"), None),
        P(),
        P(),
        P(),
        P(),
        P(),
        P(),
    )
    return jax.shard_map(
        on_device, mesh=mesh, in_specs=placed, out_specs=P("lat", "lon", None), check_vma=False
    )
```
